256 devices in a mesh: span: 4 (over y_lo, core), lat: 8 (over x, y_hi), rad: 8 (over z).
Axes of the slice: x: 4, y: 4 (y_hi: 2, y_lo: 2; y = y_hi * 2 + y_lo), z: 8, core: 2. Of those that a mesh axis runs over, the one named last changes fastest.
Arguments:
- current: float32 [3, 32, 128, 512], P(None, 'rad', 'lat', 'span'), may hold values from -6 to 6
- previous: float32 [3, 32, 128, 512], P(None, 'rad', 'lat', 'span'), may hold values from -6 to 6
- moduli: float32 [4, 32, 128, 512], P(None, 'rad', 'lat', 'span'), may hold values from 0.5 to 1.5
- density: float32 [32, 128, 512], P('rad', 'lat', 'span'), may hold values from 0.8 to 1.2
- traces: float32 [32768, 3, 512], P(('span', 'lat', 'rad')), may hold values from -12 to 12
- receivers: int32 [32768], P(('span', 'lat', 'rad')), may hold values from 0 to 8191
- owners: int32 [32768, 1], P(('span', 'lat', 'rad')), may hold values from 0 to 63; in each aligned block of 128 rows (0 to 127, 128 to 255, ...) at most 4 rows name the same one
- offsets: int32 [32768], P(('span', 'lat', 'rad')), may hold values from 0 to 508
Outputs:
- final: float32 [3, 32, 128, 512], P(None, 'rad', 'lat', 'span')
- before_final: float32 [3, 32, 128, 512], P(None, 'rad', 'lat', 'span')
The draws below stay inside these ranges and needn't reach their ends.
Inputs may be any that keep to these rules, and one draw needn't show every extreme that they name: `owners`: o identifies the owner lat * 8 + rad among the devices of the station's own face set; in the stations of one device no owner is named by more than 4 rows, and exactly 4 in some devices. `receivers`: index (r * 16 + l) * 128 + e of the cell on its owner.
All inputs are finite; a program needn't handle non-finite values.
Results may differ from the reference program's by a relative error of at most 0.00002.
Values sent between devices are 32-bit elements; how exact they have to be, the bound alone decides.
No kernel may reach another device: no remote copies, remote signals or barrier semaphores. Data moves between devices by JAX's collectives and lax.ppermute only.
A program may use at most 64 MiB of HBM per device.

```python
import math
import jax
import jax.numpy as jnp
import numpy as np

CR = 4
CL = 16
CE = 128
S_DEV = 128
NT = 512
STEPS = 4
NR = 32
NL = 128
NE = 512
NS = 32768
CAP = 4
N_LAT = 8
N_RAD = 8


def place_ends(drawn, stream_key, low, largest):
    spot = [jax.random.randint(jax.random.fold_in(stream_key, axis), (), 0, length) for axis, length in enumerate(drawn.shape)]
    widest = drawn.shape.index(max(drawn.shape))
    next_to = spot[:widest] + [(spot[widest] + 1) % drawn.shape[widest]] + spot[widest + 1:]
    return drawn.at[tuple(spot)].set(low).at[tuple(next_to)].set(largest)


def block_levels(stream_key, extent, split, smallest, top_value):
    level, own = 1.0, jax.random.fold_in(stream_key, 6)
    for dim, shards_of in split:
        draws = jnp.exp(jax.random.uniform(jax.random.fold_in(own, dim), (shards_of,), jnp.float32, smallest / len(split), top_value / len(split)))
        level = level * jnp.repeat(draws, extent[dim] // shards_of).reshape([-1 if axis == dim else 1 for axis in range(len(extent))])
    return level


def shared_out(rng, own, number, rows, number_of, top, bound, slope):
    order = jax.random.permutation(rng, number_of)
    crowded, usual = shares(number_of, rows * top, bound, slope, True), shares(number_of, rows * top, bound, slope, False)
    places = jnp.arange(number_of)

    def named(tallies, offset_by):
        used = int((tallies > 0).sum())
        fixed = max(1, used // 4)
        moved = fixed + (places - fixed + offset_by * (used - fixed)) % max(1, number_of - fixed)
        return jnp.zeros((number_of,), jnp.int32).at[order[jnp.where(places < fixed, places, moved)]].set(jnp.asarray(tallies, jnp.int32))

    tallies = jnp.where(number % 4 == 0, named(crowded, number // 4), named(usual, number - number // 4 - 1))
    mixed = jax.random.permutation(jax.random.fold_in(own, 3), number_of)
    giver, taker = mixed[0:number_of // 2 * 2:2], mixed[1:number_of // 2 * 2:2]
    slack = jnp.minimum(tallies[giver] - 1, bound - tallies[taker]) // 2
    slack = jnp.where((giver == order[0]) | (taker == order[0]) | (tallies[taker] == 0), 0, jnp.maximum(slack, 0))
    moved = jax.random.randint(jax.random.fold_in(own, 4), (number_of // 2,), 0, 1 << 20) % (slack + 1)
    tallies = tallies.at[giver].add(-moved).at[taker].add(moved)
    labels = jnp.searchsorted(jnp.cumsum(tallies), jnp.arange(rows * top), side="right").astype(jnp.int32)
    table = labels.reshape(top, rows).T
    table = table[jax.random.permutation(jax.random.fold_in(own, 1), rows)]
    offset_by = jax.random.randint(jax.random.fold_in(own, 2), (rows, 1), 0, top)
    return jnp.take_along_axis(table, (jnp.arange(top)[None, :] + offset_by) % top, axis=1)


def shares(count, total, most, slope, full):
    weights = [(1 << 20) // math.isqrt(rank ** slope) + 1 for rank in range(1, count + 1)]
    largest = most if full else min(most, max(-(-total // count), total * weights[0] // sum(weights)))
    least = 1 if total - largest >= count - 1 else 0
    given, surplus = [largest] + [least] * (count - 1), total - largest - least * (count - 1)
    while surplus > 0:
        movable = [i for i in range(1, count) if given[i] < largest] or [i for i in range(1, count) if given[i] < most]
        pool, remaining = sum([weights[i] for i in movable]), surplus
        for i in movable:
            extra = min(most - given[i], max(1, remaining * weights[i] // pool), surplus)
            given[i] = given[i] + extra
            surplus = surplus - extra
    return np.array(given)


def normal_values(stream_key, dims, scale, limit, cuts=(), kind=jnp.bfloat16):
    result = jax.random.normal(stream_key, dims, jnp.float32) * scale
    if len(cuts) > 0:
        result = block_levels(stream_key, dims, cuts, -0.22, 0.18) * result
    return jnp.clip(result, min=-limit, max=limit).astype(kind)


def setup_inputs(seed: int = 0) -> dict:
    key_of = jax.random.split(jax.random.key(seed), 9)
    current = normal_values(key_of[0], (3, NR, NL, NE), 1.0, 6.0, ((1, 8), (2, 8), (3, 4)), jnp.float32)
    previous = normal_values(key_of[1], (3, NR, NL, NE), 1.0, 6.0, ((1, 8), (2, 8), (3, 4)), jnp.float32)
    moduli = jnp.clip(jnp.exp(math.log(1.5) - 1.0986123 * jax.random.uniform(key_of[2], (4, NR, NL, NE), jnp.float32) ** block_levels(key_of[2], (4, NR, NL, NE), ((1, 8), (2, 8), (3, 4)), -0.2, 0.2)), 0.5, 1.5)
    density = jnp.clip(0.8 + 0.40000004 * jax.random.uniform(key_of[3], (NR, NL, NE), jnp.float32) ** block_levels(key_of[3], (NR, NL, NE), ((0, 8), (1, 8), (2, 4)), -0.2, 0.2), 0.8, 1.2)
    traces = normal_values(key_of[4], (NS, 3, NT), 3.0, 12.0, ((0, 256),), jnp.float32)
    receivers = place_ends(jax.random.randint(key_of[5], (NS,), 0, CR * CL * CE), jax.random.fold_in(key_of[5], 1), 0, (CR * CL * CE) - 1).astype(jnp.int32)
    owners_keys = jax.random.split(jax.random.fold_in(key_of[6], 1), NS // S_DEV)
    owners_turns = jax.random.permutation(jax.random.fold_in(key_of[6], 3), NS // S_DEV)
    owners = jax.vmap(lambda own, number: shared_out(jax.random.fold_in(key_of[6], 2), own, number, S_DEV, N_LAT * N_RAD, 1, CAP, 2))(owners_keys, owners_turns).reshape((NS, 1))
    offsets = place_ends(jax.random.randint(key_of[7], (NS,), 0, NT - STEPS + 1), jax.random.fold_in(key_of[7], 1), 0, NT - STEPS).astype(jnp.int32)
    return dict(current=current, previous=previous, moduli=moduli, density=density, traces=traces, receivers=receivers, owners=owners, offsets=offsets)


step_square = 0.16
modulus_table = ((0, 2, 2), (2, 1, 3), (2, 3, 1))


def face_flux(centre, centre_mod, upper, lower, upper_mod, lower_mod):
    return 0.5 * (centre_mod + upper_mod) * (upper - centre) + 0.5 * (centre_mod + lower_mod) * (lower - centre)


def forces(current, moduli, current_near, moduli_near):
    pieces = []
    for component in range(3):
        running = jnp.zeros_like(current[component])
        for direction in range(3):
            pick_mod = modulus_table[component][direction]
            running = running + face_flux(current[component], moduli[pick_mod], current_near[direction][0][component], current_near[direction][1][component], moduli_near[direction][0][pick_mod], moduli_near[direction][1][pick_mod])
        pieces.append(running)
    return jnp.stack(pieces)


def near_global(stacked):
    rad_pad = jnp.pad(stacked, ((0, 0), (1, 1), (0, 0), (0, 0)))
    lat_pad = jnp.pad(stacked, ((0, 0), (0, 0), (1, 1), (0, 0)))
    return ((rad_pad[:, 2:], rad_pad[:, :-2]), (lat_pad[:, :, 2:], lat_pad[:, :, :-2]), (jnp.roll(stacked, -1, 3), jnp.roll(stacked, 1, 3)))


def reference(current, previous, moduli, density, traces, receivers, owners, offsets):
    station_count = traces.shape[0]
    station_rows = jnp.arange(station_count, dtype=jnp.int32)
    face_set = station_rows // S_DEV // (N_LAT * N_RAD)
    owner_ids = owners[:, 0].astype(jnp.int32)
    owner_lat = owner_ids // N_RAD
    owner_rad = owner_ids % N_RAD
    cell_index = receivers.astype(jnp.int32)
    radial_at = owner_rad * CR + cell_index // (CL * CE)
    lateral_at = owner_lat * CL + (cell_index // CE) % CL
    around_at = face_set * CE + cell_index % CE
    flat_index = ((radial_at * NL + lateral_at) * NE + around_at).astype(jnp.int32)
    moduli_near = near_global(moduli)
    for step_index in range(STEPS):
        forcing = forces(current, moduli, near_global(current), moduli_near)
        values = traces[station_rows, :, offsets.astype(jnp.int32) + step_index]
        forcing = forcing.reshape(3, -1).at[:, flat_index].add(values.T).reshape(forcing.shape)
        following = 2.0 * current - previous + step_square * forcing / density
        previous, current = current, following
    return current, previous
```

```python
import jax
import jax.numpy as jnp
from jax import lax
from jax.experimental import pallas as pl
from jax.experimental.pallas import tpu as pltpu
from jax.sharding import PartitionSpec as P

STEPS = 4
STEP_SQUARE = 0.16
TABLE = ((0, 2, 2), (2, 1, 3), (2, 3, 1))
CR, CL, CE = 4, 16, 128
HALO = 4
ROWS = CL + 2 * HALO
CAP = 4
SLOTS = 6
STATIONS = 128
F32 = jnp.float32
I32 = jnp.int32


def iota(shape, dim):
    return lax.broadcasted_iota(I32, shape, dim)


def fold(tiles, at):
    lane, sub = iota((8, 128), 1), iota((8, 128), 0)
    rows = []
    for start in range(0, len(tiles), 16):
        gathered = jnp.zeros((8, 128), F32)
        for i, tile in enumerate(tiles[start : start + 16]):
            column = jnp.broadcast_to(tile[:, at : at + 1], (8, 128))
            gathered = jnp.where(lane == i * 8 + sub, column, gathered)
        rows.append(jnp.sum(gathered, axis=0, keepdims=True))
    return rows


def unfold(ref, first_row, tile):
    row = first_row + tile // 16
    spread = jnp.broadcast_to(ref[row : row + 1, :], (8, 128))
    return jnp.take_along_axis(spread, (tile % 16) * 8 + iota((8, 128), 0), axis=1)


def column(ref, first_row, k, r):
    first = (k * CR + r) * (ROWS // 8)
    return jnp.concatenate([unfold(ref, first_row, first + i) for i in range(ROWS // 8)], axis=0)


def tiles_of(ref, count, first=0):
    return [
        ref[first + k, r, 8 * i : 8 * i + 8, :]
        for k in range(count)
        for r in range(CR)
        for i in range(ROWS // 8)
    ]


def put_columns(tiles, left_ref, right_ref, first_row):
    for ref, at in ((left_ref, 0), (right_ref, CE - 1)):
        for i, row in enumerate(fold(tiles, at)):
            ref[first_row + i : first_row + i + 1, :] = row


def put_faces(u_ref, down_ref, up_ref, left_ref, right_ref):
    for k in range(3):
        down_ref[k] = u_ref[k, 0]
        up_ref[k] = u_ref[k, CR - 1]
    left_ref[...] = jnp.zeros_like(left_ref)
    right_ref[...] = jnp.zeros_like(right_ref)
    put_columns(tiles_of(u_ref, 3), left_ref, right_ref, 0)


def edges_kernel(cur, prv, mod, den, low, high):
    fields = (
        [cur.at[k] for k in range(3)]
        + [prv.at[k] for k in range(3)]
        + [mod.at[k] for k in range(4)]
        + [den]
    )
    for f, ref in enumerate(fields):
        for r in range(CR):
            spot = slice(HALO * (r % 2), HALO * (r % 2) + HALO)
            low[f, r // 2, spot, :] = ref[r, 0:HALO, :]
            high[f, r // 2, spot, :] = ref[r, CL - HALO : CL, :]


def pack_kernel(offsets, receivers, owners, traces, out, window):
    lane, sub = iota((8, 128), 1), iota((8, 128), 0)
    pattern = (lane // 8) % STEPS
    mine = (lane // 32) == sub
    for s in range(STATIONS):
        offset = offsets[s]
        tile = offset // 128
        inside = offset % 128
        first = traces[s, :, pl.ds(pl.multiple_of(tile * 128, 128), 128)]
        second = traces[
            s, :, pl.ds(pl.multiple_of(jnp.minimum(tile + 1, 3) * 128, 128), 128)
        ]
        merged = jnp.where(lane[:3] >= inside, first, second)
        picked = jnp.take_along_axis(merged, (inside + pattern[:3]) % 128, axis=1)
        window[s : s + 1, :] = jnp.sum(
            jnp.where(mine[:3], picked, 0.0), axis=0, keepdims=True
        )

    owner_row = owners[...]
    q = receivers[...]
    r, l, e = q // 2048, (q // 128) % CL, q % 128
    wide_sub, wide_lane = iota((128, 128), 0), iota((128, 128), 1)
    owner_cols = jnp.transpose(jnp.broadcast_to(owner_row.astype(F32), (128, 128)))
    same = (owner_cols.astype(I32) == owner_row) & (wide_sub < wide_lane)
    rank = jnp.sum(jnp.where(same, 1.0, 0.0), axis=0, keepdims=True).astype(I32)

    lefts, rights = [], []
    for shift in (-1, 0, 1):
        slot = (shift + 1) * CAP + rank
        half, j = slot // SLOTS, slot % SLOTS
        if shift == 0:
            row, near = l, l >= 0
        elif shift == -1:
            row, near = CL + l, l <= HALO - 2
        else:
            row, near = l + HALO + HALO, l >= CL - HALO + 1
        target = owner_row + 8 * shift
        ok = near & (target >= 0) & (target < 64)
        place = jnp.where(ok, half * 64 + target, -1)
        lefts.append(jnp.where(wide_sub == place, 1.0, 0.0))
        sheet = jnp.transpose(
            jnp.concatenate(
                [
                    j.astype(F32),
                    (r * ROWS + row).astype(F32),
                    e.astype(F32),
                    jnp.zeros((5, 128), F32),
                ],
                axis=0,
            )
        )
        words = jnp.where(
            wide_lane < 96,
            window[...],
            jnp.where(
                wide_lane < 104,
                jnp.broadcast_to(sheet[:, 1:2], (128, 128)),
                jnp.broadcast_to(sheet[:, 2:3], (128, 128)),
            ),
        )
        slots = jnp.broadcast_to(sheet[:, 0:1], (128, 128)).astype(I32)
        rights.append(jnp.where((wide_lane % 8 == slots) & (wide_lane < 112), words, 0.0))
    packed = lax.dot_general(
        jnp.concatenate(lefts, axis=1),
        jnp.concatenate(rights, axis=0),
        (((1,), (0,)), ((), ())),
        precision=lax.Precision.HIGHEST,
        preferred_element_type=F32,
    )
    out[:, :128] = packed[:64]
    out[:, 128:] = packed[64:]


def widen_kernel(
    cur, prv, mod, den, from_low, from_high, u, v, m, c, down, up, left, right
):
    lat = lax.axis_index("lat")
    has_low, has_high = lat > 0, lat < lax.axis_size("lat") - 1

    def ghosts(f, r):
        spot = slice(HALO * (r % 2), HALO * (r % 2) + HALO)
        return jnp.concatenate(
            [
                jnp.where(has_high, from_high[f, r // 2, spot, :], 0.0),
                jnp.where(has_low, from_low[f, r // 2, spot, :], 0.0),
            ],
            axis=0,
        )

    for r in range(CR):
        for k in range(3):
            u[k, r, 0:CL, :] = cur[k, r]
            u[k, r, CL:ROWS, :] = ghosts(k, r)
            v[k, r, 0:CL, :] = prv[k, r]
            v[k, r, CL:ROWS, :] = ghosts(3 + k, r)
        for j in range(4):
            m[j, r, 0:CL, :] = mod[j, r]
            m[j, r, CL:ROWS, :] = ghosts(6 + j, r)
        c[r, 0:CL, :] = STEP_SQUARE / den[r]
        spot = slice(HALO * (r % 2), HALO * (r % 2) + HALO)
        outer = STEP_SQUARE / jnp.concatenate(
            [from_high[10, r // 2, spot, :], from_low[10, r // 2, spot, :]], axis=0
        )
        present = jnp.where(iota((8, 128), 0) < HALO, has_high.astype(I32), has_low.astype(I32))
        c[r, CL:ROWS, :] = jnp.where(present > 0, outer, 0.0)
    for k in range(3):
        down[k] = u[k, 0]
        up[k] = u[k, CR - 1]
    for i, j in enumerate((0, 2)):
        down[3 + i] = m[j, 0]
        up[3 + i] = m[j, CR - 1]
    left[...] = jnp.zeros_like(left)
    right[...] = jnp.zeros_like(right)
    put_columns(tiles_of(u, 3), left, right, 0)
    put_columns(tiles_of(m, 3, 1), left, right, 3)


def force(k, r, u, low, high, at_left, at_right, ar, al, au, ad):
    jr, jl, je = TABLE[k]
    here = u[k, r]
    below = u[k, r - 1] if r > 0 else low[k]
    above = u[k, r + 1] if r < CR - 1 else high[k]
    total = ar[jr // 2, r + 1] * (above - here) - ar[jr // 2, r] * (here - below)
    flux = al[jl - 1, r] * (pltpu.roll(here, ROWS - 1, 0) - here)
    total = total + (flux - pltpu.roll(flux, 1, 0))
    lane = iota((ROWS, CE), 1)
    after = jnp.where(lane == CE - 1, column(at_right, 0, k, r), pltpu.roll(here, CE - 1, 1))
    before = jnp.where(lane == 0, column(at_left, 0, k, r), pltpu.roll(here, 1, 1))
    return total + (au[je - 1, r] * (after - here) + ad[je - 1, r] * (before - here))


def radial_ends(low, high, count):
    rad = lax.axis_index("rad")
    lows = [jnp.where(rad > 0, low[k], 0.0) for k in range(count)]
    highs = [
        jnp.where(rad < lax.axis_size("rad") - 1, high[k], 0.0) for k in range(count)
    ]
    return lows, highs


def prepare_kernel(u, v, m, c, low, high, at_left, at_right, ar, al, au, ad, following):
    lows, highs = radial_ends(low, high, 5)
    lane = iota((ROWS, CE), 1)
    for i, j in enumerate((0, 2)):
        layers = [lows[3 + i]] + [m[j, r] for r in range(CR)] + [highs[3 + i]]
        for face in range(CR + 1):
            ar[i, face] = 0.5 * (layers[face] + layers[face + 1])
    for j in (1, 2, 3):
        for r in range(CR):
            here = m[j, r]
            al[j - 1, r] = 0.5 * (here + pltpu.roll(here, ROWS - 1, 0))
            after = jnp.where(
                lane == CE - 1, column(at_right, 3, j - 1, r), pltpu.roll(here, CE - 1, 1)
            )
            before = jnp.where(lane == 0, column(at_left, 3, j - 1, r), pltpu.roll(here, 1, 1))
            au[j - 1, r] = 0.5 * (here + after)
            ad[j - 1, r] = 0.5 * (here + before)
    for k in range(3):
        for r in range(CR):
            total = force(k, r, u, lows, highs, at_left, at_right, ar, al, au, ad)
            following[k, r] = 2.0 * u[k, r] - v[k, r] + c[r] * total


def scatter_kernel(got, free, c, first, sources, down, up, left, right, weights, picks):
    turned = jnp.transpose(jnp.concatenate([got[:, :128], got[:, 128:]], axis=0))
    cell_rows, cell_lanes = iota((CR * ROWS, 128), 0), iota((CE, 128), 0)
    for j in range(SLOTS):
        span = slice(128 * j, 128 * j + 128)
        place = turned[96 + j : 97 + j].astype(I32)
        around = turned[104 + j : 105 + j].astype(I32)
        picks[:, span] = jnp.where(cell_lanes == around, 1.0, 0.0)
        here = cell_rows == place
        for w in range(3 * STEPS):
            weights[w * CR * ROWS : (w + 1) * CR * ROWS, span] = jnp.where(
                here, turned[w * 8 + j : w * 8 + j + 1], 0.0
            )
    summed = lax.dot_general(
        weights[...],
        picks[...],
        (((1,), (1,)), ((), ())),
        precision=lax.Precision.HIGHEST,
        preferred_element_type=F32,
    )
    for k in range(3):
        for r in range(CR):
            for t in range(STEPS):
                at = ((k * STEPS + t) * CR + r) * ROWS
                value = summed[at : at + ROWS] * c[r]
                if t == 0:
                    first[k, r] = free[k, r] + value
                else:
                    sources[t - 1, k, r] = value
    put_faces(first, down, up, left, right)


def step_kernel(t, u, v, c, sources, low, high, at_left, at_right, ar, al, au, ad, *outs):
    lows, highs = radial_ends(low, high, 3)
    following = outs[0]
    last = t == STEPS - 1
    for k in range(3):
        for r in range(CR):
            total = force(k, r, u, lows, highs, at_left, at_right, ar, al, au, ad)
            value = 2.0 * u[k, r] - v[k, r] + c[r] * total + sources[t - 1, k, r]
            if last:
                following[k, r] = value[:CL]
                outs[1][k, r] = u[k, r, 0:CL, :]
            else:
                following[k, r] = value
    if not last:
        put_faces(following, *outs[1:])


def call(kernel, outs, args, scratch=(), smem=0):
    vmem = pl.BlockSpec(memory_space=pltpu.VMEM)
    specs = [pl.BlockSpec(memory_space=pltpu.SMEM)] * smem + [vmem] * (len(args) - smem)
    return pl.pallas_call(
        kernel,
        out_shape=[jax.ShapeDtypeStruct(shape, F32) for shape in outs],
        in_specs=specs,
        out_specs=[vmem] * len(outs),
        scratch_shapes=[pltpu.VMEM(shape, F32) for shape in scratch],
        compiler_params=pltpu.CompilerParams(vmem_limit_bytes=32 * 1024 * 1024),
    )(*args)


def shifted(block, axis, by):
    count = lax.axis_size(axis)
    return lax.ppermute(block, axis, [(i, (i + by) % count) for i in range(count)])


def swap_faces(down, up, left, right):
    low = shifted(up, "rad", 1)
    high = shifted(down, "rad", -1)
    at_left = shifted(right, "span", 1)
    at_right = shifted(left, "span", -1)
    return low, high, at_left, at_right


def on_device(current, previous, moduli, density, traces, receivers, owners, offsets):
    wide = (3, CR, ROWS, CE)
    edge = (11, 2, 8, CE)
    faces = [(3, ROWS, CE), (3, ROWS, CE), (8, CE), (8, CE)]

    low_rows, high_rows = call(
        edges_kernel, [edge, edge], (current, previous, moduli, density)
    )
    from_low = shifted(high_rows, "lat", 1)
    from_high = shifted(low_rows, "lat", -1)

    (packed,) = call(
        pack_kernel,
        [(64, 256)],
        (offsets, receivers.reshape(1, 128), owners.reshape(1, 128), traces),
        scratch=[(STATIONS, 128)],
        smem=1,
    )
    got = lax.all_to_all(packed, ("lat", "rad"), 0, 0, tiled=True)

    u, v, m, c, *ends = call(
        widen_kernel,
        [wide, wide, (4, CR, ROWS, CE), (CR, ROWS, CE)]
        + [(5, ROWS, CE), (5, ROWS, CE), (8, CE), (8, CE)],
        (current, previous, moduli, density, from_low, from_high),
    )
    *coefficients, free = call(
        prepare_kernel,
        [(2, CR + 1, ROWS, CE), wide, wide, wide, wide],
        (u, v, m, c, *swap_faces(*ends)),
    )
    first, sources, *ends = call(
        scatter_kernel,
        [wide, (STEPS - 1,) + wide] + faces,
        (got, free, c),
        scratch=[(3 * STEPS * CR * ROWS, 128 * SLOTS), (CE, 128 * SLOTS)],
    )
    v, u = u, first
    for t in range(1, STEPS):
        args = (u, v, c, sources, *swap_faces(*ends), *coefficients)

        def kernel(*refs, t=t):
            step_kernel(t, *refs)

        if t == STEPS - 1:
            return tuple(call(kernel, [(3, CR, CL, CE)] * 2, args))
        following, *ends = call(kernel, [wide] + faces, args)
        v, u = u, following


def solution(mesh):
    in_specs = (
        P(None, "rad", "lat", "span"),
        P(None, "rad", "lat", "span"),
        P(None, "rad", "lat", "span"),
        P("rad", "lat", "span"),
        P(("span", "lat", "rad"), None, None),
        P(("span", "lat", "rad")),
        P(("span", "lat", "rad"), None),
        P(("span", "lat", "rad")),
    )
    out_specs = (P(None, "rad", "lat", "span"), P(None, "rad", "lat", "span"))
    return jax.shard_map(
        on_device, mesh=mesh, in_specs=in_specs, out_specs=out_specs, check_vma=False
    )
```

```python
import jax
import jax.numpy as jnp
from jax import lax
from jax.experimental import pallas as pl
from jax.experimental.pallas import tpu as pltpu
from jax.sharding import PartitionSpec as P

STEPS = 4
STEP_SQUARE = 0.16
TABLE = ((0, 2, 2), (2, 1, 3), (2, 3, 1))
CR, CL, CE = 4, 16, 128
HALO = 4
ROWS = CL + 2 * HALO
CAP = 4
SLOTS = 6
STATIONS = 128
F32 = jnp.float32
I32 = jnp.int32


def iota(shape, dim):
    return lax.broadcasted_iota(I32, shape, dim)


def fold(tiles, at):
    lane, sub = iota((8, 128), 1), iota((8, 128), 0)
    rows = []
    for start in range(0, len(tiles), 16):
        gathered = jnp.zeros((8, 128), F32)
        for i, tile in enumerate(tiles[start : start + 16]):
            column = jnp.broadcast_to(tile[:, at : at + 1], (8, 128))
            gathered = jnp.where(lane == i * 8 + sub, column, gathered)
        rows.append(jnp.sum(gathered, axis=0, keepdims=True))
    return rows


def unfold(ref, first_row, tile):
    row = first_row + tile // 16
    spread = jnp.broadcast_to(ref[row : row + 1, :], (8, 128))
    return jnp.take_along_axis(spread, (tile % 16) * 8 + iota((8, 128), 0), axis=1)


def column(ref, first_row, k, r):
    first = (k * CR + r) * (ROWS // 8)
    return jnp.concatenate([unfold(ref, first_row, first + i) for i in range(ROWS // 8)], axis=0)


def tiles_of(ref, count, first=0):
    return [
        ref[first + k, r, 8 * i : 8 * i + 8, :]
        for k in range(count)
        for r in range(CR)
        for i in range(ROWS // 8)
    ]


def put_columns(tiles, left_ref, right_ref, first_row):
    for ref, at in ((left_ref, 0), (right_ref, CE - 1)):
        for i, row in enumerate(fold(tiles, at)):
            ref[first_row + i : first_row + i + 1, :] = row


def put_faces(u_ref, down_ref, up_ref, left_ref, right_ref):
    for k in range(3):
        down_ref[k] = u_ref[k, 0]
        up_ref[k] = u_ref[k, CR - 1]
    left_ref[...] = jnp.zeros_like(left_ref)
    right_ref[...] = jnp.zeros_like(right_ref)
    put_columns(tiles_of(u_ref, 3), left_ref, right_ref, 0)


def edge_rows(start, fields, out, room, sems):
    first, copies = 0, []
    for i, ref in enumerate(fields):
        count = ref.shape[0]
        copies.append(
            pltpu.make_async_copy(
                ref.at[:, :, pl.ds(start, 8), :], room.at[pl.ds(first, count)], sems.at[i]
            )
        )
        first += count
    for copy in copies:
        copy.start()

    def finish():
        for copy in copies:
            copy.wait()
        inner = slice(0, HALO) if start == 0 else slice(8 - HALO, 8)
        for f in range(first):
            for r in range(CR):
                spot = slice(HALO * (r % 2), HALO * (r % 2) + HALO)
                out[f, r // 2, spot, :] = room[f, r, inner, :]

    return finish


def high_kernel(cur, prv, mod, den, high, room, sems):
    edge_rows(CL - 8, (cur, prv, mod, den), high, room, sems)()


def pack_kernel(
    offsets_in, receivers_in, owners_in, traces_in, cur, prv, mod, den, out, low,
    room, sems, traces, words_in, trace_sem, word_sems,
):
    copy = pltpu.make_async_copy(traces_in, traces, trace_sem)
    copy.start()
    small = [
        pltpu.make_async_copy(ref, words_in.at[pl.ds(i, 1)], word_sems.at[i])
        for i, ref in enumerate((offsets_in, receivers_in, owners_in))
    ]
    for one in small:
        one.start()
    finish_low = edge_rows(0, (cur, prv, mod, den), low, room, sems)
    for one in small:
        one.wait()
    offset_row, q, owner_row = words_in[0:1], words_in[1:2], words_in[2:3]
    r, l, e = q // 2048, (q // 128) % CL, q % 128
    wide_sub, wide_lane = iota((128, 128), 0), iota((128, 128), 1)
    sheet = jnp.transpose(
        jnp.concatenate(
            [owner_row.astype(F32), offset_row.astype(F32), jnp.zeros((6, 128), F32)], axis=0
        )
    )
    owner_cols = jnp.broadcast_to(sheet[:, 0:1], (128, 128)).astype(I32)
    offsets = jnp.broadcast_to(sheet[:, 1:2], (128, 128)).astype(I32)
    same = (owner_cols == owner_row) & (wide_sub < wide_lane)
    rank = jnp.sum(jnp.where(same, 1.0, 0.0), axis=0, keepdims=True).astype(I32)

    lefts, lines = [], [e.astype(F32)]
    for shift in (-1, 0, 1):
        slot = (shift + 1) * CAP + rank
        half, j = slot // SLOTS, slot % SLOTS
        if shift == 0:
            row, near = l, l >= 0
        elif shift == -1:
            row, near = CL + l, l <= HALO - 2
        else:
            row, near = l + HALO + HALO, l >= CL - HALO + 1
        target = owner_row + 8 * shift
        ok = near & (target >= 0) & (target < 64)
        place = jnp.where(ok, half * 64 + target, -1)
        lefts.append(jnp.where(wide_sub == place, 1.0, 0.0))
        lines += [j.astype(F32), (r * ROWS + row).astype(F32)]
    sheet = jnp.transpose(jnp.concatenate(lines + [jnp.zeros((1, 128), F32)], axis=0))
    finish_low()

    inside = offsets % 128
    tile = offsets // 128 + jnp.where(wide_lane < inside, 1, 0)
    index = (inside + (wide_lane // 8) % STEPS) % 128
    copy.wait()
    window = jnp.broadcast_to(sheet[:, 0:1], (128, 128))
    for k in range(3):
        parts = [traces[k, :, 128 * i : 128 * i + 128] for i in range(4)]
        merged = jnp.where(
            tile == 0,
            parts[0],
            jnp.where(tile == 1, parts[1], jnp.where(tile == 2, parts[2], parts[3])),
        )
        picked = jnp.take_along_axis(merged, index, axis=1)
        window = jnp.where(wide_lane // 32 == k, picked, window)
    rights = []
    for i in range(3):
        slots = jnp.broadcast_to(sheet[:, 2 * i + 1 : 2 * i + 2], (128, 128)).astype(I32)
        cells = jnp.broadcast_to(sheet[:, 2 * i + 2 : 2 * i + 3], (128, 128))
        words = jnp.where((wide_lane >= 96) & (wide_lane < 104), cells, window)
        rights.append(jnp.where((wide_lane % 8 == slots) & (wide_lane < 112), words, 0.0))
    packed = lax.dot_general(
        jnp.concatenate(lefts, axis=1),
        jnp.concatenate(rights, axis=0),
        (((1,), (0,)), ((), ())),
        precision=lax.Precision.HIGHEST,
        preferred_element_type=F32,
    )
    out[:, 0, :128] = packed[:64]
    out[:, 0, 128:] = packed[64:]


def widen_kernel(
    cur, prv, mod, den, from_low, from_high, u, v, m, c, down, up, left, right
):
    lat = lax.axis_index("lat")
    has_low, has_high = lat > 0, lat < lax.axis_size("lat") - 1

    def ghosts(f, r):
        spot = slice(HALO * (r % 2), HALO * (r % 2) + HALO)
        return jnp.concatenate(
            [
                jnp.where(has_high, from_high[f, r // 2, spot, :], 0.0),
                jnp.where(has_low, from_low[f, r // 2, spot, :], 0.0),
            ],
            axis=0,
        )

    for r in range(CR):
        for k in range(3):
            u[k, r, 0:CL, :] = cur[k, r]
            u[k, r, CL:ROWS, :] = ghosts(k, r)
            v[k, r, 0:CL, :] = prv[k, r]
            v[k, r, CL:ROWS, :] = ghosts(3 + k, r)
        for j in range(4):
            m[j, r, 0:CL, :] = mod[j, r]
            m[j, r, CL:ROWS, :] = ghosts(6 + j, r)
        c[r, 0:CL, :] = STEP_SQUARE / den[r]
        spot = slice(HALO * (r % 2), HALO * (r % 2) + HALO)
        outer = STEP_SQUARE / jnp.concatenate(
            [from_high[10, r // 2, spot, :], from_low[10, r // 2, spot, :]], axis=0
        )
        present = jnp.where(iota((8, 128), 0) < HALO, has_high.astype(I32), has_low.astype(I32))
        c[r, CL:ROWS, :] = jnp.where(present > 0, outer, 0.0)
    for k in range(3):
        down[k] = u[k, 0]
        up[k] = u[k, CR - 1]
    for i, j in enumerate((0, 2)):
        down[3 + i] = m[j, 0]
        up[3 + i] = m[j, CR - 1]
    left[...] = jnp.zeros_like(left)
    right[...] = jnp.zeros_like(right)
    put_columns(tiles_of(u, 3), left, right, 0)
    put_columns(tiles_of(m, 3, 1), left, right, 3)


def force(k, r, u, low, high, at_left, at_right, ar, al, au, ad):
    jr, jl, je = TABLE[k]
    here = u[k, r]
    below = u[k, r - 1] if r > 0 else low[k]
    above = u[k, r + 1] if r < CR - 1 else high[k]
    total = ar[jr // 2, r + 1] * (above - here) - ar[jr // 2, r] * (here - below)
    flux = al[jl - 1, r] * (pltpu.roll(here, ROWS - 1, 0) - here)
    total = total + (flux - pltpu.roll(flux, 1, 0))
    lane = iota((ROWS, CE), 1)
    after = jnp.where(lane == CE - 1, column(at_right, 0, k, r), pltpu.roll(here, CE - 1, 1))
    before = jnp.where(lane == 0, column(at_left, 0, k, r), pltpu.roll(here, 1, 1))
    return total + (au[je - 1, r] * (after - here) + ad[je - 1, r] * (before - here))


def radial_ends(low, high, count):
    rad = lax.axis_index("rad")
    lows = [jnp.where(rad > 0, low[k], 0.0) for k in range(count)]
    highs = [
        jnp.where(rad < lax.axis_size("rad") - 1, high[k], 0.0) for k in range(count)
    ]
    return lows, highs


def prepare_kernel(u, v, m, c, low, high, at_left, at_right, ar, al, au, ad, following):
    lows, highs = radial_ends(low, high, 5)
    lane = iota((ROWS, CE), 1)
    for i, j in enumerate((0, 2)):
        layers = [lows[3 + i]] + [m[j, r] for r in range(CR)] + [highs[3 + i]]
        for face in range(CR + 1):
            ar[i, face] = 0.5 * (layers[face] + layers[face + 1])
    for j in (1, 2, 3):
        for r in range(CR):
            here = m[j, r]
            al[j - 1, r] = 0.5 * (here + pltpu.roll(here, ROWS - 1, 0))
            after = jnp.where(
                lane == CE - 1, column(at_right, 3, j - 1, r), pltpu.roll(here, CE - 1, 1)
            )
            before = jnp.where(lane == 0, column(at_left, 3, j - 1, r), pltpu.roll(here, 1, 1))
            au[j - 1, r] = 0.5 * (here + after)
            ad[j - 1, r] = 0.5 * (here + before)
    for k in range(3):
        for r in range(CR):
            total = force(k, r, u, lows, highs, at_left, at_right, ar, al, au, ad)
            following[k, r] = 2.0 * u[k, r] - v[k, r] + c[r] * total


def gather_sources(steps, got, weights, picks):
    turned = jnp.transpose(jnp.concatenate([got[:, 0, :128], got[:, 0, 128:]], axis=0))
    cell_rows, cell_lanes = iota((CR * ROWS, 128), 0), iota((CE, 128), 0)
    for j in range(SLOTS):
        span = slice(128 * j, 128 * j + 128)
        place = turned[96 + j : 97 + j].astype(I32)
        around = turned[104 + j : 105 + j].astype(I32)
        picks[:, span] = jnp.where(cell_lanes == around, 1.0, 0.0)
        here = cell_rows == place
        for i, t in enumerate(steps):
            for k in range(3):
                line = (k * STEPS + t) * 8 + j
                at = (i * 3 + k) * CR * ROWS
                weights[at : at + CR * ROWS, span] = jnp.where(here, turned[line : line + 1], 0.0)
    return lax.dot_general(
        weights[...],
        picks[...],
        (((1,), (1,)), ((), ())),
        precision=lax.Precision.HIGHEST,
        preferred_element_type=F32,
    )


def first_kernel(got, free, c, first, down, up, left, right, weights, picks):
    summed = gather_sources((0,), got, weights, picks)
    for k in range(3):
        for r in range(CR):
            at = (k * CR + r) * ROWS
            first[k, r] = free[k, r] + summed[at : at + ROWS] * c[r]
    put_faces(first, down, up, left, right)


def sources_kernel(got, c, sources, weights, picks):
    summed = gather_sources(range(1, STEPS), got, weights, picks)
    for t in range(STEPS - 1):
        for k in range(3):
            for r in range(CR):
                at = ((t * 3 + k) * CR + r) * ROWS
                sources[t, k, r] = summed[at : at + ROWS] * c[r]


def step_kernel(t, u, v, c, sources, low, high, at_left, at_right, ar, al, au, ad, *outs):
    lows, highs = radial_ends(low, high, 3)
    following = outs[0]
    last = t == STEPS - 1
    for k in range(3):
        for r in range(CR):
            total = force(k, r, u, lows, highs, at_left, at_right, ar, al, au, ad)
            value = 2.0 * u[k, r] - v[k, r] + c[r] * total + sources[t - 1, k, r]
            if last:
                following[k, r] = value[:CL]
                outs[1][k, r] = u[k, r, 0:CL, :]
            else:
                following[k, r] = value
    if not last:
        put_faces(following, *outs[1:])


def call(kernel, outs, args, scratch=(), hbm=0, us=1.0):
    vmem = pl.BlockSpec(memory_space=pltpu.VMEM)
    specs = [pl.BlockSpec(memory_space=pltpu.HBM)] * hbm + [vmem] * (len(args) - hbm)
    return pl.pallas_call(
        kernel,
        out_shape=[jax.ShapeDtypeStruct(shape, F32) for shape in outs],
        in_specs=specs,
        out_specs=[vmem] * len(outs),
        scratch_shapes=[pltpu.VMEM(s, F32) if isinstance(s, tuple) else s for s in scratch],
        cost_estimate=pl.CostEstimate(
            flops=0, bytes_accessed=int(us * 3_000_000), transcendentals=0
        ),
        compiler_params=pltpu.CompilerParams(vmem_limit_bytes=(60 if hbm else 32) * 1024 * 1024),
    )(*args)


def shifted(block, axis, by):
    count = lax.axis_size(axis)
    return lax.ppermute(block, axis, [(i, (i + by) % count) for i in range(count)])


def swap_faces(down, up, left, right):
    low = shifted(up, "rad", 1)
    high = shifted(down, "rad", -1)
    at_left = shifted(right, "span", 1)
    at_right = shifted(left, "span", -1)
    return low, high, at_left, at_right


def on_device(current, previous, moduli, density, traces, receivers, owners, offsets):
    wide = (3, CR, ROWS, CE)
    edge = (11, 2, 8, CE)
    faces = [(3, ROWS, CE), (3, ROWS, CE), (8, CE), (8, CE)]

    fields = (current, previous, moduli, density.reshape((1,) + density.shape))
    rooms = [(11, CR, 8, CE), pltpu.SemaphoreType.DMA((4,))]
    (high_rows,) = call(high_kernel, [edge], fields, scratch=rooms, hbm=4)
    from_low = shifted(high_rows, "lat", 1)
    packed, low_rows = call(
        pack_kernel,
        [(64, 1, 256), edge],
        (
            offsets.reshape(1, 128),
            receivers.reshape(1, 128),
            owners.reshape(1, 128),
            traces.transpose(1, 0, 2),
        )
        + fields,
        scratch=rooms
        + [
            (3, STATIONS, 512),
            pltpu.VMEM((8, 128), I32),
            pltpu.SemaphoreType.DMA(()),
            pltpu.SemaphoreType.DMA((3,)),
        ],
        hbm=8,
        us=2.0,
    )
    from_high = shifted(low_rows, "lat", -1)
    got = lax.all_to_all(packed, ("lat", "rad"), 0, 0, tiled=True)

    u, v, m, c, *ends = call(
        widen_kernel,
        [wide, wide, (4, CR, ROWS, CE), (CR, ROWS, CE)]
        + [(5, ROWS, CE), (5, ROWS, CE), (8, CE), (8, CE)],
        (current, previous, moduli, density, from_low, from_high),
    )
    *coefficients, free = call(
        prepare_kernel,
        [(2, CR + 1, ROWS, CE), wide, wide, wide, wide],
        (u, v, m, c, *swap_faces(*ends)),
    )
    cells = CR * ROWS
    first, *ends = call(
        first_kernel,
        [wide] + faces,
        (got, free, c),
        scratch=[(3 * cells, 128 * SLOTS), (CE, 128 * SLOTS)],
    )
    (sources,) = call(
        sources_kernel,
        [(STEPS - 1,) + wide],
        (got, c),
        scratch=[(3 * (STEPS - 1) * cells, 128 * SLOTS), (CE, 128 * SLOTS)],
        us=3.0,
    )
    v, u = u, first
    for t in range(1, STEPS):
        args = (u, v, c, sources, *swap_faces(*ends), *coefficients)

        def kernel(*refs, t=t):
            step_kernel(t, *refs)

        if t == STEPS - 1:
            return tuple(call(kernel, [(3, CR, CL, CE)] * 2, args))
        following, *ends = call(kernel, [wide] + faces, args)
        v, u = u, following


def solution(mesh):
    in_specs = (
        P(None, "rad", "lat", "span"),
        P(None, "rad", "lat", "span"),
        P(None, "rad", "lat", "span"),
        P("rad", "lat", "span"),
        P(("span", "lat", "rad"), None, None),
        P(("span", "lat", "rad")),
        P(("span", "lat", "rad"), None),
        P(("span", "lat", "rad")),
    )
    out_specs = (P(None, "rad", "lat", "span"), P(None, "rad", "lat", "span"))
    return jax.shard_map(
        on_device, mesh=mesh, in_specs=in_specs, out_specs=out_specs, check_vma=False
    )
```

```python
import jax
import jax.numpy as jnp
from jax import lax
from jax.experimental import pallas as pl
from jax.experimental.pallas import tpu as pltpu
from jax.sharding import PartitionSpec as P

STEPS = 4
STEP_SQUARE = 0.16
TABLE = ((0, 2, 2), (2, 1, 3), (2, 3, 1))
CR, CL, CE = 4, 16, 128
HALO = 4
ROWS = CL + 2 * HALO
CAP = 4
SLOTS = 6
STATIONS = 128
F32 = jnp.float32
I32 = jnp.int32


def iota(shape, dim):
    return lax.broadcasted_iota(I32, shape, dim)


LAYERS = CR + 2 * HALO
LEFT_PAD = 160


def radial_list(up):
    inner = range(1, CR) if up else range(CR - 1)
    full = range(CR)
    items = [("u", k, r) for k in range(3) for r in full]
    items += [("v", k, r) for k in range(3) for r in inner]
    items += [("c", 0, r) for r in inner]
    items += [("m", j, r) for j in (0, 2) for r in full]
    items += [("m", j, r) for j in (1, 3) for r in inner]
    return items


RADIAL = len(radial_list(True))


def column_list():
    items = [("u", k, r) for k in range(3) for r in range(1, LAYERS - 1)]
    items += [("v", k, r) for k in range(3) for r in range(2, LAYERS - 2)]
    items += [("c", 0, r) for r in range(2, LAYERS - 2)]
    items += [("m", j, r) for j in range(4) for r in range(1, LAYERS - 1)]
    for t in range(STEPS - 1):
        items += [("s%d" % t, k, r) for k in range(3) for r in range(t + 2, LAYERS - t - 2)]
    return items


def fold(layer, first):
    lane, sub = iota((8, 128), 1), iota((8, 128), 0)
    gathered = jnp.zeros((8, 128), F32)
    for i in range(ROWS // 8):
        part = jnp.take_along_axis(layer[8 * i : 8 * i + 8], first + lane % 4, axis=1)
        gathered = jnp.where(lane // 4 == 8 * i + sub, part, gathered)
    return jnp.sum(gathered, axis=0, keepdims=True)


def unfold(left, right):
    lane, sub = iota((8, 128), 1), iota((8, 128), 0)
    left, right = jnp.broadcast_to(left, (8, 128)), jnp.broadcast_to(right, (8, 128))
    parts = []
    for i in range(ROWS // 8):
        index = (8 * i + sub) * 4 + lane % 4
        parts.append(
            jnp.where(
                lane < 64,
                jnp.take_along_axis(right, index, axis=1),
                jnp.take_along_axis(left, index, axis=1),
            )
        )
    return jnp.concatenate(parts, axis=0)


def edge_rows(start, fields, out, room, sems):
    first, copies = 0, []
    for i, ref in enumerate(fields):
        count = ref.shape[0]
        copies.append(
            pltpu.make_async_copy(
                ref.at[:, :, pl.ds(start, 8), :], room.at[pl.ds(first, count)], sems.at[i]
            )
        )
        first += count
    for copy in copies:
        copy.start()

    def finish():
        for copy in copies:
            copy.wait()
        inner = slice(0, HALO) if start == 0 else slice(8 - HALO, 8)
        for f in range(first):
            for r in range(CR):
                spot = slice(HALO * (r % 2), HALO * (r % 2) + HALO)
                out[f, r // 2, spot, :] = room[f, r, inner, :]

    return finish


def high_kernel(cur, prv, mod, den, high, room, sems):
    edge_rows(CL - 8, (cur, prv, mod, den), high, room, sems)()


def pack_kernel(
    offsets_in, receivers_in, owners_in, traces_in, cur, prv, mod, den, out, low,
    room, sems, traces, words_in, trace_sem, word_sems,
):
    copy = pltpu.make_async_copy(traces_in, traces, trace_sem)
    copy.start()
    small = [
        pltpu.make_async_copy(ref, words_in.at[pl.ds(i, 1)], word_sems.at[i])
        for i, ref in enumerate((offsets_in, receivers_in, owners_in))
    ]
    for one in small:
        one.start()
    finish_low = edge_rows(0, (cur, prv, mod, den), low, room, sems)
    for one in small:
        one.wait()
    offset_row, q, owner_row = words_in[0:1], words_in[1:2], words_in[2:3]
    r, l, e = q // 2048, (q // 128) % CL, q % 128
    wide_sub, wide_lane = iota((128, 128), 0), iota((128, 128), 1)
    sheet = jnp.transpose(
        jnp.concatenate(
            [owner_row.astype(F32), offset_row.astype(F32), jnp.zeros((6, 128), F32)], axis=0
        )
    )
    owner_cols = jnp.broadcast_to(sheet[:, 0:1], (128, 128)).astype(I32)
    offsets = jnp.broadcast_to(sheet[:, 1:2], (128, 128)).astype(I32)
    same = (owner_cols == owner_row) & (wide_sub < wide_lane)
    rank = jnp.sum(jnp.where(same, 1.0, 0.0), axis=0, keepdims=True).astype(I32)

    lefts, lines = [], [e.astype(F32)]
    for shift in (-1, 0, 1):
        slot = (shift + 1) * CAP + rank
        half, j = slot // SLOTS, slot % SLOTS
        if shift == 0:
            row, near = l, l >= 0
        elif shift == -1:
            row, near = CL + l, l <= HALO - 2
        else:
            row, near = l + HALO + HALO, l >= CL - HALO + 1
        target = owner_row + 8 * shift
        ok = near & (target >= 0) & (target < 64)
        place = jnp.where(ok, half * 64 + target, -1)
        lefts.append(jnp.where(wide_sub == place, 1.0, 0.0))
        lines += [j.astype(F32), (r * ROWS + row).astype(F32)]
    sheet = jnp.transpose(jnp.concatenate(lines + [jnp.zeros((1, 128), F32)], axis=0))
    finish_low()

    inside = offsets % 128
    tile = offsets // 128 + jnp.where(wide_lane < inside, 1, 0)
    index = (inside + (wide_lane // 8) % STEPS) % 128
    copy.wait()
    window = jnp.broadcast_to(sheet[:, 0:1], (128, 128))
    for k in range(3):
        parts = [traces[k, :, 128 * i : 128 * i + 128] for i in range(4)]
        merged = jnp.where(
            tile == 0,
            parts[0],
            jnp.where(tile == 1, parts[1], jnp.where(tile == 2, parts[2], parts[3])),
        )
        picked = jnp.take_along_axis(merged, index, axis=1)
        window = jnp.where(wide_lane // 32 == k, picked, window)
    rights = []
    for i in range(3):
        slots = jnp.broadcast_to(sheet[:, 2 * i + 1 : 2 * i + 2], (128, 128)).astype(I32)
        cells = jnp.broadcast_to(sheet[:, 2 * i + 2 : 2 * i + 3], (128, 128))
        words = jnp.where((wide_lane >= 96) & (wide_lane < 104), cells, window)
        rights.append(jnp.where((wide_lane % 8 == slots) & (wide_lane < 112), words, 0.0))
    packed = lax.dot_general(
        jnp.concatenate(lefts, axis=1),
        jnp.concatenate(rights, axis=0),
        (((1,), (0,)), ((), ())),
        precision=lax.Precision.HIGHEST,
        preferred_element_type=F32,
    )
    out[:, 0, :128] = packed[:64]
    out[:, 0, 128:] = packed[64:]


def widen_kernel(cur, prv, mod, den, from_low, from_high, u, v, m, c, down, up):
    lat = lax.axis_index("lat")
    has_low, has_high = lat > 0, lat < lax.axis_size("lat") - 1

    def ghosts(f, r):
        spot = slice(HALO * (r % 2), HALO * (r % 2) + HALO)
        return jnp.concatenate(
            [
                jnp.where(has_high, from_high[f, r // 2, spot, :], 0.0),
                jnp.where(has_low, from_low[f, r // 2, spot, :], 0.0),
            ],
            axis=0,
        )

    for r in range(CR):
        for k in range(3):
            u[k, r, 0:CL, :] = cur[k, r]
            u[k, r, CL:ROWS, :] = ghosts(k, r)
            v[k, r, 0:CL, :] = prv[k, r]
            v[k, r, CL:ROWS, :] = ghosts(3 + k, r)
        for j in range(4):
            m[j, r, 0:CL, :] = mod[j, r]
            m[j, r, CL:ROWS, :] = ghosts(6 + j, r)
        c[0, r, 0:CL, :] = STEP_SQUARE / den[r]
        spot = slice(HALO * (r % 2), HALO * (r % 2) + HALO)
        outer = STEP_SQUARE / jnp.concatenate(
            [from_high[10, r // 2, spot, :], from_low[10, r // 2, spot, :]], axis=0
        )
        present = jnp.where(iota((8, 128), 0) < HALO, has_high.astype(I32), has_low.astype(I32))
        c[0, r, CL:ROWS, :] = jnp.where(present > 0, outer, 0.0)
    fields = dict(u=u, v=v, m=m, c=c)
    for message, is_up in ((down, False), (up, True)):
        for i, (name, k, r) in enumerate(radial_list(is_up)):
            message[i] = fields[name][k, r]


def turn_kernel(got, _, turned):
    turned[...] = jnp.transpose(jnp.concatenate([got[:, 0, :128], got[:, 0, 128:]], axis=0))


def thirds(x):
    high = x.astype(jnp.bfloat16).astype(F32)
    rest = x - high
    middle = rest.astype(jnp.bfloat16).astype(F32)
    return high, middle, rest - middle


def gather_sources(got, ranges, weights, picks):
    turned = got[...]
    parts = thirds(turned)
    cell_lanes = iota((CE, 128), 0)
    for j in range(SLOTS):
        place = turned[96 + j : 97 + j].astype(I32)
        around = turned[104 + j : 105 + j].astype(I32)
        pick = jnp.where(cell_lanes == around, 1.0, 0.0)
        for p in range(3):
            span = slice((p * SLOTS + j) * 128, (p * SLOTS + j + 1) * 128)
            picks[:, span] = pick
            at = 0
            for t, (low, high) in enumerate(ranges):
                count = (high - low) * ROWS
                here = iota((count, 128), 0) + low * ROWS == place
                for k in range(3):
                    line = (k * STEPS + t) * 8 + j
                    weights[at : at + count, span] = jnp.where(
                        here, parts[p][line : line + 1], 0.0
                    )
                    at += count
    return lax.dot_general(
        weights[...], picks[...], (((1,), (1,)), ((), ())), preferred_element_type=F32
    )


def own_kernel(got, c, *refs):
    sources, weights, picks = refs
    ranges = [(0, CR)] * STEPS
    summed = gather_sources(got, ranges, weights, picks)
    for t in range(STEPS):
        for k in range(3):
            for r in range(CR):
                at = ((t * 3 + k) * CR + r) * ROWS
                sources[t, k, r] = summed[at : at + ROWS] * c[0, r]


def source_span(t):
    return t + 1, LAYERS - t - 1


def assemble_kernel(
    u, v, m, c, own, low, high, low_list, high_list,
    wu, wv, wm, wc, ws, left, right, weights, picks,
):
    rad = lax.axis_index("rad")
    has_low, has_high = rad > 0, rad < lax.axis_size("rad") - 1
    pairs = dict(u=(u, wu), v=(v, wv), m=(m, wm), c=(c, wc))
    for narrow, wide in pairs.values():
        for k in range(narrow.shape[0]):
            for r in range(CR):
                wide[k, HALO + r] = narrow[k, r]
    for message, is_up, present in ((low, True, has_low), (high, False, has_high)):
        for i, (name, k, r) in enumerate(radial_list(is_up)):
            at = r if is_up else HALO + CR + r
            pairs[name][1][k, at] = jnp.where(present, message[i], 0.0)
    for t in range(STEPS):
        for k in range(3):
            for r in range(CR):
                ws[t, k, HALO + r] = own[t, k, r]
    lists = (
        (low_list, [(t + 1, CR) for t in range(STEPS - 1)], 0),
        (high_list, [(0, CR - 1 - t) for t in range(STEPS - 1)], HALO + CR),
    )
    for got, ranges, base in lists:
        summed = gather_sources(got, ranges, weights, picks)
        at = 0
        for t, (first, last) in enumerate(ranges):
            for k in range(3):
                for r in range(first, last):
                    ws[t, k, base + r] = summed[at : at + ROWS] * wc[0, base + r]
                    at += ROWS
    fields = dict(u=wu, v=wv, m=wm, c=wc)
    for t in range(STEPS):
        fields["s%d" % t] = ws.at[t]
    for i, (name, k, r) in enumerate(column_list()):
        layer = fields[name][k, r]
        left[i : i + 1, :] = fold(layer, 0)
        right[i : i + 1, :] = fold(layer, CE - 4)
    used = len(column_list())
    left[used:, :] = jnp.zeros((LEFT_PAD - used, 128), F32)
    right[used:, :] = jnp.zeros((LEFT_PAD - used, 128), F32)


def radial_faces(m, ar, first, last):
    for i, j in enumerate((0, 2)):
        for r in range(first, last + 1):
            ar[i, r] = 0.5 * (m[j, r - 1] + m[j, r])


def lateral_faces(m, al, first, last):
    for j in (1, 2, 3):
        for r in range(first, last + 1):
            al[j - 1, r] = 0.5 * (m[j, r] + pltpu.roll(m[j, r], ROWS - 1, 0))


def faces_kernel(m, ar, al):
    radial_faces(m, ar, 1, LAYERS - 1)
    lateral_faces(m, al, 1, LAYERS - 2)


def after(here, there):
    lane = iota((ROWS, CE), 1)
    a, b = pltpu.roll(here, CE - 1, 1), pltpu.roll(there, CE - 1, 1)
    return jnp.where(lane == CE - 1, b, a), jnp.where(lane == CE - 1, a, b)


def before(here, there):
    lane = iota((ROWS, CE), 1)
    a, b = pltpu.roll(here, 1, 1), pltpu.roll(there, 1, 1)
    return jnp.where(lane == 0, b, a), jnp.where(lane == 0, a, b)


def still(k, r, u, ar, al):
    jr, jl, _ = TABLE[k]
    here = u[k, r]
    total = ar[jr // 2, r + 1] * (u[k, r + 1] - here) - ar[jr // 2, r] * (here - u[k, r - 1])
    flux = al[jl - 1, r] * (pltpu.roll(here, ROWS - 1, 0) - here)
    return total + (flux - pltpu.roll(flux, 1, 0))


def steps_kernel(
    u, v, m, c, s, ar, al, at_left, at_right, final, before_final,
    gu, gv, gm, gc, gs, gar, gal, ae, gae, us, gus,
):
    ghosts = dict(u=gu, v=gv, m=gm, c=gc)
    for t in range(STEPS - 1):
        ghosts["s%d" % t] = gs.at[t]
    for i, (name, k, r) in enumerate(column_list()):
        ghosts[name][k, r] = unfold(at_left[i : i + 1, :], at_right[i : i + 1, :])
    radial_faces(gm, gar, 2, LAYERS - 2)
    lateral_faces(gm, gal, 2, LAYERS - 3)
    for j in (1, 2, 3):
        for r in range(1, LAYERS - 1):
            own, other = after(m[j, r], gm[j, r])
            ae[j - 1, r] = 0.5 * (m[j, r] + own)
            gae[j - 1, r] = 0.5 * (gm[j, r] + other)
    for t in range(STEPS):
        now, gnow = (u, gu) if t == 0 else (us.at[t - 1], gus.at[t - 1])
        old, gold = (v, gv) if t == 0 else (u, gu) if t == 1 else (us.at[t - 2], gus.at[t - 2])
        for k in range(3):
            je = TABLE[k][2] - 1
            for r in range(t + 1, LAYERS - t - 1):
                here, there = now[k, r], gnow[k, r]
                own, other = after(here, there)
                flux, gflux = ae[je, r] * (own - here), gae[je, r] * (other - there)
                own, other = before(flux, gflux)
                total = still(k, r, now, ar, al) + (flux - own)
                value = 2.0 * here - old[k, r] + c[0, r] * total + s[t, k, r]
                if t == STEPS - 1:
                    final[k, r - HALO] = value[:CL]
                    before_final[k, r - HALO] = here[:CL]
                    continue
                us[t, k, r] = value
                if t + 2 <= r < LAYERS - t - 2:
                    total = still(k, r, gnow, gar, gal) + (gflux - other)
                    gus[t, k, r] = 2.0 * there - gold[k, r] + gc[0, r] * total + gs[t, k, r]


def call(kernel, outs, args, scratch=(), hbm=0, us=1.0):
    vmem = pl.BlockSpec(memory_space=pltpu.VMEM)
    specs = [pl.BlockSpec(memory_space=pltpu.HBM)] * hbm + [vmem] * (len(args) - hbm)
    return pl.pallas_call(
        kernel,
        out_shape=[jax.ShapeDtypeStruct(shape, F32) for shape in outs],
        in_specs=specs,
        out_specs=[vmem] * len(outs),
        scratch_shapes=[pltpu.VMEM(s, F32) if isinstance(s, tuple) else s for s in scratch],
        cost_estimate=pl.CostEstimate(
            flops=0, bytes_accessed=int(us * 3_000_000), transcendentals=0
        ),
        compiler_params=pltpu.CompilerParams(vmem_limit_bytes=(60 if hbm else 32) * 1024 * 1024),
    )(*args)


def shifted(block, axis, by):
    count = lax.axis_size(axis)
    return lax.ppermute(block, axis, [(i, (i + by) % count) for i in range(count)])


def on_device(current, previous, moduli, density, traces, receivers, owners, offsets):
    edge = (11, 2, 8, CE)
    fields = (current, previous, moduli, density.reshape((1,) + density.shape))
    rooms = [(11, CR, 8, CE), pltpu.SemaphoreType.DMA((4,))]
    (high_rows,) = call(high_kernel, [edge], fields, scratch=rooms, hbm=4)
    from_low = shifted(high_rows, "lat", 1)
    packed, low_rows = call(
        pack_kernel,
        [(64, 1, 256), edge],
        (
            offsets.reshape(1, 128),
            receivers.reshape(1, 128),
            owners.reshape(1, 128),
            traces.transpose(1, 0, 2),
        )
        + fields,
        scratch=rooms
        + [
            (3, STATIONS, 512),
            pltpu.VMEM((8, 128), I32),
            pltpu.SemaphoreType.DMA(()),
            pltpu.SemaphoreType.DMA((3,)),
        ],
        hbm=8,
        us=2.0,
    )
    from_high = shifted(low_rows, "lat", -1)
    got = lax.all_to_all(packed, ("lat", "rad"), 0, 0, tiled=True)

    def block(*lead):
        return lead + (ROWS, CE)

    u, v, m, c, down, up = call(
        widen_kernel,
        [block(3, CR), block(3, CR), block(4, CR), block(1, CR), block(RADIAL), block(RADIAL)],
        (current, previous, moduli, density, from_low, from_high),
    )
    low = shifted(up, "rad", 1)
    high = shifted(down, "rad", -1)
    (got,) = call(turn_kernel, [(128, 128)], (got, c))
    low_list = shifted(got, "rad", 1)
    high_list = shifted(got, "rad", -1)
    lanes = 3 * SLOTS * 128
    (own,) = call(
        own_kernel,
        [block(STEPS, 3, CR)],
        (got, c),
        scratch=[(3 * STEPS * CR * ROWS, lanes), (CE, lanes)],
        us=3.0,
    )
    wu, wv, wm, wc, ws, left, right = call(
        assemble_kernel,
        [block(3, LAYERS), block(3, LAYERS), block(4, LAYERS), block(1, LAYERS)]
        + [block(STEPS, 3, LAYERS), (LEFT_PAD, 128), (LEFT_PAD, 128)],
        (u, v, m, c, own, low, high, low_list, high_list),
        scratch=[(3 * 6 * ROWS, lanes), (CE, lanes)],
        us=3.0,
    )
    at_left = shifted(right, "span", 1)
    at_right = shifted(left, "span", -1)
    ar, al = call(faces_kernel, [block(2, LAYERS), block(3, LAYERS)], (wm,))
    return tuple(
        call(
            steps_kernel,
            [(3, CR, CL, CE)] * 2,
            (wu, wv, wm, wc, ws, ar, al, at_left, at_right),
            scratch=[block(3, LAYERS), block(3, LAYERS), block(4, LAYERS), block(1, LAYERS)]
            + [block(STEPS - 1, 3, LAYERS), block(2, LAYERS), block(3, LAYERS)]
            + [block(3, LAYERS), block(3, LAYERS)]
            + [block(STEPS - 1, 3, LAYERS), block(STEPS - 1, 3, LAYERS)],
            us=5.0,
        )
    )


def solution(mesh):
    in_specs = (
        P(None, "rad", "lat", "span"),
        P(None, "rad", "lat", "span"),
        P(None, "rad", "lat", "span"),
        P("rad", "lat", "span"),
        P(("span", "lat", "rad"), None, None),
        P(("span", "lat", "rad")),
        P(("span", "lat", "rad"), None),
        P(("span", "lat", "rad")),
    )
    out_specs = (P(None, "rad", "lat", "span"), P(None, "rad", "lat", "span"))
    return jax.shard_map(
        on_device, mesh=mesh, in_specs=in_specs, out_specs=out_specs, check_vma=False
    )
```

```python
import jax
import jax.numpy as jnp
from jax import lax
from jax.experimental import pallas as pl
from jax.experimental.pallas import tpu as pltpu
from jax.sharding import PartitionSpec as P

STEPS = 4
STEP_SQUARE = 0.16
TABLE = ((0, 2, 2), (2, 1, 3), (2, 3, 1))
CR, CL, CE = 4, 16, 128
HALO = 4
ROWS = CL + 2 * HALO
CAP = 4
SLOTS = 6
STATIONS = 128
F32 = jnp.float32
I32 = jnp.int32


def iota(shape, dim):
    return lax.broadcasted_iota(I32, shape, dim)


def fold(tiles, at):
    lane, sub = iota((8, 128), 1), iota((8, 128), 0)
    rows = []
    for start in range(0, len(tiles), 16):
        gathered = jnp.zeros((8, 128), F32)
        for i, tile in enumerate(tiles[start : start + 16]):
            column = jnp.broadcast_to(tile[:, at : at + 1], (8, 128))
            gathered = jnp.where(lane == i * 8 + sub, column, gathered)
        rows.append(jnp.sum(gathered, axis=0, keepdims=True))
    return rows


def unfold(ref, first_row, tile):
    row = first_row + tile // 16
    spread = jnp.broadcast_to(ref[row : row + 1, :], (8, 128))
    return jnp.take_along_axis(spread, (tile % 16) * 8 + iota((8, 128), 0), axis=1)


def column(ref, first_row, k, r):
    first = (k * CR + r) * (ROWS // 8)
    return jnp.concatenate([unfold(ref, first_row, first + i) for i in range(ROWS // 8)], axis=0)


def tiles_of(ref, count, first=0):
    return [
        ref[first + k, r, 8 * i : 8 * i + 8, :]
        for k in range(count)
        for r in range(CR)
        for i in range(ROWS // 8)
    ]


def put_columns(tiles, left_ref, right_ref, first_row):
    for ref, at in ((left_ref, 0), (right_ref, CE - 1)):
        for i, row in enumerate(fold(tiles, at)):
            ref[first_row + i : first_row + i + 1, :] = row


def rad_is_even():
    return lax.axis_index("rad") % 2 == 0


def put_layers(ref, ks, even_ref, odd_ref, first=0):
    top = jnp.where(rad_is_even(), CR - 1, 0)
    rows = even_ref.shape[1]
    for i, k in enumerate(ks):
        even_ref[first + i] = ref[k, top, :rows, :]
        odd_ref[first + i] = ref[k, CR - 1 - top, :rows, :]


def put_faces(u_ref, even_ref, odd_ref, left_ref, right_ref):
    put_layers(u_ref, range(3), even_ref, odd_ref)
    left_ref[...] = jnp.zeros_like(left_ref)
    right_ref[...] = jnp.zeros_like(right_ref)
    put_columns(tiles_of(u_ref, 3), left_ref, right_ref, 0)


def edge_rows(start, fields, out, room, sems):
    first, copies = 0, []
    for i, ref in enumerate(fields):
        count = ref.shape[0]
        copies.append(
            pltpu.make_async_copy(
                ref.at[:, :, pl.ds(start, 8), :], room.at[pl.ds(first, count)], sems.at[i]
            )
        )
        first += count
    for copy in copies:
        copy.start()

    def finish():
        for copy in copies:
            copy.wait()
        inner = slice(0, HALO) if start == 0 else slice(8 - HALO, 8)
        for f in range(first):
            for r in range(CR):
                spot = slice(HALO * (r % 2), HALO * (r % 2) + HALO)
                out[f, r // 2, spot, :] = room[f, r, inner, :]

    return finish


def high_kernel(cur, prv, mod, den, high, room, sems):
    edge_rows(CL - 8, (cur, prv, mod, den), high, room, sems)()


def pack_kernel(
    offsets_in, receivers_in, owners_in, traces_in, cur, prv, mod, den, out, low,
    room, sems, traces, words_in, trace_sem, word_sems,
):
    copy = pltpu.make_async_copy(traces_in, traces, trace_sem)
    copy.start()
    small = [
        pltpu.make_async_copy(ref, words_in.at[pl.ds(i, 1)], word_sems.at[i])
        for i, ref in enumerate((offsets_in, receivers_in, owners_in))
    ]
    for one in small:
        one.start()
    finish_low = edge_rows(0, (cur, prv, mod, den), low, room, sems)
    for one in small:
        one.wait()
    offset_row, q, owner_row = words_in[0:1], words_in[1:2], words_in[2:3]
    r, l, e = q // 2048, (q // 128) % CL, q % 128
    wide_sub, wide_lane = iota((128, 128), 0), iota((128, 128), 1)
    sheet = jnp.transpose(
        jnp.concatenate(
            [owner_row.astype(F32), offset_row.astype(F32), jnp.zeros((6, 128), F32)], axis=0
        )
    )
    owner_cols = jnp.broadcast_to(sheet[:, 0:1], (128, 128)).astype(I32)
    offsets = jnp.broadcast_to(sheet[:, 1:2], (128, 128)).astype(I32)
    same = (owner_cols == owner_row) & (wide_sub < wide_lane)
    rank = jnp.sum(jnp.where(same, 1.0, 0.0), axis=0, keepdims=True).astype(I32)

    lefts, lines = [], [e.astype(F32)]
    for shift in (-1, 0, 1):
        slot = (shift + 1) * CAP + rank
        half, j = slot // SLOTS, slot % SLOTS
        if shift == 0:
            row, near = l, l >= 0
        elif shift == -1:
            row, near = CL + l, l <= HALO - 2
        else:
            row, near = l + HALO + HALO, l >= CL - HALO + 1
        target = owner_row + 8 * shift
        ok = near & (target >= 0) & (target < 64)
        place = jnp.where(ok, half * 64 + target, -1)
        lefts.append(jnp.where(wide_sub == place, 1.0, 0.0))
        lines += [j.astype(F32), (r * ROWS + row).astype(F32)]
    sheet = jnp.transpose(jnp.concatenate(lines + [jnp.zeros((1, 128), F32)], axis=0))
    finish_low()

    inside = offsets % 128
    tile = offsets // 128 + jnp.where(wide_lane < inside, 1, 0)
    index = (inside + (wide_lane // 8) % STEPS) % 128
    copy.wait()
    window = jnp.broadcast_to(sheet[:, 0:1], (128, 128))
    for k in range(3):
        parts = [traces[k, :, 128 * i : 128 * i + 128] for i in range(4)]
        merged = jnp.where(
            tile == 0,
            parts[0],
            jnp.where(tile == 1, parts[1], jnp.where(tile == 2, parts[2], parts[3])),
        )
        picked = jnp.take_along_axis(merged, index, axis=1)
        window = jnp.where(wide_lane // 32 == k, picked, window)
    rights = []
    for i in range(3):
        slots = jnp.broadcast_to(sheet[:, 2 * i + 1 : 2 * i + 2], (128, 128)).astype(I32)
        cells = jnp.broadcast_to(sheet[:, 2 * i + 2 : 2 * i + 3], (128, 128))
        words = jnp.where((wide_lane >= 96) & (wide_lane < 104), cells, window)
        rights.append(jnp.where((wide_lane % 8 == slots) & (wide_lane < 112), words, 0.0))
    packed = lax.dot_general(
        jnp.concatenate(lefts, axis=1),
        jnp.concatenate(rights, axis=0),
        (((1,), (0,)), ((), ())),
        precision=lax.Precision.HIGHEST,
        preferred_element_type=F32,
    )
    out[:, 0, :128] = packed[:64]
    out[:, 0, 128:] = packed[64:]


def widen_kernel(
    cur, prv, mod, den, from_low, from_high, u, v, m, c, even, odd, left, right
):
    lat = lax.axis_index("lat")
    has_low, has_high = lat > 0, lat < lax.axis_size("lat") - 1

    def ghosts(f, r):
        spot = slice(HALO * (r % 2), HALO * (r % 2) + HALO)
        return jnp.concatenate(
            [
                jnp.where(has_high, from_high[f, r // 2, spot, :], 0.0),
                jnp.where(has_low, from_low[f, r // 2, spot, :], 0.0),
            ],
            axis=0,
        )

    for r in range(CR):
        for k in range(3):
            u[k, r, 0:CL, :] = cur[k, r]
            u[k, r, CL:ROWS, :] = ghosts(k, r)
            v[k, r, 0:CL, :] = prv[k, r]
            v[k, r, CL:ROWS, :] = ghosts(3 + k, r)
        for j in range(4):
            m[j, r, 0:CL, :] = mod[j, r]
            m[j, r, CL:ROWS, :] = ghosts(6 + j, r)
        c[r, 0:CL, :] = STEP_SQUARE / den[r]
        spot = slice(HALO * (r % 2), HALO * (r % 2) + HALO)
        outer = STEP_SQUARE / jnp.concatenate(
            [from_high[10, r // 2, spot, :], from_low[10, r // 2, spot, :]], axis=0
        )
        present = jnp.where(iota((8, 128), 0) < HALO, has_high.astype(I32), has_low.astype(I32))
        c[r, CL:ROWS, :] = jnp.where(present > 0, outer, 0.0)
    put_layers(u, range(3), even, odd)
    put_layers(m, (0, 2), even, odd, 3)
    left[...] = jnp.zeros_like(left)
    right[...] = jnp.zeros_like(right)
    put_columns(tiles_of(u, 3), left, right, 0)
    put_columns(tiles_of(m, 3, 1), left, right, 3)


def force(k, r, u, low, high, at_left, at_right, ar, al, au, ad):
    jr, jl, je = TABLE[k]
    here = u[k, r]
    below = u[k, r - 1] if r > 0 else low[k]
    above = u[k, r + 1] if r < CR - 1 else high[k]
    total = ar[jr // 2, r + 1] * (above - here) - ar[jr // 2, r] * (here - below)
    flux = al[jl - 1, r] * (pltpu.roll(here, ROWS - 1, 0) - here)
    total = total + (flux - pltpu.roll(flux, 1, 0))
    lane = iota((ROWS, CE), 1)
    after = jnp.where(lane == CE - 1, column(at_right, 0, k, r), pltpu.roll(here, CE - 1, 1))
    before = jnp.where(lane == 0, column(at_left, 0, k, r), pltpu.roll(here, 1, 1))
    return total + (au[je - 1, r] * (after - here) + ad[je - 1, r] * (before - here))


def radial_ends(even, odd, count):
    rad, is_even = lax.axis_index("rad"), rad_is_even()
    lows, highs = [], []
    for k in range(count):
        low = jnp.where(is_even, odd[k], even[k])
        high = jnp.where(is_even, even[k], odd[k])
        lows.append(jnp.where(rad > 0, low, 0.0))
        highs.append(jnp.where(rad < lax.axis_size("rad") - 1, high, 0.0))
    return lows, highs


def prepare_kernel(u, v, m, c, even, odd, at_left, at_right, ar, al, au, ad, following):
    lows, highs = radial_ends(even, odd, 5)
    lane = iota((ROWS, CE), 1)
    for i, j in enumerate((0, 2)):
        layers = [lows[3 + i]] + [m[j, r] for r in range(CR)] + [highs[3 + i]]
        for face in range(CR + 1):
            ar[i, face] = 0.5 * (layers[face] + layers[face + 1])
    for j in (1, 2, 3):
        for r in range(CR):
            here = m[j, r]
            al[j - 1, r] = 0.5 * (here + pltpu.roll(here, ROWS - 1, 0))
            after = jnp.where(
                lane == CE - 1, column(at_right, 3, j - 1, r), pltpu.roll(here, CE - 1, 1)
            )
            before = jnp.where(lane == 0, column(at_left, 3, j - 1, r), pltpu.roll(here, 1, 1))
            au[j - 1, r] = 0.5 * (here + after)
            ad[j - 1, r] = 0.5 * (here + before)
    for k in range(3):
        for r in range(CR):
            total = force(k, r, u, lows, highs, at_left, at_right, ar, al, au, ad)
            following[k, r] = 2.0 * u[k, r] - v[k, r] + c[r] * total


def thirds(x):
    high = x.astype(jnp.bfloat16).astype(F32)
    rest = x - high
    middle = rest.astype(jnp.bfloat16).astype(F32)
    return high, middle, rest - middle


def gather_sources(steps, got, weights, picks):
    turned = jnp.transpose(jnp.concatenate([got[:, 0, :128], got[:, 0, 128:]], axis=0))
    parts = thirds(turned)
    cell_rows, cell_lanes = iota((CR * ROWS, 128), 0), iota((CE, 128), 0)
    for j in range(SLOTS):
        place = turned[96 + j : 97 + j].astype(I32)
        around = turned[104 + j : 105 + j].astype(I32)
        pick = jnp.where(cell_lanes == around, 1.0, 0.0)
        here = cell_rows == place
        for p in range(3):
            span = slice((p * SLOTS + j) * 128, (p * SLOTS + j + 1) * 128)
            picks[:, span] = pick
            for i, t in enumerate(steps):
                for k in range(3):
                    line = (k * STEPS + t) * 8 + j
                    at = (i * 3 + k) * CR * ROWS
                    weights[at : at + CR * ROWS, span] = jnp.where(
                        here, parts[p][line : line + 1], 0.0
                    )
    return lax.dot_general(
        weights[...], picks[...], (((1,), (1,)), ((), ())), preferred_element_type=F32
    )


def first_kernel(got, free, c, first, even, odd, left, right, weights, picks):
    summed = gather_sources((0,), got, weights, picks)
    for k in range(3):
        for r in range(CR):
            at = (k * CR + r) * ROWS
            first[k, r] = free[k, r] + summed[at : at + ROWS] * c[r]
    put_faces(first, even, odd, left, right)


def sources_kernel(got, c, sources, weights, picks):
    summed = gather_sources(range(1, STEPS), got, weights, picks)
    for t in range(STEPS - 1):
        for k in range(3):
            for r in range(CR):
                at = ((t * 3 + k) * CR + r) * ROWS
                sources[t, k, r] = summed[at : at + ROWS] * c[r]


def step_kernel(t, u, v, c, sources, even, odd, at_left, at_right, ar, al, au, ad, *outs):
    lows, highs = radial_ends(even, odd, 3)
    following = outs[0]
    last = t == STEPS - 1
    for k in range(3):
        for r in range(CR):
            total = force(k, r, u, lows, highs, at_left, at_right, ar, al, au, ad)
            value = 2.0 * u[k, r] - v[k, r] + c[r] * total + sources[t - 1, k, r]
            if last:
                following[k, r] = value[:CL]
                outs[1][k, r] = u[k, r, 0:CL, :]
            else:
                following[k, r] = value
    if not last:
        put_faces(following, *outs[1:])


def call(kernel, outs, args, scratch=(), hbm=0, us=1.0):
    vmem = pl.BlockSpec(memory_space=pltpu.VMEM)
    specs = [pl.BlockSpec(memory_space=pltpu.HBM)] * hbm + [vmem] * (len(args) - hbm)
    return pl.pallas_call(
        kernel,
        out_shape=[jax.ShapeDtypeStruct(shape, F32) for shape in outs],
        in_specs=specs,
        out_specs=[vmem] * len(outs),
        scratch_shapes=[pltpu.VMEM(s, F32) if isinstance(s, tuple) else s for s in scratch],
        cost_estimate=pl.CostEstimate(
            flops=0, bytes_accessed=int(us * 3_000_000), transcendentals=0
        ),
        compiler_params=pltpu.CompilerParams(vmem_limit_bytes=(60 if hbm else 32) * 1024 * 1024),
    )(*args)


def shifted(block, axis, by):
    count = lax.axis_size(axis)
    return lax.ppermute(block, axis, [(i, (i + by) % count) for i in range(count)])


def swapped(block, axis, odd):
    count = lax.axis_size(axis)
    pairs = [(i, (i + (1 if (i + odd) % 2 == 0 else -1)) % count) for i in range(count)]
    return lax.ppermute(block, axis, pairs)


def swap_faces(even, odd, left, right):
    even, odd = swapped(even, "rad", 0), swapped(odd, "rad", 1)
    at_left = shifted(right, "span", 1)
    at_right = shifted(left, "span", -1)
    return even, odd, at_left, at_right


def on_device(current, previous, moduli, density, traces, receivers, owners, offsets):
    wide = (3, CR, ROWS, CE)
    edge = (11, 2, 8, CE)
    faces = [(3, ROWS, CE), (3, ROWS, CE), (8, CE), (8, CE)]

    fields = (current, previous, moduli, density.reshape((1,) + density.shape))
    rooms = [(11, CR, 8, CE), pltpu.SemaphoreType.DMA((4,))]
    (high_rows,) = call(high_kernel, [edge], fields, scratch=rooms, hbm=4)
    from_low = shifted(high_rows, "lat", 1)
    packed, low_rows = call(
        pack_kernel,
        [(64, 1, 256), edge],
        (
            offsets.reshape(1, 128),
            receivers.reshape(1, 128),
            owners.reshape(1, 128),
            traces.transpose(1, 0, 2),
        )
        + fields,
        scratch=rooms
        + [
            (3, STATIONS, 512),
            pltpu.VMEM((8, 128), I32),
            pltpu.SemaphoreType.DMA(()),
            pltpu.SemaphoreType.DMA((3,)),
        ],
        hbm=8,
        us=2.0,
    )
    from_high = shifted(low_rows, "lat", -1)
    got = lax.all_to_all(packed, ("lat", "rad"), 0, 0, tiled=True)

    u, v, m, c, *ends = call(
        widen_kernel,
        [wide, wide, (4, CR, ROWS, CE), (CR, ROWS, CE)]
        + [(5, ROWS, CE), (5, ROWS, CE), (8, CE), (8, CE)],
        (current, previous, moduli, density, from_low, from_high),
    )
    *coefficients, free = call(
        prepare_kernel,
        [(2, CR + 1, ROWS, CE), wide, wide, wide, wide],
        (u, v, m, c, *swap_faces(*ends)),
    )
    cells, lanes = CR * ROWS, 3 * SLOTS * 128
    first, *ends = call(
        first_kernel,
        [wide] + faces,
        (got, free, c),
        scratch=[(3 * cells, lanes), (CE, lanes)],
    )
    (sources,) = call(
        sources_kernel,
        [(STEPS - 1,) + wide],
        (got, c),
        scratch=[(3 * (STEPS - 1) * cells, lanes), (CE, lanes)],
        us=3.0,
    )
    v, u = u, first
    for t in range(1, STEPS):
        args = (u, v, c, sources, *swap_faces(*ends), *coefficients)

        def kernel(*refs, t=t):
            step_kernel(t, *refs)

        if t == STEPS - 1:
            return tuple(call(kernel, [(3, CR, CL, CE)] * 2, args))
        following, *ends = call(kernel, [wide] + faces, args)
        v, u = u, following


def solution(mesh):
    in_specs = (
        P(None, "rad", "lat", "span"),
        P(None, "rad", "lat", "span"),
        P(None, "rad", "lat", "span"),
        P("rad", "lat", "span"),
        P(("span", "lat", "rad"), None, None),
        P(("span", "lat", "rad")),
        P(("span", "lat", "rad"), None),
        P(("span", "lat", "rad")),
    )
    out_specs = (P(None, "rad", "lat", "span"), P(None, "rad", "lat", "span"))
    return jax.shard_map(
        on_device, mesh=mesh, in_specs=in_specs, out_specs=out_specs, check_vma=False
    )
```

```python
import jax
import jax.numpy as jnp
from jax import lax
from jax.experimental import pallas as pl
from jax.experimental.pallas import tpu as pltpu
from jax.sharding import PartitionSpec as P

STEPS = 4
STEP_SQUARE = 0.16
TABLE = ((0, 2, 2), (2, 1, 3), (2, 3, 1))
CR, CL, CE = 4, 16, 128
HALO = 4
ROWS = CL + 2 * HALO
CAP = 4
SLOTS = 6
STATIONS = 128
F32 = jnp.float32
I32 = jnp.int32


def iota(shape, dim):
    return lax.broadcasted_iota(I32, shape, dim)


def fold(tiles, at):
    lane, sub = iota((8, 128), 1), iota((8, 128), 0)
    rows = []
    for start in range(0, len(tiles), 16):
        gathered = jnp.zeros((8, 128), F32)
        for i, tile in enumerate(tiles[start : start + 16]):
            column = jnp.broadcast_to(tile[:, at : at + 1], (8, 128))
            gathered = jnp.where(lane == i * 8 + sub, column, gathered)
        rows.append(jnp.sum(gathered, axis=0, keepdims=True))
    return rows


def unfold(ref, first_row, tile):
    row = first_row + tile // 16
    spread = jnp.broadcast_to(ref[row : row + 1, :], (8, 128))
    return jnp.take_along_axis(spread, (tile % 16) * 8 + iota((8, 128), 0), axis=1)


def column(ref, first_row, k, r):
    first = (k * CR + r) * (ROWS // 8)
    return jnp.concatenate([unfold(ref, first_row, first + i) for i in range(ROWS // 8)], axis=0)


def tiles_of(ref, count, first=0):
    return [
        ref[first + k, r, 8 * i : 8 * i + 8, :]
        for k in range(count)
        for r in range(CR)
        for i in range(ROWS // 8)
    ]


def put_columns(tiles, left_ref, right_ref, first_row):
    for ref, at in ((left_ref, 0), (right_ref, CE - 1)):
        for i, row in enumerate(fold(tiles, at)):
            ref[first_row + i : first_row + i + 1, :] = row


def is_even(axis):
    return lax.axis_index(axis) % 2 == 0


def put_layers(ref, ks, even_ref, odd_ref, first=0):
    top = jnp.where(is_even("rad"), CR - 1, 0)
    rows = even_ref.shape[1]
    for i, k in enumerate(ks):
        even_ref[first + i] = ref[k, top, :rows, :]
        odd_ref[first + i] = ref[k, CR - 1 - top, :rows, :]


def put_faces(u_ref, even_ref, odd_ref, left_ref, right_ref):
    put_layers(u_ref, range(3), even_ref, odd_ref)
    left_ref[...] = jnp.zeros_like(left_ref)
    right_ref[...] = jnp.zeros_like(right_ref)
    put_columns(tiles_of(u_ref, 3), left_ref, right_ref, 0)


def edge_rows(upper, fields, out, room, sems):
    first, copies = 0, []
    start = pl.multiple_of(jnp.where(upper, CL - 8, 0), 8)
    for i, ref in enumerate(fields):
        count = ref.shape[0]
        copies.append(
            pltpu.make_async_copy(
                ref.at[:, :, pl.ds(start, 8), :], room.at[pl.ds(first, count)], sems.at[i]
            )
        )
        first += count
    for copy in copies:
        copy.start()

    def finish():
        for copy in copies:
            copy.wait()
        for f in range(first):
            for r in range(CR):
                spot = slice(HALO * (r % 2), HALO * (r % 2) + HALO)
                out[f, r // 2, spot, :] = jnp.where(
                    upper, room[f, r, 8 - HALO : 8, :], room[f, r, 0:HALO, :]
                )

    return finish


def even_edge_kernel(cur, prv, mod, den, edge, room, sems):
    edge_rows(is_even("lat"), (cur, prv, mod, den), edge, room, sems)()


def pack_kernel(
    offsets_in, receivers_in, owners_in, traces_in, cur, prv, mod, den, out, edge,
    room, sems, traces, words_in, trace_sem, word_sems,
):
    copy = pltpu.make_async_copy(traces_in, traces, trace_sem)
    copy.start()
    small = [
        pltpu.make_async_copy(ref, words_in.at[pl.ds(i, 1)], word_sems.at[i])
        for i, ref in enumerate((offsets_in, receivers_in, owners_in))
    ]
    for one in small:
        one.start()
    finish_edge = edge_rows(~is_even("lat"), (cur, prv, mod, den), edge, room, sems)
    for one in small:
        one.wait()
    offset_row, q, owner_row = words_in[0:1], words_in[1:2], words_in[2:3]
    r, l, e = q // 2048, (q // 128) % CL, q % 128
    wide_sub, wide_lane = iota((128, 128), 0), iota((128, 128), 1)
    sheet = jnp.transpose(
        jnp.concatenate(
            [owner_row.astype(F32), offset_row.astype(F32), jnp.zeros((6, 128), F32)], axis=0
        )
    )
    owner_cols = jnp.broadcast_to(sheet[:, 0:1], (128, 128)).astype(I32)
    offsets = jnp.broadcast_to(sheet[:, 1:2], (128, 128)).astype(I32)
    same = (owner_cols == owner_row) & (wide_sub < wide_lane)
    rank = jnp.sum(jnp.where(same, 1.0, 0.0), axis=0, keepdims=True).astype(I32)

    lefts, lines = [], [e.astype(F32)]
    for shift in (-1, 0, 1):
        slot = (shift + 1) * CAP + rank
        half, j = slot // SLOTS, slot % SLOTS
        if shift == 0:
            row, near = l, l >= 0
        elif shift == -1:
            row, near = CL + l, l <= HALO - 2
        else:
            row, near = l + HALO + HALO, l >= CL - HALO + 1
        target = owner_row + 8 * shift
        ok = near & (target >= 0) & (target < 64)
        place = jnp.where(ok, half * 64 + target, -1)
        lefts.append(jnp.where(wide_sub == place, 1.0, 0.0))
        lines += [j.astype(F32), (r * ROWS + row).astype(F32)]
    sheet = jnp.transpose(jnp.concatenate(lines + [jnp.zeros((1, 128), F32)], axis=0))
    finish_edge()

    inside = offsets % 128
    tile = offsets // 128 + jnp.where(wide_lane < inside, 1, 0)
    index = (inside + (wide_lane // 8) % STEPS) % 128
    copy.wait()
    window = jnp.broadcast_to(sheet[:, 0:1], (128, 128))
    for k in range(3):
        parts = [traces[k, :, 128 * i : 128 * i + 128] for i in range(4)]
        merged = jnp.where(
            tile == 0,
            parts[0],
            jnp.where(tile == 1, parts[1], jnp.where(tile == 2, parts[2], parts[3])),
        )
        picked = jnp.take_along_axis(merged, index, axis=1)
        window = jnp.where(wide_lane // 32 == k, picked, window)
    rights = []
    for i in range(3):
        slots = jnp.broadcast_to(sheet[:, 2 * i + 1 : 2 * i + 2], (128, 128)).astype(I32)
        cells = jnp.broadcast_to(sheet[:, 2 * i + 2 : 2 * i + 3], (128, 128))
        words = jnp.where((wide_lane >= 96) & (wide_lane < 104), cells, window)
        rights.append(jnp.where((wide_lane % 8 == slots) & (wide_lane < 112), words, 0.0))
    packed = lax.dot_general(
        jnp.concatenate(lefts, axis=1),
        jnp.concatenate(rights, axis=0),
        (((1,), (0,)), ((), ())),
        precision=lax.Precision.HIGHEST,
        preferred_element_type=F32,
    )
    out[:, 0, :128] = packed[:64]
    out[:, 0, 128:] = packed[64:]


def widen_kernel(
    cur, prv, mod, den, by_even, by_odd, u, v, m, c, even, odd, left, right
):
    lat = lax.axis_index("lat")
    has_low, has_high = lat > 0, lat < lax.axis_size("lat") - 1
    even_lat = is_even("lat")

    def received(f, r):
        spot = slice(HALO * (r % 2), HALO * (r % 2) + HALO)
        one, other = by_even[f, r // 2, spot, :], by_odd[f, r // 2, spot, :]
        return jnp.where(even_lat, one, other), jnp.where(even_lat, other, one)

    def ghosts(f, r):
        high, low = received(f, r)
        return jnp.concatenate(
            [jnp.where(has_high, high, 0.0), jnp.where(has_low, low, 0.0)], axis=0
        )

    for r in range(CR):
        for k in range(3):
            u[k, r, 0:CL, :] = cur[k, r]
            u[k, r, CL:ROWS, :] = ghosts(k, r)
            v[k, r, 0:CL, :] = prv[k, r]
            v[k, r, CL:ROWS, :] = ghosts(3 + k, r)
        for j in range(4):
            m[j, r, 0:CL, :] = mod[j, r]
            m[j, r, CL:ROWS, :] = ghosts(6 + j, r)
        c[r, 0:CL, :] = STEP_SQUARE / den[r]
        outer = STEP_SQUARE / jnp.concatenate(received(10, r), axis=0)
        present = jnp.where(iota((8, 128), 0) < HALO, has_high.astype(I32), has_low.astype(I32))
        c[r, CL:ROWS, :] = jnp.where(present > 0, outer, 0.0)
    put_layers(u, range(3), even, odd)
    put_layers(m, (0, 2), even, odd, 3)
    left[...] = jnp.zeros_like(left)
    right[...] = jnp.zeros_like(right)
    put_columns(tiles_of(u, 3), left, right, 0)
    put_columns(tiles_of(m, 3, 1), left, right, 3)


def force(k, r, u, low, high, at_left, at_right, ar, al, au, ad):
    jr, jl, je = TABLE[k]
    here = u[k, r]
    below = u[k, r - 1] if r > 0 else low[k]
    above = u[k, r + 1] if r < CR - 1 else high[k]
    total = ar[jr // 2, r + 1] * (above - here) - ar[jr // 2, r] * (here - below)
    flux = al[jl - 1, r] * (pltpu.roll(here, ROWS - 1, 0) - here)
    total = total + (flux - pltpu.roll(flux, 1, 0))
    lane = iota((ROWS, CE), 1)
    after = jnp.where(lane == CE - 1, column(at_right, 0, k, r), pltpu.roll(here, CE - 1, 1))
    before = jnp.where(lane == 0, column(at_left, 0, k, r), pltpu.roll(here, 1, 1))
    return total + (au[je - 1, r] * (after - here) + ad[je - 1, r] * (before - here))


def radial_ends(even, odd, count):
    rad, even_rad = lax.axis_index("rad"), is_even("rad")
    lows, highs = [], []
    for k in range(count):
        low = jnp.where(even_rad, odd[k], even[k])
        high = jnp.where(even_rad, even[k], odd[k])
        lows.append(jnp.where(rad > 0, low, 0.0))
        highs.append(jnp.where(rad < lax.axis_size("rad") - 1, high, 0.0))
    return lows, highs


def prepare_kernel(u, v, m, c, even, odd, at_left, at_right, ar, al, au, ad, following):
    lows, highs = radial_ends(even, odd, 5)
    lane = iota((ROWS, CE), 1)
    for i, j in enumerate((0, 2)):
        layers = [lows[3 + i]] + [m[j, r] for r in range(CR)] + [highs[3 + i]]
        for face in range(CR + 1):
            ar[i, face] = 0.5 * (layers[face] + layers[face + 1])
    for j in (1, 2, 3):
        for r in range(CR):
            here = m[j, r]
            al[j - 1, r] = 0.5 * (here + pltpu.roll(here, ROWS - 1, 0))
            after = jnp.where(
                lane == CE - 1, column(at_right, 3, j - 1, r), pltpu.roll(here, CE - 1, 1)
            )
            before = jnp.where(lane == 0, column(at_left, 3, j - 1, r), pltpu.roll(here, 1, 1))
            au[j - 1, r] = 0.5 * (here + after)
            ad[j - 1, r] = 0.5 * (here + before)
    for k in range(3):
        for r in range(CR):
            total = force(k, r, u, lows, highs, at_left, at_right, ar, al, au, ad)
            following[k, r] = 2.0 * u[k, r] - v[k, r] + c[r] * total


def thirds(x):
    high = x.astype(jnp.bfloat16).astype(F32)
    rest = x - high
    middle = rest.astype(jnp.bfloat16).astype(F32)
    return high, middle, rest - middle


def gather_sources(steps, got, weights, picks):
    turned = jnp.transpose(jnp.concatenate([got[:, 0, :128], got[:, 0, 128:]], axis=0))
    parts = thirds(turned)
    cell_rows, cell_lanes = iota((CR * ROWS, 128), 0), iota((CE, 128), 0)
    for j in range(SLOTS):
        place = turned[96 + j : 97 + j].astype(I32)
        around = turned[104 + j : 105 + j].astype(I32)
        pick = jnp.where(cell_lanes == around, 1.0, 0.0)
        here = cell_rows == place
        for p in range(3):
            span = slice((p * SLOTS + j) * 128, (p * SLOTS + j + 1) * 128)
            picks[:, span] = pick
            for i, t in enumerate(steps):
                for k in range(3):
                    line = (k * STEPS + t) * 8 + j
                    at = (i * 3 + k) * CR * ROWS
                    weights[at : at + CR * ROWS, span] = jnp.where(
                        here, parts[p][line : line + 1], 0.0
                    )
    return lax.dot_general(
        weights[...], picks[...], (((1,), (1,)), ((), ())), preferred_element_type=F32
    )


def first_kernel(got, free, c, first, even, odd, left, right, weights, picks):
    summed = gather_sources((0,), got, weights, picks)
    for k in range(3):
        for r in range(CR):
            at = (k * CR + r) * ROWS
            first[k, r] = free[k, r] + summed[at : at + ROWS] * c[r]
    put_faces(first, even, odd, left, right)


def sources_kernel(got, c, sources, weights, picks):
    summed = gather_sources(range(1, STEPS), got, weights, picks)
    for t in range(STEPS - 1):
        for k in range(3):
            for r in range(CR):
                at = ((t * 3 + k) * CR + r) * ROWS
                sources[t, k, r] = summed[at : at + ROWS] * c[r]


def step_kernel(
    t, u, v, c, sources, even, odd, at_left, at_right, ar, al, au, ad, following, *faces
):
    lows, highs = radial_ends(even, odd, 3)
    for k in range(3):
        for r in range(CR):
            total = force(k, r, u, lows, highs, at_left, at_right, ar, al, au, ad)
            following[k, r] = 2.0 * u[k, r] - v[k, r] + c[r] * total + sources[t - 1, k, r]
    put_faces(following, *faces)


def last_kernel(
    u, v, c, sources, even, odd, at_left, at_right, ar, al, au, ad, final, before_final,
    made, sems,
):
    copies = [pltpu.make_async_copy(u.at[:, :, pl.ds(0, CL), :], before_final, sems.at[3])]
    copies[0].start()
    lows, highs = radial_ends(even, odd, 3)
    rest = jnp.zeros((ROWS - CL, CE), F32)
    lows = [jnp.concatenate([x, rest], axis=0) for x in lows]
    highs = [jnp.concatenate([x, rest], axis=0) for x in highs]
    for k in range(3):
        for r in range(CR):
            total = force(k, r, u, lows, highs, at_left, at_right, ar, al, au, ad)
            value = 2.0 * u[k, r] - v[k, r] + c[r] * total + sources[STEPS - 2, k, r]
            made[k, r] = value[:CL]
        copies.append(pltpu.make_async_copy(made.at[k], final.at[k], sems.at[k]))
        copies[-1].start()
    for copy in copies:
        copy.wait()


def call(kernel, outs, args, scratch=(), hbm=0, us=1.0, out_space=pltpu.VMEM):
    vmem = pl.BlockSpec(memory_space=pltpu.VMEM)
    specs = [pl.BlockSpec(memory_space=pltpu.HBM)] * hbm + [vmem] * (len(args) - hbm)
    return pl.pallas_call(
        kernel,
        out_shape=[jax.ShapeDtypeStruct(shape, F32) for shape in outs],
        in_specs=specs,
        out_specs=[pl.BlockSpec(memory_space=out_space)] * len(outs),
        scratch_shapes=[pltpu.VMEM(s, F32) if isinstance(s, tuple) else s for s in scratch],
        cost_estimate=pl.CostEstimate(
            flops=0, bytes_accessed=int(us * 3_000_000), transcendentals=0
        ),
        compiler_params=pltpu.CompilerParams(vmem_limit_bytes=(60 if hbm else 32) * 1024 * 1024),
    )(*args)


def shifted(block, axis, by):
    count = lax.axis_size(axis)
    return lax.ppermute(block, axis, [(i, (i + by) % count) for i in range(count)])


def swapped(block, axis, odd):
    count = lax.axis_size(axis)
    pairs = [(i, (i + (1 if (i + odd) % 2 == 0 else -1)) % count) for i in range(count)]
    return lax.ppermute(block, axis, pairs)


def swap_faces(even, odd, left, right):
    odd, even = swapped(odd, "rad", 1), swapped(even, "rad", 0)
    at_left = shifted(right, "span", 1)
    at_right = shifted(left, "span", -1)
    return even, odd, at_left, at_right


def on_device(current, previous, moduli, density, traces, receivers, owners, offsets):
    wide = (3, CR, ROWS, CE)
    edge = (11, 2, 8, CE)
    faces = [(3, ROWS, CE), (3, ROWS, CE), (8, CE), (8, CE)]

    fields = (current, previous, moduli, density.reshape((1,) + density.shape))
    rooms = [(11, CR, 8, CE), pltpu.SemaphoreType.DMA((4,))]
    (even_rows,) = call(even_edge_kernel, [edge], fields, scratch=rooms, hbm=4)
    by_even = swapped(even_rows, "lat", 0)
    packed, odd_rows = call(
        pack_kernel,
        [(64, 1, 256), edge],
        (
            offsets.reshape(1, 128),
            receivers.reshape(1, 128),
            owners.reshape(1, 128),
            traces.transpose(1, 0, 2),
        )
        + fields,
        scratch=rooms
        + [
            (3, STATIONS, 512),
            pltpu.VMEM((8, 128), I32),
            pltpu.SemaphoreType.DMA(()),
            pltpu.SemaphoreType.DMA((3,)),
        ],
        hbm=8,
        us=2.0,
    )
    by_odd = swapped(odd_rows, "lat", 1)
    got = lax.all_to_all(packed, ("lat", "rad"), 0, 0, tiled=True)

    u, v, m, c, *ends = call(
        widen_kernel,
        [wide, wide, (4, CR, ROWS, CE), (CR, ROWS, CE)]
        + [(5, ROWS, CE), (5, ROWS, CE), (8, CE), (8, CE)],
        (current, previous, moduli, density, by_even, by_odd),
    )
    *coefficients, free = call(
        prepare_kernel,
        [(2, CR + 1, ROWS, CE), wide, wide, wide, wide],
        (u, v, m, c, *swap_faces(*ends)),
    )
    cells, lanes = CR * ROWS, 3 * SLOTS * 128
    first, *ends = call(
        first_kernel,
        [wide] + faces,
        (got, free, c),
        scratch=[(3 * cells, lanes), (CE, lanes)],
    )
    (sources,) = call(
        sources_kernel,
        [(STEPS - 1,) + wide],
        (got, c),
        scratch=[(3 * (STEPS - 1) * cells, lanes), (CE, lanes)],
        us=3.0,
    )
    v, u = u, first
    for t in range(1, STEPS - 1):

        def kernel(*refs, t=t):
            step_kernel(t, *refs)

        if t == STEPS - 2:
            faces = [(3, CL, CE)] * 2 + faces[2:]
        following, *next_ends = call(
            kernel, [wide] + faces, (u, v, c, sources, *swap_faces(*ends), *coefficients)
        )
        v, u, ends = u, following, next_ends
    return tuple(
        call(
            last_kernel,
            [(3, CR, CL, CE)] * 2,
            (u, v, c, sources, *swap_faces(*ends), *coefficients),
            scratch=[(3, CR, CL, CE), pltpu.SemaphoreType.DMA((4,))],
            out_space=pltpu.HBM,
        )
    )


def solution(mesh):
    in_specs = (
        P(None, "rad", "lat", "span"),
        P(None, "rad", "lat", "span"),
        P(None, "rad", "lat", "span"),
        P("rad", "lat", "span"),
        P(("span", "lat", "rad"), None, None),
        P(("span", "lat", "rad")),
        P(("span", "lat", "rad"), None),
        P(("span", "lat", "rad")),
    )
    out_specs = (P(None, "rad", "lat", "span"), P(None, "rad", "lat", "span"))
    return jax.shard_map(
        on_device, mesh=mesh, in_specs=in_specs, out_specs=out_specs, check_vma=False
    )
```

```python
import jax
import jax.numpy as jnp
from jax import lax
from jax.experimental import pallas as pl
from jax.experimental.pallas import tpu as pltpu
from jax.sharding import PartitionSpec as P

STEPS = 4
STEP_SQUARE = 0.16
TABLE = ((0, 2, 2), (2, 1, 3), (2, 3, 1))
CR, CL, CE = 4, 16, 128
HALO = 4
ROWS = CL + 2 * HALO
CAP = 4
SLOTS = 6
STATIONS = 128
F32 = jnp.float32
I32 = jnp.int32


def iota(shape, dim):
    return lax.broadcasted_iota(I32, shape, dim)


def fold(tiles, at):
    lane, sub = iota((8, 128), 1), iota((8, 128), 0)
    rows = []
    for start in range(0, len(tiles), 16):
        gathered = jnp.zeros((8, 128), F32)
        for i, tile in enumerate(tiles[start : start + 16]):
            column = jnp.broadcast_to(tile[:, at : at + 1], (8, 128))
            gathered = jnp.where(lane == i * 8 + sub, column, gathered)
        rows.append(jnp.sum(gathered, axis=0, keepdims=True))
    return rows


def unfold(ref, first_row, tile):
    row = first_row + tile // 16
    spread = jnp.broadcast_to(ref[pl.ds(row, 1), :], (8, 128))
    return jnp.take_along_axis(spread, (tile % 16) * 8 + iota((8, 128), 0), axis=1)


def column(ref, first_row, k, r):
    first = (k * CR + r) * (ROWS // 8)
    return jnp.concatenate([unfold(ref, first_row, first + i) for i in range(ROWS // 8)], axis=0)


def tiles_of(ref, count, first=0):
    return [
        ref[first + k, r, 8 * i : 8 * i + 8, :]
        for k in range(count)
        for r in range(CR)
        for i in range(ROWS // 8)
    ]


def put_columns(tiles, left_ref, right_ref, first_row):
    for ref, at in ((left_ref, 0), (right_ref, CE - 1)):
        for i, row in enumerate(fold(tiles, at)):
            ref[first_row + i : first_row + i + 1, :] = row


def rad_is_even():
    return lax.axis_index("rad") % 2 == 0


def end_layers():
    top = jnp.where(rad_is_even(), CR - 1, 0)
    return top, CR - 1 - top


def put_rest(u_ref, odd_ref, left_ref, right_ref):
    _, bottom = end_layers()
    rows = odd_ref.shape[1]
    for k in range(3):
        odd_ref[k] = u_ref[k, bottom, :rows, :]
    left_ref[...] = jnp.zeros_like(left_ref)
    right_ref[...] = jnp.zeros_like(right_ref)
    put_columns(tiles_of(u_ref, 3), left_ref, right_ref, 0)


def edge_rows(start, fields, out, room, sems):
    first, copies = 0, []
    for i, ref in enumerate(fields):
        count = ref.shape[0]
        copies.append(
            pltpu.make_async_copy(
                ref.at[:, :, pl.ds(start, 8), :], room.at[pl.ds(first, count)], sems.at[i]
            )
        )
        first += count
    for copy in copies:
        copy.start()

    def finish():
        for copy in copies:
            copy.wait()
        inner = slice(0, HALO) if start == 0 else slice(8 - HALO, 8)
        for f in range(first):
            for r in range(CR):
                spot = slice(HALO * (r % 2), HALO * (r % 2) + HALO)
                out[f, r // 2, spot, :] = room[f, r, inner, :]

    return finish


def high_kernel(cur, prv, mod, den, high, room, sems):
    edge_rows(CL - 8, (cur, prv, mod, den), high, room, sems)()


def pack_kernel(
    offsets_in, receivers_in, owners_in, traces_in, cur, prv, mod, den, out, low,
    room, sems, traces, words_in, trace_sem, word_sems,
):
    copy = pltpu.make_async_copy(traces_in, traces, trace_sem)
    copy.start()
    small = [
        pltpu.make_async_copy(ref, words_in.at[pl.ds(i, 1)], word_sems.at[i])
        for i, ref in enumerate((offsets_in, receivers_in, owners_in))
    ]
    for one in small:
        one.start()
    finish_low = edge_rows(0, (cur, prv, mod, den), low, room, sems)
    for one in small:
        one.wait()
    offset_row, q, owner_row = words_in[0:1], words_in[1:2], words_in[2:3]
    r, l, e = q // 2048, (q // 128) % CL, q % 128
    wide_sub, wide_lane = iota((128, 128), 0), iota((128, 128), 1)
    sheet = jnp.transpose(
        jnp.concatenate(
            [owner_row.astype(F32), offset_row.astype(F32), jnp.zeros((6, 128), F32)], axis=0
        )
    )
    owner_cols = jnp.broadcast_to(sheet[:, 0:1], (128, 128)).astype(I32)
    offsets = jnp.broadcast_to(sheet[:, 1:2], (128, 128)).astype(I32)
    same = (owner_cols == owner_row) & (wide_sub < wide_lane)
    rank = jnp.sum(jnp.where(same, 1.0, 0.0), axis=0, keepdims=True).astype(I32)

    lefts, lines = [], [e.astype(F32)]
    for shift in (-1, 0, 1):
        slot = (shift + 1) * CAP + rank
        half, j = slot // SLOTS, slot % SLOTS
        if shift == 0:
            row, near = l, l >= 0
        elif shift == -1:
            row, near = CL + l, l <= HALO - 2
        else:
            row, near = l + HALO + HALO, l >= CL - HALO + 1
        target = owner_row + 8 * shift
        ok = near & (target >= 0) & (target < 64)
        place = jnp.where(ok, half * 64 + target, -1)
        lefts.append(jnp.where(wide_sub == place, 1.0, 0.0))
        lines += [j.astype(F32), (r * ROWS + row).astype(F32)]
    sheet = jnp.transpose(jnp.concatenate(lines + [jnp.zeros((1, 128), F32)], axis=0))
    finish_low()

    inside = offsets % 128
    tile = offsets // 128 + jnp.where(wide_lane < inside, 1, 0)
    index = (inside + (wide_lane // 8) % STEPS) % 128
    copy.wait()
    window = jnp.broadcast_to(sheet[:, 0:1], (128, 128))
    for k in range(3):
        parts = [traces[k, :, 128 * i : 128 * i + 128] for i in range(4)]
        merged = jnp.where(
            tile == 0,
            parts[0],
            jnp.where(tile == 1, parts[1], jnp.where(tile == 2, parts[2], parts[3])),
        )
        picked = jnp.take_along_axis(merged, index, axis=1)
        window = jnp.where(wide_lane // 32 == k, picked, window)
    rights = []
    for i in range(3):
        slots = jnp.broadcast_to(sheet[:, 2 * i + 1 : 2 * i + 2], (128, 128)).astype(I32)
        cells = jnp.broadcast_to(sheet[:, 2 * i + 2 : 2 * i + 3], (128, 128))
        words = jnp.where((wide_lane >= 96) & (wide_lane < 104), cells, window)
        rights.append(jnp.where((wide_lane % 8 == slots) & (wide_lane < 112), words, 0.0))
    packed = lax.dot_general(
        jnp.concatenate(lefts, axis=1),
        jnp.concatenate(rights, axis=0),
        (((1,), (0,)), ((), ())),
        precision=lax.Precision.HIGHEST,
        preferred_element_type=F32,
    )
    out[:, 0, :128] = packed[:64]
    out[:, 0, 128:] = packed[64:]


def widen_kernel(
    cur, prv, mod, den, from_low, from_high, u, v, m, c, even, odd, left, right
):
    lat = lax.axis_index("lat")
    has_low, has_high = lat > 0, lat < lax.axis_size("lat") - 1

    def ghosts(f, r):
        spot = slice(HALO * (r % 2), HALO * (r % 2) + HALO)
        return jnp.concatenate(
            [
                jnp.where(has_high, from_high[f, r // 2, spot, :], 0.0),
                jnp.where(has_low, from_low[f, r // 2, spot, :], 0.0),
            ],
            axis=0,
        )

    for r in range(CR):
        for k in range(3):
            u[k, r, 0:CL, :] = cur[k, r]
            u[k, r, CL:ROWS, :] = ghosts(k, r)
            v[k, r, 0:CL, :] = prv[k, r]
            v[k, r, CL:ROWS, :] = ghosts(3 + k, r)
        for j in range(4):
            m[j, r, 0:CL, :] = mod[j, r]
            m[j, r, CL:ROWS, :] = ghosts(6 + j, r)
        c[r, 0:CL, :] = STEP_SQUARE / den[r]
        spot = slice(HALO * (r % 2), HALO * (r % 2) + HALO)
        outer = STEP_SQUARE / jnp.concatenate(
            [from_high[10, r // 2, spot, :], from_low[10, r // 2, spot, :]], axis=0
        )
        present = jnp.where(iota((8, 128), 0) < HALO, has_high.astype(I32), has_low.astype(I32))
        c[r, CL:ROWS, :] = jnp.where(present > 0, outer, 0.0)
    top, bottom = end_layers()
    for i, (field, k) in enumerate(((u, 0), (u, 1), (u, 2), (m, 0), (m, 2))):
        even[i] = field[k, top]
        odd[i] = field[k, bottom]
    left[...] = jnp.zeros_like(left)
    right[...] = jnp.zeros_like(right)
    put_columns(tiles_of(u, 3), left, right, 0)
    put_columns(tiles_of(m, 3, 1), left, right, 3)


def level(k, r, here, at_left, at_right, al, au, ad):
    _, jl, je = TABLE[k]
    flux = al[jl - 1, r] * (pltpu.roll(here, ROWS - 1, 0) - here)
    total = flux - pltpu.roll(flux, 1, 0)
    lane = iota((ROWS, CE), 1)
    after = jnp.where(lane == CE - 1, column(at_right, 0, k, r), pltpu.roll(here, CE - 1, 1))
    before = jnp.where(lane == 0, column(at_left, 0, k, r), pltpu.roll(here, 1, 1))
    return total + (au[je - 1, r] * (after - here) + ad[je - 1, r] * (before - here))


def force(k, r, u, low, high, at_left, at_right, ar, al, au, ad):
    i, here = TABLE[k][0] // 2, u[k, r]
    below = u[k, r - 1] if r > 0 else low[k]
    above = u[k, r + 1] if r < CR - 1 else high[k]
    total = ar[i, r + 1] * (above - here) - ar[i, r] * (here - below)
    return total + level(k, r, here, at_left, at_right, al, au, ad)


def radial_ends(even, odd, count):
    rad, is_even = lax.axis_index("rad"), rad_is_even()
    lows, highs = [], []
    for k in range(count):
        low = jnp.where(is_even, odd[k], even[k])
        high = jnp.where(is_even, even[k], odd[k])
        lows.append(jnp.where(rad > 0, low, 0.0))
        highs.append(jnp.where(rad < lax.axis_size("rad") - 1, high, 0.0))
    return lows, highs


def prepare_kernel(u, v, m, c, even, odd, at_left, at_right, ar, al, au, ad, following):
    lows, highs = radial_ends(even, odd, 5)
    lane = iota((ROWS, CE), 1)
    for i, j in enumerate((0, 2)):
        layers = [lows[3 + i]] + [m[j, r] for r in range(CR)] + [highs[3 + i]]
        for face in range(CR + 1):
            ar[i, face] = 0.5 * (layers[face] + layers[face + 1])
    for j in (1, 2, 3):
        for r in range(CR):
            here = m[j, r]
            al[j - 1, r] = 0.5 * (here + pltpu.roll(here, ROWS - 1, 0))
            after = jnp.where(
                lane == CE - 1, column(at_right, 3, j - 1, r), pltpu.roll(here, CE - 1, 1)
            )
            before = jnp.where(lane == 0, column(at_left, 3, j - 1, r), pltpu.roll(here, 1, 1))
            au[j - 1, r] = 0.5 * (here + after)
            ad[j - 1, r] = 0.5 * (here + before)
    for k in range(3):
        for r in range(CR):
            total = force(k, r, u, lows, highs, at_left, at_right, ar, al, au, ad)
            following[k, r] = 2.0 * u[k, r] - v[k, r] + c[r] * total


def thirds(x):
    high = x.astype(jnp.bfloat16).astype(F32)
    rest = x - high
    middle = rest.astype(jnp.bfloat16).astype(F32)
    return high, middle, rest - middle


def gather_sources(steps, got, weights, picks, layer=0, layers=CR):
    turned = jnp.transpose(jnp.concatenate([got[:, 0, :128], got[:, 0, 128:]], axis=0))
    parts = thirds(turned)
    cells = layers * ROWS
    cell_rows, cell_lanes = iota((cells, 128), 0) + layer * ROWS, iota((CE, 128), 0)
    for j in range(SLOTS):
        place = turned[96 + j : 97 + j].astype(I32)
        around = turned[104 + j : 105 + j].astype(I32)
        pick = jnp.where(cell_lanes == around, 1.0, 0.0)
        here = cell_rows == place
        for p in range(3):
            span = slice((p * SLOTS + j) * 128, (p * SLOTS + j + 1) * 128)
            picks[:, span] = pick
            for i, t in enumerate(steps):
                for k in range(3):
                    line = (k * STEPS + t) * 8 + j
                    at = (i * 3 + k) * cells
                    weights[at : at + cells, span] = jnp.where(
                        here, parts[p][line : line + 1], 0.0
                    )
    return lax.dot_general(
        weights[...], picks[...], (((1,), (1,)), ((), ())), preferred_element_type=F32
    )


def first_lead_kernel(got, free, c, even, weights, picks):
    top, _ = end_layers()
    summed = gather_sources((0,), got, weights, picks, top, 1)
    for k in range(3):
        even[k] = free[k, top] + summed[k * ROWS : (k + 1) * ROWS] * c[top]


def first_kernel(got, free, c, first, odd, left, right, weights, picks):
    summed = gather_sources((0,), got, weights, picks)
    for k in range(3):
        for r in range(CR):
            at = (k * CR + r) * ROWS
            first[k, r] = free[k, r] + summed[at : at + ROWS] * c[r]
    put_rest(first, odd, left, right)


def sources_kernel(got, c, sources, weights, picks):
    summed = gather_sources(range(1, STEPS), got, weights, picks)
    for t in range(STEPS - 1):
        for k in range(3):
            for r in range(CR):
                at = ((t * 3 + k) * CR + r) * ROWS
                sources[t, k, r] = summed[at : at + ROWS] * c[r]


def lead_kernel(t, u, v, c, sources, even, at_left, at_right, ar, al, au, ad, out):
    top, _ = end_layers()
    upwards = rad_is_even()
    inner = jnp.where(upwards, CR - 2, 1)
    outer_face, inner_face = jnp.where(upwards, CR, 0), jnp.where(upwards, CR - 1, 1)
    for k in range(3):
        i, here = TABLE[k][0] // 2, u[k, top]
        total = ar[i, outer_face] * (even[k] - here) + ar[i, inner_face] * (u[k, inner] - here)
        total = total + level(k, top, here, at_left, at_right, al, au, ad)
        value = 2.0 * here - v[k, top] + c[top] * total + sources[t - 1, k, top]
        out[k] = value[: out.shape[1]]


def step_kernel(
    t, u, v, c, sources, even, odd, at_left, at_right, ar, al, au, ad, following, *rest
):
    lows, highs = radial_ends(even, odd, 3)
    for k in range(3):
        for r in range(CR):
            total = force(k, r, u, lows, highs, at_left, at_right, ar, al, au, ad)
            following[k, r] = 2.0 * u[k, r] - v[k, r] + c[r] * total + sources[t - 1, k, r]
    put_rest(following, *rest)


def last_kernel(
    u, v, c, sources, even, odd, at_left, at_right, ar, al, au, ad, final, before_final
):
    lows, highs = radial_ends(even, odd, 3)
    beside = jnp.zeros((ROWS - CL, CE), F32)
    lows = [jnp.concatenate([x, beside], axis=0) for x in lows]
    highs = [jnp.concatenate([x, beside], axis=0) for x in highs]
    for k in range(3):
        for r in range(CR):
            total = force(k, r, u, lows, highs, at_left, at_right, ar, al, au, ad)
            value = 2.0 * u[k, r] - v[k, r] + c[r] * total + sources[STEPS - 2, k, r]
            final[k, r] = value[:CL]
            before_final[k, r] = u[k, r, 0:CL, :]


def call(kernel, outs, args, scratch=(), hbm=0, us=1.0):
    vmem = pl.BlockSpec(memory_space=pltpu.VMEM)
    specs = [pl.BlockSpec(memory_space=pltpu.HBM)] * hbm + [vmem] * (len(args) - hbm)
    return pl.pallas_call(
        kernel,
        out_shape=[jax.ShapeDtypeStruct(shape, F32) for shape in outs],
        in_specs=specs,
        out_specs=[vmem] * len(outs),
        scratch_shapes=[pltpu.VMEM(s, F32) if isinstance(s, tuple) else s for s in scratch],
        cost_estimate=pl.CostEstimate(
            flops=0, bytes_accessed=int(us * 3_000_000), transcendentals=0
        ),
        compiler_params=pltpu.CompilerParams(vmem_limit_bytes=(60 if hbm else 32) * 1024 * 1024),
    )(*args)


def shifted(block, axis, by):
    count = lax.axis_size(axis)
    return lax.ppermute(block, axis, [(i, (i + by) % count) for i in range(count)])


def swapped(block, axis, odd):
    count = lax.axis_size(axis)
    pairs = [(i, (i + (1 if (i + odd) % 2 == 0 else -1)) % count) for i in range(count)]
    return lax.ppermute(block, axis, pairs)


def swap_columns(left, right):
    return shifted(right, "span", 1), shifted(left, "span", -1)


def on_device(current, previous, moduli, density, traces, receivers, owners, offsets):
    wide = (3, CR, ROWS, CE)
    edge = (11, 2, 8, CE)
    layer, columns = (3, ROWS, CE), [(8, CE), (8, CE)]

    fields = (current, previous, moduli, density.reshape((1,) + density.shape))
    rooms = [(11, CR, 8, CE), pltpu.SemaphoreType.DMA((4,))]
    (high_rows,) = call(high_kernel, [edge], fields, scratch=rooms, hbm=4)
    from_low = shifted(high_rows, "lat", 1)
    packed, low_rows = call(
        pack_kernel,
        [(64, 1, 256), edge],
        (
            offsets.reshape(1, 128),
            receivers.reshape(1, 128),
            owners.reshape(1, 128),
            traces.transpose(1, 0, 2),
        )
        + fields,
        scratch=rooms
        + [
            (3, STATIONS, 512),
            pltpu.VMEM((8, 128), I32),
            pltpu.SemaphoreType.DMA(()),
            pltpu.SemaphoreType.DMA((3,)),
        ],
        hbm=8,
        us=2.0,
    )
    from_high = shifted(low_rows, "lat", -1)
    got = lax.all_to_all(packed, ("lat", "rad"), 0, 0, tiled=True)

    u, v, m, c, even, odd, *ends = call(
        widen_kernel,
        [wide, wide, (4, CR, ROWS, CE), (CR, ROWS, CE)]
        + [(5, ROWS, CE), (5, ROWS, CE), (8, CE), (8, CE)],
        (current, previous, moduli, density, from_low, from_high),
    )
    *coefficients, free = call(
        prepare_kernel,
        [(2, CR + 1, ROWS, CE), wide, wide, wide, wide],
        (u, v, m, c, swapped(even, "rad", 0), swapped(odd, "rad", 1), *swap_columns(*ends)),
    )
    cells, lanes = CR * ROWS, 3 * SLOTS * 128
    (even,) = call(
        first_lead_kernel,
        [layer],
        (got, free, c),
        scratch=[(3 * ROWS, lanes), (CE, lanes)],
    )
    even = swapped(even, "rad", 0)
    first, odd, *ends = call(
        first_kernel,
        [wide, layer] + columns,
        (got, free, c),
        scratch=[(3 * cells, lanes), (CE, lanes)],
    )
    (sources,) = call(
        sources_kernel,
        [(STEPS - 1,) + wide],
        (got, c),
        scratch=[(3 * (STEPS - 1) * cells, lanes), (CE, lanes)],
        us=3.0,
    )
    v, u = u, first
    for t in range(1, STEPS):
        odd = swapped(odd, "rad", 1)
        at_left, at_right = swap_columns(*ends)
        before = (u, v, c, sources, even)
        after = (at_left, at_right, *coefficients)
        if t == STEPS - 1:
            return tuple(call(last_kernel, [(3, CR, CL, CE)] * 2, before + (odd,) + after))
        if t == STEPS - 2:
            layer = (3, CL, CE)

        def lead(*refs, t=t):
            lead_kernel(t, *refs)

        def step(*refs, t=t):
            step_kernel(t, *refs)

        (next_even,) = call(lead, [layer], before + after)
        next_even = swapped(next_even, "rad", 0)
        following, odd, *ends = call(step, [wide, layer] + columns, before + (odd,) + after)
        v, u, even = u, following, next_even


def solution(mesh):
    in_specs = (
        P(None, "rad", "lat", "span"),
        P(None, "rad", "lat", "span"),
        P(None, "rad", "lat", "span"),
        P("rad", "lat", "span"),
        P(("span", "lat", "rad"), None, None),
        P(("span", "lat", "rad")),
        P(("span", "lat", "rad"), None),
        P(("span", "lat", "rad")),
    )
    out_specs = (P(None, "rad", "lat", "span"), P(None, "rad", "lat", "span"))
    return jax.shard_map(
        on_device, mesh=mesh, in_specs=in_specs, out_specs=out_specs, check_vma=False
    )
```

```python
import jax
import jax.numpy as jnp
from jax import lax
from jax.experimental import pallas as pl
from jax.experimental.pallas import tpu as pltpu
from jax.sharding import PartitionSpec as P

STEPS = 4
STEP_SQUARE = 0.16
TABLE = ((0, 2, 2), (2, 1, 3), (2, 3, 1))
CR, CL, CE = 4, 16, 128
HALO = 4
ROWS = CL + 2 * HALO
CAP = 4
SLOTS = 6
STATIONS = 128
F32 = jnp.float32
I32 = jnp.int32


def iota(shape, dim):
    return lax.broadcasted_iota(I32, shape, dim)


def fold(tiles, at):
    lane, sub = iota((8, 128), 1), iota((8, 128), 0)
    rows = []
    for start in range(0, len(tiles), 16):
        gathered = jnp.zeros((8, 128), F32)
        for i, tile in enumerate(tiles[start : start + 16]):
            column = jnp.broadcast_to(tile[:, at : at + 1], (8, 128))
            gathered = jnp.where(lane == i * 8 + sub, column, gathered)
        rows.append(jnp.sum(gathered, axis=0, keepdims=True))
    return rows


def unfold(ref, first_row, tile):
    row = first_row + tile // 16
    spread = jnp.broadcast_to(ref[pl.ds(row, 1), :], (8, 128))
    return jnp.take_along_axis(spread, (tile % 16) * 8 + iota((8, 128), 0), axis=1)


def column(ref, first_row, k, r):
    first = (k * CR + r) * (ROWS // 8)
    return jnp.concatenate([unfold(ref, first_row, first + i) for i in range(ROWS // 8)], axis=0)


def tiles_of(ref, count, first=0):
    return [
        ref[first + k, r, 8 * i : 8 * i + 8, :]
        for k in range(count)
        for r in range(CR)
        for i in range(ROWS // 8)
    ]


def put_columns(tiles, left_ref, right_ref, first_row):
    for ref, at in ((left_ref, 0), (right_ref, CE - 1)):
        for i, row in enumerate(fold(tiles, at)):
            ref[first_row + i : first_row + i + 1, :] = row


def rad_is_even():
    return lax.axis_index("rad") % 2 == 0


def end_layers():
    lead = jnp.where(rad_is_even(), 0, CR - 1)
    return lead, CR - 1 - lead


def keep_lead(u_ref, made):
    lead, _ = end_layers()
    rows = made.shape[1]
    for k in range(3):
        u_ref[k, lead, :rows, :] = made[k]


def put_rest(u_ref, even_ref, left_ref, right_ref):
    _, rest = end_layers()
    rows = even_ref.shape[1]
    for k in range(3):
        even_ref[k] = u_ref[k, rest, :rows, :]
    left_ref[...] = jnp.zeros_like(left_ref)
    right_ref[...] = jnp.zeros_like(right_ref)
    put_columns(tiles_of(u_ref, 3), left_ref, right_ref, 0)


def edge_rows(start, fields, out, room, sems):
    first, copies = 0, []
    for i, ref in enumerate(fields):
        count = ref.shape[0]
        copies.append(
            pltpu.make_async_copy(
                ref.at[:, :, pl.ds(start, 8), :], room.at[pl.ds(first, count)], sems.at[i]
            )
        )
        first += count
    for copy in copies:
        copy.start()

    def finish():
        for copy in copies:
            copy.wait()
        inner = slice(0, HALO) if start == 0 else slice(8 - HALO, 8)
        for f in range(first):
            for r in range(CR):
                spot = slice(HALO * (r % 2), HALO * (r % 2) + HALO)
                out[f, r // 2, spot, :] = room[f, r, inner, :]

    return finish


def high_kernel(cur, prv, mod, den, high, room, sems):
    edge_rows(CL - 8, (cur, prv, mod, den), high, room, sems)()


def pack_kernel(
    offsets_in, receivers_in, owners_in, traces_in, cur, prv, mod, den, out, low,
    room, sems, traces, words_in, trace_sem, word_sems,
):
    copy = pltpu.make_async_copy(traces_in, traces, trace_sem)
    copy.start()
    small = [
        pltpu.make_async_copy(ref, words_in.at[pl.ds(i, 1)], word_sems.at[i])
        for i, ref in enumerate((offsets_in, receivers_in, owners_in))
    ]
    for one in small:
        one.start()
    finish_low = edge_rows(0, (cur, prv, mod, den), low, room, sems)
    for one in small:
        one.wait()
    offset_row, q, owner_row = words_in[0:1], words_in[1:2], words_in[2:3]
    r, l, e = q // 2048, (q // 128) % CL, q % 128
    wide_sub, wide_lane = iota((128, 128), 0), iota((128, 128), 1)
    sheet = jnp.transpose(
        jnp.concatenate(
            [owner_row.astype(F32), offset_row.astype(F32), jnp.zeros((6, 128), F32)], axis=0
        )
    )
    owner_cols = jnp.broadcast_to(sheet[:, 0:1], (128, 128)).astype(I32)
    offsets = jnp.broadcast_to(sheet[:, 1:2], (128, 128)).astype(I32)
    same = (owner_cols == owner_row) & (wide_sub < wide_lane)
    rank = jnp.sum(jnp.where(same, 1.0, 0.0), axis=0, keepdims=True).astype(I32)

    lefts, lines = [], [e.astype(F32)]
    for shift in (-1, 0, 1):
        slot = (shift + 1) * CAP + rank
        half, j = slot // SLOTS, slot % SLOTS
        if shift == 0:
            row, near = l, l >= 0
        elif shift == -1:
            row, near = CL + l, l <= HALO - 2
        else:
            row, near = l + HALO + HALO, l >= CL - HALO + 1
        target = owner_row + 8 * shift
        ok = near & (target >= 0) & (target < 64)
        place = jnp.where(ok, half * 64 + target, -1)
        lefts.append(jnp.where(wide_sub == place, 1.0, 0.0))
        lines += [j.astype(F32), (r * ROWS + row).astype(F32)]
    sheet = jnp.transpose(jnp.concatenate(lines + [jnp.zeros((1, 128), F32)], axis=0))
    finish_low()

    inside = offsets % 128
    tile = offsets // 128 + jnp.where(wide_lane < inside, 1, 0)
    index = (inside + (wide_lane // 8) % STEPS) % 128
    copy.wait()
    window = jnp.broadcast_to(sheet[:, 0:1], (128, 128))
    for k in range(3):
        parts = [traces[k, :, 128 * i : 128 * i + 128] for i in range(4)]
        merged = jnp.where(
            tile == 0,
            parts[0],
            jnp.where(tile == 1, parts[1], jnp.where(tile == 2, parts[2], parts[3])),
        )
        picked = jnp.take_along_axis(merged, index, axis=1)
        window = jnp.where(wide_lane // 32 == k, picked, window)
    rights = []
    for i in range(3):
        slots = jnp.broadcast_to(sheet[:, 2 * i + 1 : 2 * i + 2], (128, 128)).astype(I32)
        cells = jnp.broadcast_to(sheet[:, 2 * i + 2 : 2 * i + 3], (128, 128))
        words = jnp.where((wide_lane >= 96) & (wide_lane < 104), cells, window)
        rights.append(jnp.where((wide_lane % 8 == slots) & (wide_lane < 112), words, 0.0))
    packed = lax.dot_general(
        jnp.concatenate(lefts, axis=1),
        jnp.concatenate(rights, axis=0),
        (((1,), (0,)), ((), ())),
        precision=lax.Precision.HIGHEST,
        preferred_element_type=F32,
    )
    out[:, 0, :128] = packed[:64]
    out[:, 0, 128:] = packed[64:]


def widen_kernel(
    cur, prv, mod, den, from_low, from_high, u, v, m, c, even, odd, left, right
):
    lat = lax.axis_index("lat")
    has_low, has_high = lat > 0, lat < lax.axis_size("lat") - 1

    def ghosts(f, r):
        spot = slice(HALO * (r % 2), HALO * (r % 2) + HALO)
        return jnp.concatenate(
            [
                jnp.where(has_high, from_high[f, r // 2, spot, :], 0.0),
                jnp.where(has_low, from_low[f, r // 2, spot, :], 0.0),
            ],
            axis=0,
        )

    for r in range(CR):
        for k in range(3):
            u[k, r, 0:CL, :] = cur[k, r]
            u[k, r, CL:ROWS, :] = ghosts(k, r)
            v[k, r, 0:CL, :] = prv[k, r]
            v[k, r, CL:ROWS, :] = ghosts(3 + k, r)
        for j in range(4):
            m[j, r, 0:CL, :] = mod[j, r]
            m[j, r, CL:ROWS, :] = ghosts(6 + j, r)
        c[r, 0:CL, :] = STEP_SQUARE / den[r]
        spot = slice(HALO * (r % 2), HALO * (r % 2) + HALO)
        outer = STEP_SQUARE / jnp.concatenate(
            [from_high[10, r // 2, spot, :], from_low[10, r // 2, spot, :]], axis=0
        )
        present = jnp.where(iota((8, 128), 0) < HALO, has_high.astype(I32), has_low.astype(I32))
        c[r, CL:ROWS, :] = jnp.where(present > 0, outer, 0.0)
    lead, rest = end_layers()
    for i, (field, k) in enumerate(((u, 0), (u, 1), (u, 2), (m, 0), (m, 2))):
        even[i] = field[k, rest]
        odd[i] = field[k, lead]
    left[...] = jnp.zeros_like(left)
    right[...] = jnp.zeros_like(right)
    put_columns(tiles_of(u, 3), left, right, 0)
    put_columns(tiles_of(m, 3, 1), left, right, 3)


def level(k, r, here, at_left, at_right, al, au, ad):
    _, jl, je = TABLE[k]
    flux = al[jl - 1, r] * (pltpu.roll(here, ROWS - 1, 0) - here)
    total = flux - pltpu.roll(flux, 1, 0)
    lane = iota((ROWS, CE), 1)
    after = jnp.where(lane == CE - 1, column(at_right, 0, k, r), pltpu.roll(here, CE - 1, 1))
    before = jnp.where(lane == 0, column(at_left, 0, k, r), pltpu.roll(here, 1, 1))
    return total + (au[je - 1, r] * (after - here) + ad[je - 1, r] * (before - here))


def force(k, r, u, low, high, at_left, at_right, ar, al, au, ad):
    i, here = TABLE[k][0] // 2, u[k, r]
    below = u[k, r - 1] if r > 0 else low[k]
    above = u[k, r + 1] if r < CR - 1 else high[k]
    total = ar[i, r + 1] * (above - here) - ar[i, r] * (here - below)
    return total + level(k, r, here, at_left, at_right, al, au, ad)


def radial_ends(even, odd, count):
    rad, is_even = lax.axis_index("rad"), rad_is_even()
    lows, highs = [], []
    for k in range(count):
        low = jnp.where(is_even, odd[k], even[k])
        high = jnp.where(is_even, even[k], odd[k])
        lows.append(jnp.where(rad > 0, low, 0.0))
        highs.append(jnp.where(rad < lax.axis_size("rad") - 1, high, 0.0))
    return lows, highs


def prepare_kernel(u, v, m, c, even, odd, at_left, at_right, ar, al, au, ad, following):
    lows, highs = radial_ends(even, odd, 5)
    lane = iota((ROWS, CE), 1)
    for i, j in enumerate((0, 2)):
        layers = [lows[3 + i]] + [m[j, r] for r in range(CR)] + [highs[3 + i]]
        for face in range(CR + 1):
            ar[i, face] = 0.5 * (layers[face] + layers[face + 1])
    for j in (1, 2, 3):
        for r in range(CR):
            here = m[j, r]
            al[j - 1, r] = 0.5 * (here + pltpu.roll(here, ROWS - 1, 0))
            after = jnp.where(
                lane == CE - 1, column(at_right, 3, j - 1, r), pltpu.roll(here, CE - 1, 1)
            )
            before = jnp.where(lane == 0, column(at_left, 3, j - 1, r), pltpu.roll(here, 1, 1))
            au[j - 1, r] = 0.5 * (here + after)
            ad[j - 1, r] = 0.5 * (here + before)
    for k in range(3):
        for r in range(CR):
            total = force(k, r, u, lows, highs, at_left, at_right, ar, al, au, ad)
            following[k, r] = 2.0 * u[k, r] - v[k, r] + c[r] * total


def thirds(x):
    high = x.astype(jnp.bfloat16).astype(F32)
    rest = x - high
    middle = rest.astype(jnp.bfloat16).astype(F32)
    return high, middle, rest - middle


def gather_sources(steps, got, weights, picks, layer=0, layers=CR):
    turned = jnp.transpose(jnp.concatenate([got[:, 0, :128], got[:, 0, 128:]], axis=0))
    parts = thirds(turned)
    cells = layers * ROWS
    cell_rows, cell_lanes = iota((cells, 128), 0) + layer * ROWS, iota((CE, 128), 0)
    for j in range(SLOTS):
        place = turned[96 + j : 97 + j].astype(I32)
        around = turned[104 + j : 105 + j].astype(I32)
        pick = jnp.where(cell_lanes == around, 1.0, 0.0)
        here = cell_rows == place
        for p in range(3):
            span = slice((p * SLOTS + j) * 128, (p * SLOTS + j + 1) * 128)
            picks[:, span] = pick
            for i, t in enumerate(steps):
                for k in range(3):
                    line = (k * STEPS + t) * 8 + j
                    at = (i * 3 + k) * cells
                    weights[at : at + cells, span] = jnp.where(
                        here, parts[p][line : line + 1], 0.0
                    )
    return lax.dot_general(
        weights[...], picks[...], (((1,), (1,)), ((), ())), preferred_element_type=F32
    )


def first_lead_kernel(got, free, c, odd, weights, picks):
    lead, _ = end_layers()
    summed = gather_sources((0,), got, weights, picks, lead, 1)
    for k in range(3):
        odd[k] = free[k, lead] + summed[k * ROWS : (k + 1) * ROWS] * c[lead]


def first_kernel(got, free, c, made, first, even, left, right, weights, picks):
    summed = gather_sources((0,), got, weights, picks)
    for k in range(3):
        for r in range(CR):
            at = (k * CR + r) * ROWS
            first[k, r] = free[k, r] + summed[at : at + ROWS] * c[r]
    keep_lead(first, made)
    put_rest(first, even, left, right)


def sources_kernel(got, c, sources, weights, picks):
    summed = gather_sources(range(1, STEPS), got, weights, picks)
    for t in range(STEPS - 1):
        for k in range(3):
            for r in range(CR):
                at = ((t * 3 + k) * CR + r) * ROWS
                sources[t, k, r] = summed[at : at + ROWS] * c[r]


def lead_kernel(t, u, v, c, sources, odd, at_left, at_right, ar, al, au, ad, out):
    lead, _ = end_layers()
    rad, downwards = lax.axis_index("rad"), rad_is_even()
    joined = jnp.where(downwards, rad > 0, rad < lax.axis_size("rad") - 1)
    inner = jnp.where(downwards, 1, CR - 2)
    outer_face, inner_face = jnp.where(downwards, 0, CR), jnp.where(downwards, 1, CR - 1)
    for k in range(3):
        i, here = TABLE[k][0] // 2, u[k, lead]
        outer = jnp.where(joined, odd[k], 0.0)
        total = ar[i, outer_face] * (outer - here) + ar[i, inner_face] * (u[k, inner] - here)
        total = total + level(k, lead, here, at_left, at_right, al, au, ad)
        value = 2.0 * here - v[k, lead] + c[lead] * total + sources[t - 1, k, lead]
        out[k] = value[: out.shape[1]]


def step_kernel(
    t, u, v, c, sources, even, odd, at_left, at_right, ar, al, au, ad, made, following, *rest
):
    lows, highs = radial_ends(even, odd, 3)
    for k in range(3):
        for r in range(CR):
            total = force(k, r, u, lows, highs, at_left, at_right, ar, al, au, ad)
            following[k, r] = 2.0 * u[k, r] - v[k, r] + c[r] * total + sources[t - 1, k, r]
    keep_lead(following, made)
    put_rest(following, *rest)


def last_kernel(
    u, v, c, sources, even, odd, at_left, at_right, ar, al, au, ad, final, before_final
):
    lows, highs = radial_ends(even, odd, 3)
    beside = jnp.zeros((ROWS - CL, CE), F32)
    lows = [jnp.concatenate([x, beside], axis=0) for x in lows]
    highs = [jnp.concatenate([x, beside], axis=0) for x in highs]
    for k in range(3):
        for r in range(CR):
            total = force(k, r, u, lows, highs, at_left, at_right, ar, al, au, ad)
            value = 2.0 * u[k, r] - v[k, r] + c[r] * total + sources[STEPS - 2, k, r]
            final[k, r] = value[:CL]
            before_final[k, r] = u[k, r, 0:CL, :]


def call(kernel, outs, args, scratch=(), hbm=0, us=1.0):
    vmem = pl.BlockSpec(memory_space=pltpu.VMEM)
    specs = [pl.BlockSpec(memory_space=pltpu.HBM)] * hbm + [vmem] * (len(args) - hbm)
    return pl.pallas_call(
        kernel,
        out_shape=[jax.ShapeDtypeStruct(shape, F32) for shape in outs],
        in_specs=specs,
        out_specs=[vmem] * len(outs),
        scratch_shapes=[pltpu.VMEM(s, F32) if isinstance(s, tuple) else s for s in scratch],
        cost_estimate=pl.CostEstimate(
            flops=0, bytes_accessed=int(us * 3_000_000), transcendentals=0
        ),
        compiler_params=pltpu.CompilerParams(vmem_limit_bytes=(60 if hbm else 32) * 1024 * 1024),
    )(*args)


def shifted(block, axis, by):
    count = lax.axis_size(axis)
    return lax.ppermute(block, axis, [(i, (i + by) % count) for i in range(count)])


def swapped(block, axis, odd):
    count = lax.axis_size(axis)
    pairs = [(i, (i + (1 if (i + odd) % 2 == 0 else -1)) % count) for i in range(count)]
    return lax.ppermute(block, axis, pairs)


def swap_columns(left, right):
    return shifted(right, "span", 1), shifted(left, "span", -1)


def on_device(current, previous, moduli, density, traces, receivers, owners, offsets):
    wide = (3, CR, ROWS, CE)
    edge = (11, 2, 8, CE)
    layer, columns = (3, ROWS, CE), [(8, CE), (8, CE)]

    fields = (current, previous, moduli, density.reshape((1,) + density.shape))
    rooms = [(11, CR, 8, CE), pltpu.SemaphoreType.DMA((4,))]
    (high_rows,) = call(high_kernel, [edge], fields, scratch=rooms, hbm=4)
    from_low = shifted(high_rows, "lat", 1)
    packed, low_rows = call(
        pack_kernel,
        [(64, 1, 256), edge],
        (
            offsets.reshape(1, 128),
            receivers.reshape(1, 128),
            owners.reshape(1, 128),
            traces.transpose(1, 0, 2),
        )
        + fields,
        scratch=rooms
        + [
            (3, STATIONS, 512),
            pltpu.VMEM((8, 128), I32),
            pltpu.SemaphoreType.DMA(()),
            pltpu.SemaphoreType.DMA((3,)),
        ],
        hbm=8,
        us=2.0,
    )
    from_high = shifted(low_rows, "lat", -1)
    got = lax.all_to_all(packed, ("lat", "rad"), 0, 0, tiled=True)

    u, v, m, c, even, odd, *ends = call(
        widen_kernel,
        [wide, wide, (4, CR, ROWS, CE), (CR, ROWS, CE)]
        + [(5, ROWS, CE), (5, ROWS, CE), (8, CE), (8, CE)],
        (current, previous, moduli, density, from_low, from_high),
    )
    *coefficients, free = call(
        prepare_kernel,
        [(2, CR + 1, ROWS, CE), wide, wide, wide, wide],
        (u, v, m, c, swapped(even, "rad", 0), swapped(odd, "rad", 1), *swap_columns(*ends)),
    )
    cells, lanes = CR * ROWS, 3 * SLOTS * 128
    (made,) = call(
        first_lead_kernel,
        [layer],
        (got, free, c),
        scratch=[(3 * ROWS, lanes), (CE, lanes)],
    )
    odd = swapped(made, "rad", 1)
    first, even, *ends = call(
        first_kernel,
        [wide, layer] + columns,
        (got, free, c, made),
        scratch=[(3 * cells, lanes), (CE, lanes)],
    )
    (sources,) = call(
        sources_kernel,
        [(STEPS - 1,) + wide],
        (got, c),
        scratch=[(3 * (STEPS - 1) * cells, lanes), (CE, lanes)],
        us=3.0,
    )
    v, u = u, first
    for t in range(1, STEPS):
        even = swapped(even, "rad", 0)
        at_left, at_right = swap_columns(*ends)
        before = (u, v, c, sources)
        after = (at_left, at_right, *coefficients)
        if t == STEPS - 1:
            return tuple(call(last_kernel, [(3, CR, CL, CE)] * 2, before + (even, odd) + after))
        if t == STEPS - 2:
            layer = (3, CL, CE)

        def lead(*refs, t=t):
            lead_kernel(t, *refs)

        def step(*refs, t=t):
            step_kernel(t, *refs)

        (made,) = call(lead, [layer], before + (odd,) + after)
        next_odd = swapped(made, "rad", 1)
        following, even, *ends = call(
            step, [wide, layer] + columns, before + (even, odd) + after + (made,)
        )
        v, u, odd = u, following, next_odd


def solution(mesh):
    in_specs = (
        P(None, "rad", "lat", "span"),
        P(None, "rad", "lat", "span"),
        P(None, "rad", "lat", "span"),
        P("rad", "lat", "span"),
        P(("span", "lat", "rad"), None, None),
        P(("span", "lat", "rad")),
        P(("span", "lat", "rad"), None),
        P(("span", "lat", "rad")),
    )
    out_specs = (P(None, "rad", "lat", "span"), P(None, "rad", "lat", "span"))
    return jax.shard_map(
        on_device, mesh=mesh, in_specs=in_specs, out_specs=out_specs, check_vma=False
    )
```

```python
import jax
import jax.numpy as jnp
from jax import lax
from jax.experimental import pallas as pl
from jax.experimental.pallas import tpu as pltpu
from jax.sharding import PartitionSpec as P

STEPS = 4
STEP_SQUARE = 0.16
TABLE = ((0, 2, 2), (2, 1, 3), (2, 3, 1))
CR, CL, CE = 4, 16, 128
HALO = 4
ROWS = CL + 2 * HALO
CAP = 4
SLOTS = 6
STATIONS = 128
F32 = jnp.float32
I32 = jnp.int32


def iota(shape, dim):
    return lax.broadcasted_iota(I32, shape, dim)


def fold(tiles, at):
    lane, sub = iota((8, 128), 1), iota((8, 128), 0)
    rows = []
    for start in range(0, len(tiles), 16):
        gathered = jnp.zeros((8, 128), F32)
        for i, tile in enumerate(tiles[start : start + 16]):
            column = jnp.broadcast_to(tile[:, at : at + 1], (8, 128))
            gathered = jnp.where(lane == i * 8 + sub, column, gathered)
        rows.append(jnp.sum(gathered, axis=0, keepdims=True))
    return rows


def unfold(ref, first_row, tile):
    row = first_row + tile // 16
    spread = jnp.broadcast_to(ref[pl.ds(row, 1), :], (8, 128))
    return jnp.take_along_axis(spread, (tile % 16) * 8 + iota((8, 128), 0), axis=1)


def column(ref, first_row, k, r):
    first = (k * CR + r) * (ROWS // 8)
    return jnp.concatenate([unfold(ref, first_row, first + i) for i in range(ROWS // 8)], axis=0)


def tiles_of(ref, count, first=0):
    return [
        ref[first + k, r, 8 * i : 8 * i + 8, :]
        for k in range(count)
        for r in range(CR)
        for i in range(ROWS // 8)
    ]


def put_columns(tiles, left_ref, right_ref, first_row):
    for ref, at in ((left_ref, 0), (right_ref, CE - 1)):
        for i, row in enumerate(fold(tiles, at)):
            ref[first_row + i : first_row + i + 1, :] = row


def rad_is_even():
    return lax.axis_index("rad") % 2 == 0


def end_layers():
    lead = jnp.where(rad_is_even(), 0, CR - 1)
    return lead, CR - 1 - lead


def keep_lead(u_ref, made):
    lead, _ = end_layers()
    for k in range(3):
        u_ref[k, lead] = made[k]


def put_rest(u_ref, even_ref, left_ref, right_ref):
    _, rest = end_layers()
    for k in range(3):
        even_ref[k] = u_ref[k, rest]
    left_ref[...] = jnp.zeros_like(left_ref)
    right_ref[...] = jnp.zeros_like(right_ref)
    put_columns(tiles_of(u_ref, 3), left_ref, right_ref, 0)


def edge_rows(start, fields, out, room, sems):
    first, copies = 0, []
    for i, ref in enumerate(fields):
        count = ref.shape[0]
        copies.append(
            pltpu.make_async_copy(
                ref.at[:, :, pl.ds(start, 8), :], room.at[pl.ds(first, count)], sems.at[i]
            )
        )
        first += count
    for copy in copies:
        copy.start()

    def finish():
        for copy in copies:
            copy.wait()
        inner = slice(0, HALO) if start == 0 else slice(8 - HALO, 8)
        for f in range(first):
            for r in range(CR):
                spot = slice(HALO * (r % 2), HALO * (r % 2) + HALO)
                out[f, r // 2, spot, :] = room[f, r, inner, :]

    return finish


def high_kernel(cur, prv, mod, den, high, room, sems):
    edge_rows(CL - 8, (cur, prv, mod, den), high, room, sems)()


def pack_kernel(
    offsets_in, receivers_in, owners_in, traces_in, cur, prv, mod, den, out, low,
    room, sems, traces, words_in, trace_sem, word_sems,
):
    copy = pltpu.make_async_copy(traces_in, traces, trace_sem)
    copy.start()
    small = [
        pltpu.make_async_copy(ref, words_in.at[pl.ds(i, 1)], word_sems.at[i])
        for i, ref in enumerate((offsets_in, receivers_in, owners_in))
    ]
    for one in small:
        one.start()
    finish_low = edge_rows(0, (cur, prv, mod, den), low, room, sems)
    for one in small:
        one.wait()
    offset_row, q, owner_row = words_in[0:1], words_in[1:2], words_in[2:3]
    r, l, e = q // 2048, (q // 128) % CL, q % 128
    wide_sub, wide_lane = iota((128, 128), 0), iota((128, 128), 1)
    sheet = jnp.transpose(
        jnp.concatenate(
            [owner_row.astype(F32), offset_row.astype(F32), jnp.zeros((6, 128), F32)], axis=0
        )
    )
    owner_cols = jnp.broadcast_to(sheet[:, 0:1], (128, 128)).astype(I32)
    offsets = jnp.broadcast_to(sheet[:, 1:2], (128, 128)).astype(I32)
    same = (owner_cols == owner_row) & (wide_sub < wide_lane)
    rank = jnp.sum(jnp.where(same, 1.0, 0.0), axis=0, keepdims=True).astype(I32)

    lefts, lines = [], [e.astype(F32)]
    for shift in (-1, 0, 1):
        slot = (shift + 1) * CAP + rank
        half, j = slot // SLOTS, slot % SLOTS
        if shift == 0:
            row, near = l, l >= 0
        elif shift == -1:
            row, near = CL + l, l <= HALO - 2
        else:
            row, near = l + HALO + HALO, l >= CL - HALO + 1
        target = owner_row + 8 * shift
        ok = near & (target >= 0) & (target < 64)
        place = jnp.where(ok, half * 64 + target, -1)
        lefts.append(jnp.where(wide_sub == place, 1.0, 0.0))
        lines += [j.astype(F32), (r * ROWS + row).astype(F32)]
    sheet = jnp.transpose(jnp.concatenate(lines + [jnp.zeros((1, 128), F32)], axis=0))
    finish_low()

    inside = offsets % 128
    tile = offsets // 128 + jnp.where(wide_lane < inside, 1, 0)
    index = (inside + (wide_lane // 8) % STEPS) % 128
    copy.wait()
    window = jnp.broadcast_to(sheet[:, 0:1], (128, 128))
    for k in range(3):
        parts = [traces[k, :, 128 * i : 128 * i + 128] for i in range(4)]
        merged = jnp.where(
            tile == 0,
            parts[0],
            jnp.where(tile == 1, parts[1], jnp.where(tile == 2, parts[2], parts[3])),
        )
        picked = jnp.take_along_axis(merged, index, axis=1)
        window = jnp.where(wide_lane // 32 == k, picked, window)
    rights = []
    for i in range(3):
        slots = jnp.broadcast_to(sheet[:, 2 * i + 1 : 2 * i + 2], (128, 128)).astype(I32)
        cells = jnp.broadcast_to(sheet[:, 2 * i + 2 : 2 * i + 3], (128, 128))
        words = jnp.where((wide_lane >= 96) & (wide_lane < 104), cells, window)
        rights.append(jnp.where((wide_lane % 8 == slots) & (wide_lane < 112), words, 0.0))
    packed = lax.dot_general(
        jnp.concatenate(lefts, axis=1),
        jnp.concatenate(rights, axis=0),
        (((1,), (0,)), ((), ())),
        precision=lax.Precision.HIGHEST,
        preferred_element_type=F32,
    )
    out[:, 0, :128] = packed[:64]
    out[:, 0, 128:] = packed[64:]


def widen_kernel(
    cur, prv, mod, den, from_low, from_high, u, v, m, c, even, odd, left, right
):
    lat = lax.axis_index("lat")
    has_low, has_high = lat > 0, lat < lax.axis_size("lat") - 1

    def ghosts(f, r):
        spot = slice(HALO * (r % 2), HALO * (r % 2) + HALO)
        return jnp.concatenate(
            [
                jnp.where(has_high, from_high[f, r // 2, spot, :], 0.0),
                jnp.where(has_low, from_low[f, r // 2, spot, :], 0.0),
            ],
            axis=0,
        )

    for r in range(CR):
        for k in range(3):
            u[k, r, 0:CL, :] = cur[k, r]
            u[k, r, CL:ROWS, :] = ghosts(k, r)
            v[k, r, 0:CL, :] = prv[k, r]
            v[k, r, CL:ROWS, :] = ghosts(3 + k, r)
        for j in range(4):
            m[j, r, 0:CL, :] = mod[j, r]
            m[j, r, CL:ROWS, :] = ghosts(6 + j, r)
        c[r, 0:CL, :] = STEP_SQUARE / den[r]
        spot = slice(HALO * (r % 2), HALO * (r % 2) + HALO)
        outer = STEP_SQUARE / jnp.concatenate(
            [from_high[10, r // 2, spot, :], from_low[10, r // 2, spot, :]], axis=0
        )
        present = jnp.where(iota((8, 128), 0) < HALO, has_high.astype(I32), has_low.astype(I32))
        c[r, CL:ROWS, :] = jnp.where(present > 0, outer, 0.0)
    lead, rest = end_layers()
    for i, (field, k) in enumerate(((u, 0), (u, 1), (u, 2), (m, 0), (m, 2))):
        even[i] = field[k, rest]
        odd[i] = field[k, lead]
    left[...] = jnp.zeros_like(left)
    right[...] = jnp.zeros_like(right)
    put_columns(tiles_of(u, 3), left, right, 0)
    put_columns(tiles_of(m, 3, 1), left, right, 3)


def level(k, r, here, at_left, at_right, al, au, ad):
    _, jl, je = TABLE[k]
    flux = al[jl - 1, r] * (pltpu.roll(here, ROWS - 1, 0) - here)
    total = flux - pltpu.roll(flux, 1, 0)
    lane = iota((ROWS, CE), 1)
    after = jnp.where(lane == CE - 1, column(at_right, 0, k, r), pltpu.roll(here, CE - 1, 1))
    before = jnp.where(lane == 0, column(at_left, 0, k, r), pltpu.roll(here, 1, 1))
    return total + (au[je - 1, r] * (after - here) + ad[je - 1, r] * (before - here))


def force(k, r, u, low, high, at_left, at_right, ar, al, au, ad):
    i, here = TABLE[k][0] // 2, u[k, r]
    below = u[k, r - 1] if r > 0 else low[k]
    above = u[k, r + 1] if r < CR - 1 else high[k]
    total = ar[i, r + 1] * (above - here) - ar[i, r] * (here - below)
    return total + level(k, r, here, at_left, at_right, al, au, ad)


def radial_ends(even, odd, count):
    rad, is_even = lax.axis_index("rad"), rad_is_even()
    lows, highs = [], []
    for k in range(count):
        low = jnp.where(is_even, odd[k], even[k])
        high = jnp.where(is_even, even[k], odd[k])
        lows.append(jnp.where(rad > 0, low, 0.0))
        highs.append(jnp.where(rad < lax.axis_size("rad") - 1, high, 0.0))
    return lows, highs


def prepare_kernel(u, v, m, c, even, odd, at_left, at_right, ar, al, au, ad, following):
    lows, highs = radial_ends(even, odd, 5)
    lane = iota((ROWS, CE), 1)
    for i, j in enumerate((0, 2)):
        layers = [lows[3 + i]] + [m[j, r] for r in range(CR)] + [highs[3 + i]]
        for face in range(CR + 1):
            ar[i, face] = 0.5 * (layers[face] + layers[face + 1])
    for j in (1, 2, 3):
        for r in range(CR):
            here = m[j, r]
            al[j - 1, r] = 0.5 * (here + pltpu.roll(here, ROWS - 1, 0))
            after = jnp.where(
                lane == CE - 1, column(at_right, 3, j - 1, r), pltpu.roll(here, CE - 1, 1)
            )
            before = jnp.where(lane == 0, column(at_left, 3, j - 1, r), pltpu.roll(here, 1, 1))
            au[j - 1, r] = 0.5 * (here + after)
            ad[j - 1, r] = 0.5 * (here + before)
    for k in range(3):
        for r in range(CR):
            total = force(k, r, u, lows, highs, at_left, at_right, ar, al, au, ad)
            following[k, r] = 2.0 * u[k, r] - v[k, r] + c[r] * total


def thirds(x):
    high = x.astype(jnp.bfloat16).astype(F32)
    rest = x - high
    middle = rest.astype(jnp.bfloat16).astype(F32)
    return high, middle, rest - middle


def gather_sources(steps, got, weights, picks, layer=0, layers=CR):
    turned = jnp.transpose(jnp.concatenate([got[:, 0, :128], got[:, 0, 128:]], axis=0))
    parts = thirds(turned)
    cells = layers * ROWS
    cell_rows, cell_lanes = iota((cells, 128), 0) + layer * ROWS, iota((CE, 128), 0)
    for j in range(SLOTS):
        place = turned[96 + j : 97 + j].astype(I32)
        around = turned[104 + j : 105 + j].astype(I32)
        pick = jnp.where(cell_lanes == around, 1.0, 0.0)
        here = cell_rows == place
        for p in range(3):
            span = slice((p * SLOTS + j) * 128, (p * SLOTS + j + 1) * 128)
            picks[:, span] = pick
            for i, t in enumerate(steps):
                for k in range(3):
                    line = (k * STEPS + t) * 8 + j
                    at = (i * 3 + k) * cells
                    weights[at : at + cells, span] = jnp.where(
                        here, parts[p][line : line + 1], 0.0
                    )
    return lax.dot_general(
        weights[...], picks[...], (((1,), (1,)), ((), ())), preferred_element_type=F32
    )


def first_kernel(got, free, c, first, even, odd, left, right, weights, picks):
    summed = gather_sources((0,), got, weights, picks)
    for k in range(3):
        for r in range(CR):
            at = (k * CR + r) * ROWS
            first[k, r] = free[k, r] + summed[at : at + ROWS] * c[r]
    lead, _ = end_layers()
    for k in range(3):
        odd[k] = first[k, lead]
    put_rest(first, even, left, right)


def sources_kernel(got, c, sources, weights, picks):
    summed = gather_sources(range(1, STEPS), got, weights, picks)
    for t in range(STEPS - 1):
        for k in range(3):
            for r in range(CR):
                at = ((t * 3 + k) * CR + r) * ROWS
                sources[t, k, r] = summed[at : at + ROWS] * c[r]


def lead_kernel(t, u, v, c, sources, odd, at_left, at_right, ar, al, au, ad, out):
    lead, _ = end_layers()
    rad, downwards = lax.axis_index("rad"), rad_is_even()
    joined = jnp.where(downwards, rad > 0, rad < lax.axis_size("rad") - 1)
    inner = jnp.where(downwards, 1, CR - 2)
    outer_face, inner_face = jnp.where(downwards, 0, CR), jnp.where(downwards, 1, CR - 1)
    for k in range(3):
        i, here = TABLE[k][0] // 2, u[k, lead]
        outer = jnp.where(joined, odd[k], 0.0)
        total = ar[i, outer_face] * (outer - here) + ar[i, inner_face] * (u[k, inner] - here)
        total = total + level(k, lead, here, at_left, at_right, al, au, ad)
        out[k] = 2.0 * here - v[k, lead] + c[lead] * total + sources[t - 1, k, lead]


def step_kernel(
    t, u, v, c, sources, even, odd, at_left, at_right, ar, al, au, ad, made, following, *rest
):
    lows, highs = radial_ends(even, odd, 3)
    for k in range(3):
        for r in range(CR):
            total = force(k, r, u, lows, highs, at_left, at_right, ar, al, au, ad)
            following[k, r] = 2.0 * u[k, r] - v[k, r] + c[r] * total + sources[t - 1, k, r]
    keep_lead(following, made)
    put_rest(following, *rest)


def last_kernel(
    u, v, c, sources, even, odd, at_left, at_right, ar, al, au, ad, made, final, before_final
):
    lows, highs = radial_ends(even, odd, 3)
    for k in range(3):
        for r in range(CR):
            total = force(k, r, u, lows, highs, at_left, at_right, ar, al, au, ad)
            value = 2.0 * u[k, r] - v[k, r] + c[r] * total + sources[STEPS - 2, k, r]
            final[k, r] = value[:CL]
            before_final[k, r] = u[k, r, 0:CL, :]
    lead, _ = end_layers()
    for k in range(3):
        final[k, lead] = made[k, 0:CL, :]


def call(kernel, outs, args, scratch=(), hbm=0, us=1.0):
    vmem = pl.BlockSpec(memory_space=pltpu.VMEM)
    specs = [pl.BlockSpec(memory_space=pltpu.HBM)] * hbm + [vmem] * (len(args) - hbm)
    return pl.pallas_call(
        kernel,
        out_shape=[jax.ShapeDtypeStruct(shape, F32) for shape in outs],
        in_specs=specs,
        out_specs=[vmem] * len(outs),
        scratch_shapes=[pltpu.VMEM(s, F32) if isinstance(s, tuple) else s for s in scratch],
        cost_estimate=pl.CostEstimate(
            flops=0, bytes_accessed=int(us * 3_000_000), transcendentals=0
        ),
        compiler_params=pltpu.CompilerParams(vmem_limit_bytes=(60 if hbm else 32) * 1024 * 1024),
    )(*args)


def shifted(block, axis, by):
    count = lax.axis_size(axis)
    return lax.ppermute(block, axis, [(i, (i + by) % count) for i in range(count)])


def swapped(block, axis, odd):
    count = lax.axis_size(axis)
    pairs = [(i, (i + (1 if (i + odd) % 2 == 0 else -1)) % count) for i in range(count)]
    return lax.ppermute(block, axis, pairs)


def swap_columns(left, right):
    return shifted(right, "span", 1), shifted(left, "span", -1)


def on_device(current, previous, moduli, density, traces, receivers, owners, offsets):
    wide = (3, CR, ROWS, CE)
    edge = (11, 2, 8, CE)
    layer, columns = (3, ROWS, CE), [(8, CE), (8, CE)]

    fields = (current, previous, moduli, density.reshape((1,) + density.shape))
    rooms = [(11, CR, 8, CE), pltpu.SemaphoreType.DMA((4,))]
    (high_rows,) = call(high_kernel, [edge], fields, scratch=rooms, hbm=4)
    from_low = shifted(high_rows, "lat", 1)
    packed, low_rows = call(
        pack_kernel,
        [(64, 1, 256), edge],
        (
            offsets.reshape(1, 128),
            receivers.reshape(1, 128),
            owners.reshape(1, 128),
            traces.transpose(1, 0, 2),
        )
        + fields,
        scratch=rooms
        + [
            (3, STATIONS, 512),
            pltpu.VMEM((8, 128), I32),
            pltpu.SemaphoreType.DMA(()),
            pltpu.SemaphoreType.DMA((3,)),
        ],
        hbm=8,
        us=2.0,
    )
    from_high = shifted(low_rows, "lat", -1)
    got = lax.all_to_all(packed, ("lat", "rad"), 0, 0, tiled=True)

    u, v, m, c, even, odd, *ends = call(
        widen_kernel,
        [wide, wide, (4, CR, ROWS, CE), (CR, ROWS, CE)]
        + [(5, ROWS, CE), (5, ROWS, CE), (8, CE), (8, CE)],
        (current, previous, moduli, density, from_low, from_high),
    )
    *coefficients, free = call(
        prepare_kernel,
        [(2, CR + 1, ROWS, CE), wide, wide, wide, wide],
        (u, v, m, c, swapped(even, "rad", 0), swapped(odd, "rad", 1), *swap_columns(*ends)),
    )
    cells, lanes = CR * ROWS, 3 * SLOTS * 128
    first, even, odd, *ends = call(
        first_kernel,
        [wide, layer, layer] + columns,
        (got, free, c),
        scratch=[(3 * cells, lanes), (CE, lanes)],
    )
    (sources,) = call(
        sources_kernel,
        [(STEPS - 1,) + wide],
        (got, c),
        scratch=[(3 * (STEPS - 1) * cells, lanes), (CE, lanes)],
        us=3.0,
    )
    odd = swapped(odd, "rad", 1)
    v, u = u, first
    for t in range(1, STEPS):
        even = swapped(even, "rad", 0)
        at_left, at_right = swap_columns(*ends)
        before = (u, v, c, sources)
        after = (at_left, at_right, *coefficients)

        def lead(*refs, t=t):
            lead_kernel(t, *refs)

        def step(*refs, t=t):
            step_kernel(t, *refs)

        (made,) = call(lead, [layer], before + (odd,) + after)
        if t == STEPS - 1:
            args = before + (even, odd) + after + (made,)
            return tuple(call(last_kernel, [(3, CR, CL, CE)] * 2, args))
        next_odd = swapped(made, "rad", 1)
        following, even, *ends = call(
            step, [wide, layer] + columns, before + (even, odd) + after + (made,)
        )
        v, u, odd = u, following, next_odd


def solution(mesh):
    in_specs = (
        P(None, "rad", "lat", "span"),
        P(None, "rad", "lat", "span"),
        P(None, "rad", "lat", "span"),
        P("rad", "lat", "span"),
        P(("span", "lat", "rad"), None, None),
        P(("span", "lat", "rad")),
        P(("span", "lat", "rad"), None),
        P(("span", "lat", "rad")),
    )
    out_specs = (P(None, "rad", "lat", "span"), P(None, "rad", "lat", "span"))
    return jax.shard_map(
        on_device, mesh=mesh, in_specs=in_specs, out_specs=out_specs, check_vma=False
    )
```

```python
import jax
import jax.numpy as jnp
from jax import lax
from jax.experimental import pallas as pl
from jax.experimental.pallas import tpu as pltpu
from jax.sharding import PartitionSpec as P

STEPS = 4
STEP_SQUARE = 0.16
TABLE = ((0, 2, 2), (2, 1, 3), (2, 3, 1))
CR, CL, CE = 4, 16, 128
HALO = 4
ROWS = CL + 2 * HALO
CAP = 4
SLOTS = 6
STATIONS = 128
F32 = jnp.float32
I32 = jnp.int32


def iota(shape, dim):
    return lax.broadcasted_iota(I32, shape, dim)


def fold(tiles, at):
    lane, sub = iota((8, 128), 1), iota((8, 128), 0)
    rows = []
    for start in range(0, len(tiles), 16):
        gathered = jnp.zeros((8, 128), F32)
        for i, tile in enumerate(tiles[start : start + 16]):
            column = jnp.broadcast_to(tile[:, at : at + 1], (8, 128))
            gathered = jnp.where(lane == i * 8 + sub, column, gathered)
        rows.append(jnp.sum(gathered, axis=0, keepdims=True))
    return rows


def unfold(ref, first_row, tile):
    row = first_row + tile // 16
    spread = jnp.broadcast_to(ref[pl.ds(row, 1), :], (8, 128))
    return jnp.take_along_axis(spread, (tile % 16) * 8 + iota((8, 128), 0), axis=1)


def column(ref, first_row, k, r):
    first = (k * CR + r) * (ROWS // 8)
    return jnp.concatenate([unfold(ref, first_row, first + i) for i in range(ROWS // 8)], axis=0)


def tiles_of(ref, count, first=0):
    return [
        ref[first + k, r, 8 * i : 8 * i + 8, :]
        for k in range(count)
        for r in range(CR)
        for i in range(ROWS // 8)
    ]


def put_columns(tiles, left_ref, right_ref, first_row):
    for ref, at in ((left_ref, 0), (right_ref, CE - 1)):
        for i, row in enumerate(fold(tiles, at)):
            ref[first_row + i : first_row + i + 1, :] = row


def rad_is_even():
    return lax.axis_index("rad") % 2 == 0


def end_layers():
    lead = jnp.where(rad_is_even(), 0, CR - 1)
    return lead, CR - 1 - lead


def keep_lead(u_ref, made):
    lead, _ = end_layers()
    for k in range(3):
        u_ref[k, lead] = made[k]


def put_rest(u_ref, even_ref, left_ref, right_ref):
    _, rest = end_layers()
    for k in range(3):
        even_ref[k] = u_ref[k, rest]
    left_ref[...] = jnp.zeros_like(left_ref)
    right_ref[...] = jnp.zeros_like(right_ref)
    put_columns(tiles_of(u_ref, 3), left_ref, right_ref, 0)


def edge_rows(start, fields, out, room, sems):
    first, copies = 0, []
    for i, ref in enumerate(fields):
        count = ref.shape[0]
        copies.append(
            pltpu.make_async_copy(
                ref.at[:, :, pl.ds(start, 8), :], room.at[pl.ds(first, count)], sems.at[i]
            )
        )
        first += count
    for copy in copies:
        copy.start()

    def finish():
        for copy in copies:
            copy.wait()
        inner = slice(0, HALO) if start == 0 else slice(8 - HALO, 8)
        for f in range(first):
            for r in range(CR):
                spot = slice(HALO * (r % 2), HALO * (r % 2) + HALO)
                out[f, r // 2, spot, :] = room[f, r, inner, :]

    return finish


def high_kernel(cur, prv, mod, den, high, room, sems):
    edge_rows(CL - 8, (cur, prv, mod, den), high, room, sems)()


def pack_kernel(
    offsets_in, receivers_in, owners_in, traces_in, cur, prv, mod, den, out, low,
    room, sems, traces, words_in, trace_sem, word_sems,
):
    copy = pltpu.make_async_copy(traces_in, traces, trace_sem)
    copy.start()
    small = [
        pltpu.make_async_copy(ref, words_in.at[pl.ds(i, 1)], word_sems.at[i])
        for i, ref in enumerate((offsets_in, receivers_in, owners_in))
    ]
    for one in small:
        one.start()
    finish_low = edge_rows(0, (cur, prv, mod, den), low, room, sems)
    for one in small:
        one.wait()
    offset_row, q, owner_row = words_in[0:1], words_in[1:2], words_in[2:3]
    r, l, e = q // 2048, (q // 128) % CL, q % 128
    wide_sub, wide_lane = iota((128, 128), 0), iota((128, 128), 1)
    sheet = jnp.transpose(
        jnp.concatenate(
            [owner_row.astype(F32), offset_row.astype(F32), jnp.zeros((6, 128), F32)], axis=0
        )
    )
    owner_cols = jnp.broadcast_to(sheet[:, 0:1], (128, 128)).astype(I32)
    offsets = jnp.broadcast_to(sheet[:, 1:2], (128, 128)).astype(I32)
    same = (owner_cols == owner_row) & (wide_sub < wide_lane)
    rank = jnp.sum(jnp.where(same, 1.0, 0.0), axis=0, keepdims=True).astype(I32)

    lefts, lines = [], [e.astype(F32)]
    for shift in (-1, 0, 1):
        slot = (shift + 1) * CAP + rank
        half, j = slot // SLOTS, slot % SLOTS
        if shift == 0:
            row, near = l, l >= 0
        elif shift == -1:
            row, near = CL + l, l <= HALO - 2
        else:
            row, near = l + HALO + HALO, l >= CL - HALO + 1
        target = owner_row + 8 * shift
        ok = near & (target >= 0) & (target < 64)
        place = jnp.where(ok, half * 64 + target, -1)
        lefts.append(jnp.where(wide_sub == place, 1.0, 0.0))
        lines += [j.astype(F32), (r * ROWS + row).astype(F32)]
    sheet = jnp.transpose(jnp.concatenate(lines + [jnp.zeros((1, 128), F32)], axis=0))
    finish_low()

    inside = offsets % 128
    tile = offsets // 128 + jnp.where(wide_lane < inside, 1, 0)
    index = (inside + (wide_lane // 8) % STEPS) % 128
    copy.wait()
    window = jnp.broadcast_to(sheet[:, 0:1], (128, 128))
    for k in range(3):
        parts = [traces[k, :, 128 * i : 128 * i + 128] for i in range(4)]
        merged = jnp.where(
            tile == 0,
            parts[0],
            jnp.where(tile == 1, parts[1], jnp.where(tile == 2, parts[2], parts[3])),
        )
        picked = jnp.take_along_axis(merged, index, axis=1)
        window = jnp.where(wide_lane // 32 == k, picked, window)
    rights = []
    for i in range(3):
        slots = jnp.broadcast_to(sheet[:, 2 * i + 1 : 2 * i + 2], (128, 128)).astype(I32)
        cells = jnp.broadcast_to(sheet[:, 2 * i + 2 : 2 * i + 3], (128, 128))
        words = jnp.where((wide_lane >= 96) & (wide_lane < 104), cells, window)
        rights.append(jnp.where((wide_lane % 8 == slots) & (wide_lane < 112), words, 0.0))
    packed = lax.dot_general(
        jnp.concatenate(lefts, axis=1),
        jnp.concatenate(rights, axis=0),
        (((1,), (0,)), ((), ())),
        precision=lax.Precision.HIGHEST,
        preferred_element_type=F32,
    )
    out[:, 0, :128] = packed[:64]
    out[:, 0, 128:] = packed[64:]


def widen_kernel(
    cur, prv, mod, den, from_low, from_high, u, v, m, c, even, odd, left, right
):
    lat = lax.axis_index("lat")
    has_low, has_high = lat > 0, lat < lax.axis_size("lat") - 1

    def ghosts(f, r):
        spot = slice(HALO * (r % 2), HALO * (r % 2) + HALO)
        return jnp.concatenate(
            [
                jnp.where(has_high, from_high[f, r // 2, spot, :], 0.0),
                jnp.where(has_low, from_low[f, r // 2, spot, :], 0.0),
            ],
            axis=0,
        )

    for r in range(CR):
        for k in range(3):
            u[k, r, 0:CL, :] = cur[k, r]
            u[k, r, CL:ROWS, :] = ghosts(k, r)
            v[k, r, 0:CL, :] = prv[k, r]
            v[k, r, CL:ROWS, :] = ghosts(3 + k, r)
        for j in range(4):
            m[j, r, 0:CL, :] = mod[j, r]
            m[j, r, CL:ROWS, :] = ghosts(6 + j, r)
        c[r, 0:CL, :] = STEP_SQUARE / den[r]
        spot = slice(HALO * (r % 2), HALO * (r % 2) + HALO)
        outer = STEP_SQUARE / jnp.concatenate(
            [from_high[10, r // 2, spot, :], from_low[10, r // 2, spot, :]], axis=0
        )
        present = jnp.where(iota((8, 128), 0) < HALO, has_high.astype(I32), has_low.astype(I32))
        c[r, CL:ROWS, :] = jnp.where(present > 0, outer, 0.0)
    lead, rest = end_layers()
    for i, (field, k) in enumerate(((u, 0), (u, 1), (u, 2), (m, 0), (m, 2))):
        even[i] = field[k, rest]
        odd[i] = field[k, lead]
    left[...] = jnp.zeros_like(left)
    right[...] = jnp.zeros_like(right)
    put_columns(tiles_of(u, 3), left, right, 0)
    put_columns(tiles_of(m, 3, 1), left, right, 3)


def level(k, r, here, at_left, at_right, al, au, ad):
    _, jl, je = TABLE[k]
    flux = al[jl - 1, r] * (pltpu.roll(here, ROWS - 1, 0) - here)
    total = flux - pltpu.roll(flux, 1, 0)
    lane = iota((ROWS, CE), 1)
    after = jnp.where(lane == CE - 1, column(at_right, 0, k, r), pltpu.roll(here, CE - 1, 1))
    before = jnp.where(lane == 0, column(at_left, 0, k, r), pltpu.roll(here, 1, 1))
    return total + (au[je - 1, r] * (after - here) + ad[je - 1, r] * (before - here))


def force(k, r, u, low, high, at_left, at_right, ar, al, au, ad):
    i, here = TABLE[k][0] // 2, u[k, r]
    below = u[k, r - 1] if r > 0 else low[k]
    above = u[k, r + 1] if r < CR - 1 else high[k]
    total = ar[i, r + 1] * (above - here) - ar[i, r] * (here - below)
    return total + level(k, r, here, at_left, at_right, al, au, ad)


def radial_ends(even, odd, count):
    rad, is_even = lax.axis_index("rad"), rad_is_even()
    lows, highs = [], []
    for k in range(count):
        low = jnp.where(is_even, odd[k], even[k])
        high = jnp.where(is_even, even[k], odd[k])
        lows.append(jnp.where(rad > 0, low, 0.0))
        highs.append(jnp.where(rad < lax.axis_size("rad") - 1, high, 0.0))
    return lows, highs


def prepare_kernel(u, v, m, c, even, odd, at_left, at_right, ar, al, au, ad, following):
    lows, highs = radial_ends(even, odd, 5)
    lane = iota((ROWS, CE), 1)
    for i, j in enumerate((0, 2)):
        layers = [lows[3 + i]] + [m[j, r] for r in range(CR)] + [highs[3 + i]]
        for face in range(CR + 1):
            ar[i, face] = 0.5 * (layers[face] + layers[face + 1])
    for j in (1, 2, 3):
        for r in range(CR):
            here = m[j, r]
            al[j - 1, r] = 0.5 * (here + pltpu.roll(here, ROWS - 1, 0))
            after = jnp.where(
                lane == CE - 1, column(at_right, 3, j - 1, r), pltpu.roll(here, CE - 1, 1)
            )
            before = jnp.where(lane == 0, column(at_left, 3, j - 1, r), pltpu.roll(here, 1, 1))
            au[j - 1, r] = 0.5 * (here + after)
            ad[j - 1, r] = 0.5 * (here + before)
    for k in range(3):
        for r in range(CR):
            total = force(k, r, u, lows, highs, at_left, at_right, ar, al, au, ad)
            following[k, r] = 2.0 * u[k, r] - v[k, r] + c[r] * total


def thirds(x):
    high = x.astype(jnp.bfloat16).astype(F32)
    rest = x - high
    middle = rest.astype(jnp.bfloat16).astype(F32)
    return high, middle, rest - middle


def gather_sources(steps, got, weights, picks, layer=0, layers=CR):
    turned = jnp.transpose(jnp.concatenate([got[:, 0, :128], got[:, 0, 128:]], axis=0))
    parts = thirds(turned)
    cells = layers * ROWS
    cell_rows, cell_lanes = iota((cells, 128), 0) + layer * ROWS, iota((CE, 128), 0)
    for j in range(SLOTS):
        place = turned[96 + j : 97 + j].astype(I32)
        around = turned[104 + j : 105 + j].astype(I32)
        pick = jnp.where(cell_lanes == around, 1.0, 0.0)
        here = cell_rows == place
        for p in range(3):
            span = slice((p * SLOTS + j) * 128, (p * SLOTS + j + 1) * 128)
            picks[:, span] = pick
            for i, t in enumerate(steps):
                for k in range(3):
                    line = (k * STEPS + t) * 8 + j
                    at = (i * 3 + k) * cells
                    weights[at : at + cells, span] = jnp.where(
                        here, parts[p][line : line + 1], 0.0
                    )
    return lax.dot_general(
        weights[...], picks[...], (((1,), (1,)), ((), ())), preferred_element_type=F32
    )


def first_kernel(got, free, c, first, even, odd, left, right, weights, picks):
    summed = gather_sources((0,), got, weights, picks)
    for k in range(3):
        for r in range(CR):
            at = (k * CR + r) * ROWS
            first[k, r] = free[k, r] + summed[at : at + ROWS] * c[r]
    lead, _ = end_layers()
    for k in range(3):
        odd[k] = first[k, lead]
    put_rest(first, even, left, right)


def sources_kernel(got, c, sources, weights, picks):
    summed = gather_sources(range(1, STEPS), got, weights, picks)
    for t in range(STEPS - 1):
        for k in range(3):
            for r in range(CR):
                at = ((t * 3 + k) * CR + r) * ROWS
                sources[t, k, r] = summed[at : at + ROWS] * c[r]


def lead_kernel(t, u, v, c, sources, odd, at_left, at_right, ar, al, au, ad, out):
    lead, _ = end_layers()
    rad, downwards = lax.axis_index("rad"), rad_is_even()
    joined = jnp.where(downwards, rad > 0, rad < lax.axis_size("rad") - 1)
    inner = jnp.where(downwards, 1, CR - 2)
    outer_face, inner_face = jnp.where(downwards, 0, CR), jnp.where(downwards, 1, CR - 1)
    for k in range(3):
        i, here = TABLE[k][0] // 2, u[k, lead]
        outer = jnp.where(joined, odd[k], 0.0)
        total = ar[i, outer_face] * (outer - here) + ar[i, inner_face] * (u[k, inner] - here)
        total = total + level(k, lead, here, at_left, at_right, al, au, ad)
        out[k] = 2.0 * here - v[k, lead] + c[lead] * total + sources[t - 1, k, lead]


def step_kernel(
    t, u, v, c, sources, even, odd, at_left, at_right, ar, al, au, ad, made, following, *rest
):
    lows, highs = radial_ends(even, odd, 3)
    for k in range(3):
        for r in range(CR):
            total = force(k, r, u, lows, highs, at_left, at_right, ar, al, au, ad)
            following[k, r] = 2.0 * u[k, r] - v[k, r] + c[r] * total + sources[t - 1, k, r]
    keep_lead(following, made)
    put_rest(following, *rest)


def base_kernel(u, v, c, sources, ar, al, base, before_final):
    for k in range(3):
        i, jl = TABLE[k][0] // 2, TABLE[k][1] - 1
        for r in range(CR):
            here = u[k, r]
            flux = al[jl, r] * (pltpu.roll(here, ROWS - 1, 0) - here)
            total = flux - pltpu.roll(flux, 1, 0)
            if r < CR - 1:
                total = total + ar[i, r + 1] * (u[k, r + 1] - here)
            if r > 0:
                total = total - ar[i, r] * (here - u[k, r - 1])
            value = 2.0 * here - v[k, r] + c[r] * total + sources[STEPS - 2, k, r]
            base[k, r] = value[:CL]
            before_final[k, r] = here[:CL]


def end_kernel(u, c, odd, ar, out):
    lead, _ = end_layers()
    rad, downwards = lax.axis_index("rad"), rad_is_even()
    joined = jnp.where(downwards, rad > 0, rad < lax.axis_size("rad") - 1)
    face = jnp.where(downwards, 0, CR)
    for k in range(3):
        outer = jnp.where(joined, odd[k, 0:CL, :], 0.0)
        coefficient = c[lead, 0:CL, :] * ar[TABLE[k][0] // 2, face, 0:CL, :]
        out[k] = coefficient * (outer - u[k, lead, 0:CL, :])


def last_kernel(u, c, base, even, made, at_left, at_right, ar, au, ad, final):
    lane = iota((CL, CE), 1)
    for k in range(3):
        je = TABLE[k][2] - 1
        for r in range(CR):
            here = u[k, r, 0:CL, :]
            right, left = column(at_right, 0, k, r)[:CL], column(at_left, 0, k, r)[:CL]
            after = jnp.where(lane == CE - 1, right, pltpu.roll(here, CE - 1, 1))
            before = jnp.where(lane == 0, left, pltpu.roll(here, 1, 1))
            total = au[je, r, 0:CL, :] * (after - here) + ad[je, r, 0:CL, :] * (before - here)
            final[k, r] = base[k, r] + c[r, 0:CL, :] * total
    lead, rest = end_layers()
    face = jnp.where(rad_is_even(), CR, 0)
    for k in range(3):
        coefficient = c[rest, 0:CL, :] * ar[TABLE[k][0] // 2, face, 0:CL, :]
        flux = coefficient * (even[k, 0:CL, :] - u[k, rest, 0:CL, :])
        final[k, rest] = final[k, rest] + flux
        final[k, lead] = final[k, lead] + made[k]


def call(kernel, outs, args, scratch=(), hbm=0, us=1.0):
    vmem = pl.BlockSpec(memory_space=pltpu.VMEM)
    specs = [pl.BlockSpec(memory_space=pltpu.HBM)] * hbm + [vmem] * (len(args) - hbm)
    return pl.pallas_call(
        kernel,
        out_shape=[jax.ShapeDtypeStruct(shape, F32) for shape in outs],
        in_specs=specs,
        out_specs=[vmem] * len(outs),
        scratch_shapes=[pltpu.VMEM(s, F32) if isinstance(s, tuple) else s for s in scratch],
        cost_estimate=pl.CostEstimate(
            flops=0, bytes_accessed=int(us * 3_000_000), transcendentals=0
        ),
        compiler_params=pltpu.CompilerParams(vmem_limit_bytes=(60 if hbm else 32) * 1024 * 1024),
    )(*args)


def shifted(block, axis, by):
    count = lax.axis_size(axis)
    return lax.ppermute(block, axis, [(i, (i + by) % count) for i in range(count)])


def swapped(block, axis, odd):
    count = lax.axis_size(axis)
    pairs = [(i, (i + (1 if (i + odd) % 2 == 0 else -1)) % count) for i in range(count)]
    return lax.ppermute(block, axis, pairs)


def swap_columns(left, right):
    return shifted(right, "span", 1), shifted(left, "span", -1)


def on_device(current, previous, moduli, density, traces, receivers, owners, offsets):
    wide = (3, CR, ROWS, CE)
    edge = (11, 2, 8, CE)
    layer, columns = (3, ROWS, CE), [(8, CE), (8, CE)]

    fields = (current, previous, moduli, density.reshape((1,) + density.shape))
    rooms = [(11, CR, 8, CE), pltpu.SemaphoreType.DMA((4,))]
    (high_rows,) = call(high_kernel, [edge], fields, scratch=rooms, hbm=4)
    from_low = shifted(high_rows, "lat", 1)
    packed, low_rows = call(
        pack_kernel,
        [(64, 1, 256), edge],
        (
            offsets.reshape(1, 128),
            receivers.reshape(1, 128),
            owners.reshape(1, 128),
            traces.transpose(1, 0, 2),
        )
        + fields,
        scratch=rooms
        + [
            (3, STATIONS, 512),
            pltpu.VMEM((8, 128), I32),
            pltpu.SemaphoreType.DMA(()),
            pltpu.SemaphoreType.DMA((3,)),
        ],
        hbm=8,
        us=2.0,
    )
    from_high = shifted(low_rows, "lat", -1)
    got = lax.all_to_all(packed, ("lat", "rad"), 0, 0, tiled=True)

    u, v, m, c, even, odd, *ends = call(
        widen_kernel,
        [wide, wide, (4, CR, ROWS, CE), (CR, ROWS, CE)]
        + [(5, ROWS, CE), (5, ROWS, CE), (8, CE), (8, CE)],
        (current, previous, moduli, density, from_low, from_high),
    )
    *coefficients, free = call(
        prepare_kernel,
        [(2, CR + 1, ROWS, CE), wide, wide, wide, wide],
        (u, v, m, c, swapped(even, "rad", 0), swapped(odd, "rad", 1), *swap_columns(*ends)),
    )
    cells, lanes = CR * ROWS, 3 * SLOTS * 128
    first, even, odd, *ends = call(
        first_kernel,
        [wide, layer, layer] + columns,
        (got, free, c),
        scratch=[(3 * cells, lanes), (CE, lanes)],
    )
    (sources,) = call(
        sources_kernel,
        [(STEPS - 1,) + wide],
        (got, c),
        scratch=[(3 * (STEPS - 1) * cells, lanes), (CE, lanes)],
        us=3.0,
    )
    odd = swapped(odd, "rad", 1)
    v, u = u, first
    for t in range(1, STEPS):
        even = swapped(even, "rad", 0)
        at_left, at_right = swap_columns(*ends)
        if t == STEPS - 1:
            ar, al, au, ad = coefficients
            own = (3, CR, CL, CE)
            base, before_final = call(base_kernel, [own, own], (u, v, c, sources, ar, al))
            (made,) = call(end_kernel, [(3, CL, CE)], (u, c, odd, ar), us=0.3)
            (final,) = call(
                last_kernel, [own], (u, c, base, even, made, at_left, at_right, ar, au, ad)
            )
            return final, before_final
        before = (u, v, c, sources)
        after = (at_left, at_right, *coefficients)

        def lead(*refs, t=t):
            lead_kernel(t, *refs)

        def step(*refs, t=t):
            step_kernel(t, *refs)

        (made,) = call(lead, [layer], before + (odd,) + after)
        next_odd = swapped(made, "rad", 1)
        following, even, *ends = call(
            step, [wide, layer] + columns, before + (even, odd) + after + (made,)
        )
        v, u, odd = u, following, next_odd


def solution(mesh):
    in_specs = (
        P(None, "rad", "lat", "span"),
        P(None, "rad", "lat", "span"),
        P(None, "rad", "lat", "span"),
        P("rad", "lat", "span"),
        P(("span", "lat", "rad"), None, None),
        P(("span", "lat", "rad")),
        P(("span", "lat", "rad"), None),
        P(("span", "lat", "rad")),
    )
    out_specs = (P(None, "rad", "lat", "span"), P(None, "rad", "lat", "span"))
    return jax.shard_map(
        on_device, mesh=mesh, in_specs=in_specs, out_specs=out_specs, check_vma=False
    )
```

```python
import jax
import jax.numpy as jnp
from jax import lax
from jax.experimental import pallas as pl
from jax.experimental.pallas import tpu as pltpu
from jax.sharding import PartitionSpec as P

STEPS = 4
STEP_SQUARE = 0.16
TABLE = ((0, 2, 2), (2, 1, 3), (2, 3, 1))
CR, CL, CE = 4, 16, 128
HALO = 4
ROWS = CL + 2 * HALO
CAP = 4
SLOTS = 6
STATIONS = 128
F32 = jnp.float32
I32 = jnp.int32


def iota(shape, dim):
    return lax.broadcasted_iota(I32, shape, dim)


def fold(tiles, at):
    lane, sub = iota((8, 128), 1), iota((8, 128), 0)
    rows = []
    for start in range(0, len(tiles), 16):
        gathered = jnp.zeros((8, 128), F32)
        for i, tile in enumerate(tiles[start : start + 16]):
            column = jnp.broadcast_to(tile[:, at : at + 1], (8, 128))
            gathered = jnp.where(lane == i * 8 + sub, column, gathered)
        rows.append(jnp.sum(gathered, axis=0, keepdims=True))
    return rows


def unfold(ref, first_row, tile):
    row = first_row + tile // 16
    spread = jnp.broadcast_to(ref[pl.ds(row, 1), :], (8, 128))
    return jnp.take_along_axis(spread, (tile % 16) * 8 + iota((8, 128), 0), axis=1)


def column(ref, first_row, k, r):
    first = (k * CR + r) * (ROWS // 8)
    return jnp.concatenate([unfold(ref, first_row, first + i) for i in range(ROWS // 8)], axis=0)


def tiles_of(ref, count, first=0):
    return [
        ref[first + k, r, 8 * i : 8 * i + 8, :]
        for k in range(count)
        for r in range(CR)
        for i in range(ROWS // 8)
    ]


def put_columns(tiles, left_ref, right_ref, first_row):
    for ref, at in ((left_ref, 0), (right_ref, CE - 1)):
        for i, row in enumerate(fold(tiles, at)):
            ref[first_row + i : first_row + i + 1, :] = row


def rad_is_even():
    return lax.axis_index("rad") % 2 == 0


def end_layers():
    lead = jnp.where(rad_is_even(), 0, CR - 1)
    return lead, CR - 1 - lead


def keep_lead(u_ref, made):
    lead, _ = end_layers()
    for k in range(3):
        u_ref[k, lead] = made[k]


def put_rest(u_ref, even_ref, left_ref, right_ref):
    _, rest = end_layers()
    for k in range(3):
        even_ref[k] = u_ref[k, rest]
    left_ref[...] = jnp.zeros_like(left_ref)
    right_ref[...] = jnp.zeros_like(right_ref)
    put_columns(tiles_of(u_ref, 3), left_ref, right_ref, 0)


def edge_rows(start, fields, out, room, sems):
    first, copies = 0, []
    for i, ref in enumerate(fields):
        count = ref.shape[0]
        copies.append(
            pltpu.make_async_copy(
                ref.at[:, :, pl.ds(start, 8), :], room.at[pl.ds(first, count)], sems.at[i]
            )
        )
        first += count
    for copy in copies:
        copy.start()

    def finish():
        for copy in copies:
            copy.wait()
        inner = slice(0, HALO) if start == 0 else slice(8 - HALO, 8)
        for f in range(first):
            for r in range(CR):
                spot = slice(HALO * (r % 2), HALO * (r % 2) + HALO)
                out[f, r // 2, spot, :] = room[f, r, inner, :]

    return finish


def high_kernel(cur, prv, mod, den, high, room, sems):
    edge_rows(CL - 8, (cur, prv, mod, den), high, room, sems)()


def pack_kernel(
    offsets_in, receivers_in, owners_in, traces_in, cur, prv, mod, den, out, low,
    room, sems, traces, words_in, trace_sem, word_sems,
):
    copy = pltpu.make_async_copy(traces_in, traces, trace_sem)
    copy.start()
    small = [
        pltpu.make_async_copy(ref, words_in.at[pl.ds(i, 1)], word_sems.at[i])
        for i, ref in enumerate((offsets_in, receivers_in, owners_in))
    ]
    for one in small:
        one.start()
    finish_low = edge_rows(0, (cur, prv, mod, den), low, room, sems)
    for one in small:
        one.wait()
    offset_row, q, owner_row = words_in[0:1], words_in[1:2], words_in[2:3]
    r, l, e = q // 2048, (q // 128) % CL, q % 128
    wide_sub, wide_lane = iota((128, 128), 0), iota((128, 128), 1)
    sheet = jnp.transpose(
        jnp.concatenate(
            [owner_row.astype(F32), offset_row.astype(F32), jnp.zeros((6, 128), F32)], axis=0
        )
    )
    owner_cols = jnp.broadcast_to(sheet[:, 0:1], (128, 128)).astype(I32)
    offsets = jnp.broadcast_to(sheet[:, 1:2], (128, 128)).astype(I32)
    same = (owner_cols == owner_row) & (wide_sub < wide_lane)
    rank = jnp.sum(jnp.where(same, 1.0, 0.0), axis=0, keepdims=True).astype(I32)

    lefts, lines = [], [e.astype(F32)]
    for shift in (-1, 0, 1):
        slot = (shift + 1) * CAP + rank
        half, j = slot // SLOTS, slot % SLOTS
        if shift == 0:
            row, near = l, l >= 0
        elif shift == -1:
            row, near = CL + l, l <= HALO - 2
        else:
            row, near = l + HALO + HALO, l >= CL - HALO + 1
        target = owner_row + 8 * shift
        ok = near & (target >= 0) & (target < 64)
        place = jnp.where(ok, half * 64 + target, -1)
        lefts.append(jnp.where(wide_sub == place, 1.0, 0.0))
        lines += [j.astype(F32), (r * ROWS + row).astype(F32)]
    sheet = jnp.transpose(jnp.concatenate(lines + [jnp.zeros((1, 128), F32)], axis=0))
    finish_low()

    inside = offsets % 128
    tile = offsets // 128 + jnp.where(wide_lane < inside, 1, 0)
    index = (inside + (wide_lane // 8) % STEPS) % 128
    copy.wait()
    window = jnp.broadcast_to(sheet[:, 0:1], (128, 128))
    for k in range(3):
        parts = [traces[k, :, 128 * i : 128 * i + 128] for i in range(4)]
        merged = jnp.where(
            tile == 0,
            parts[0],
            jnp.where(tile == 1, parts[1], jnp.where(tile == 2, parts[2], parts[3])),
        )
        picked = jnp.take_along_axis(merged, index, axis=1)
        window = jnp.where(wide_lane // 32 == k, picked, window)
    rights = []
    for i in range(3):
        slots = jnp.broadcast_to(sheet[:, 2 * i + 1 : 2 * i + 2], (128, 128)).astype(I32)
        cells = jnp.broadcast_to(sheet[:, 2 * i + 2 : 2 * i + 3], (128, 128))
        words = jnp.where((wide_lane >= 96) & (wide_lane < 104), cells, window)
        rights.append(jnp.where((wide_lane % 8 == slots) & (wide_lane < 112), words, 0.0))
    packed = lax.dot_general(
        jnp.concatenate(lefts, axis=1),
        jnp.concatenate(rights, axis=0),
        (((1,), (0,)), ((), ())),
        precision=lax.Precision.HIGHEST,
        preferred_element_type=F32,
    )
    out[:, 0, :128] = packed[:64]
    out[:, 0, 128:] = packed[64:]


def widen_kernel(
    cur, prv, mod, den, from_low, from_high, u, v, m, c, even, odd, left, right
):
    lat = lax.axis_index("lat")
    has_low, has_high = lat > 0, lat < lax.axis_size("lat") - 1

    def ghosts(f, r):
        spot = slice(HALO * (r % 2), HALO * (r % 2) + HALO)
        return jnp.concatenate(
            [
                jnp.where(has_high, from_high[f, r // 2, spot, :], 0.0),
                jnp.where(has_low, from_low[f, r // 2, spot, :], 0.0),
            ],
            axis=0,
        )

    for r in range(CR):
        for k in range(3):
            u[k, r, 0:CL, :] = cur[k, r]
            u[k, r, CL:ROWS, :] = ghosts(k, r)
            v[k, r, 0:CL, :] = prv[k, r]
            v[k, r, CL:ROWS, :] = ghosts(3 + k, r)
        for j in range(4):
            m[j, r, 0:CL, :] = mod[j, r]
            m[j, r, CL:ROWS, :] = ghosts(6 + j, r)
        c[r, 0:CL, :] = STEP_SQUARE / den[r]
        spot = slice(HALO * (r % 2), HALO * (r % 2) + HALO)
        outer = STEP_SQUARE / jnp.concatenate(
            [from_high[10, r // 2, spot, :], from_low[10, r // 2, spot, :]], axis=0
        )
        present = jnp.where(iota((8, 128), 0) < HALO, has_high.astype(I32), has_low.astype(I32))
        c[r, CL:ROWS, :] = jnp.where(present > 0, outer, 0.0)
    lead, rest = end_layers()
    for i, (field, k) in enumerate(((u, 0), (u, 1), (u, 2), (m, 0), (m, 2))):
        even[i] = field[k, rest]
        odd[i] = field[k, lead]
    left[...] = jnp.zeros_like(left)
    right[...] = jnp.zeros_like(right)
    put_columns(tiles_of(u, 3), left, right, 0)
    put_columns(tiles_of(m, 3, 1), left, right, 3)


def level(k, r, here, at_left, at_right, al, au, ad):
    _, jl, je = TABLE[k]
    flux = al[jl - 1, r] * (pltpu.roll(here, ROWS - 1, 0) - here)
    total = flux - pltpu.roll(flux, 1, 0)
    lane = iota((ROWS, CE), 1)
    after = jnp.where(lane == CE - 1, column(at_right, 0, k, r), pltpu.roll(here, CE - 1, 1))
    before = jnp.where(lane == 0, column(at_left, 0, k, r), pltpu.roll(here, 1, 1))
    return total + (au[je - 1, r] * (after - here) + ad[je - 1, r] * (before - here))


def force(k, r, u, low, high, at_left, at_right, ar, al, au, ad):
    i, here = TABLE[k][0] // 2, u[k, r]
    below = u[k, r - 1] if r > 0 else low[k]
    above = u[k, r + 1] if r < CR - 1 else high[k]
    total = ar[i, r + 1] * (above - here) - ar[i, r] * (here - below)
    return total + level(k, r, here, at_left, at_right, al, au, ad)


def radial_ends(even, odd, count):
    rad, is_even = lax.axis_index("rad"), rad_is_even()
    lows, highs = [], []
    for k in range(count):
        low = jnp.where(is_even, odd[k], even[k])
        high = jnp.where(is_even, even[k], odd[k])
        lows.append(jnp.where(rad > 0, low, 0.0))
        highs.append(jnp.where(rad < lax.axis_size("rad") - 1, high, 0.0))
    return lows, highs


def joined_kernel(odd, out):
    rad = lax.axis_index("rad")
    joined = jnp.where(rad_is_even(), rad > 0, rad < lax.axis_size("rad") - 1)
    for k in range(odd.shape[0]):
        out[k] = jnp.where(joined, odd[k], 0.0)


def prepare_kernel(u, v, m, c, even, odd, at_left, at_right, ar, al, au, ad, following):
    lows, highs = radial_ends(even, odd, 5)
    lane = iota((ROWS, CE), 1)
    for i, j in enumerate((0, 2)):
        layers = [lows[3 + i]] + [m[j, r] for r in range(CR)] + [highs[3 + i]]
        for face in range(CR + 1):
            ar[i, face] = 0.5 * (layers[face] + layers[face + 1])
    for j in (1, 2, 3):
        for r in range(CR):
            here = m[j, r]
            al[j - 1, r] = 0.5 * (here + pltpu.roll(here, ROWS - 1, 0))
            after = jnp.where(
                lane == CE - 1, column(at_right, 3, j - 1, r), pltpu.roll(here, CE - 1, 1)
            )
            before = jnp.where(lane == 0, column(at_left, 3, j - 1, r), pltpu.roll(here, 1, 1))
            au[j - 1, r] = 0.5 * (here + after)
            ad[j - 1, r] = 0.5 * (here + before)
    for k in range(3):
        for r in range(CR):
            total = force(k, r, u, lows, highs, at_left, at_right, ar, al, au, ad)
            following[k, r] = 2.0 * u[k, r] - v[k, r] + c[r] * total


def thirds(x):
    high = x.astype(jnp.bfloat16).astype(F32)
    rest = x - high
    middle = rest.astype(jnp.bfloat16).astype(F32)
    return high, middle, rest - middle


def gather_sources(steps, got, weights, picks, layer=0, layers=CR):
    turned = jnp.transpose(jnp.concatenate([got[:, 0, :128], got[:, 0, 128:]], axis=0))
    parts = thirds(turned)
    cells = layers * ROWS
    cell_rows, cell_lanes = iota((cells, 128), 0) + layer * ROWS, iota((CE, 128), 0)
    for j in range(SLOTS):
        place = turned[96 + j : 97 + j].astype(I32)
        around = turned[104 + j : 105 + j].astype(I32)
        pick = jnp.where(cell_lanes == around, 1.0, 0.0)
        here = cell_rows == place
        for p in range(3):
            span = slice((p * SLOTS + j) * 128, (p * SLOTS + j + 1) * 128)
            picks[:, span] = pick
            for i, t in enumerate(steps):
                for k in range(3):
                    line = (k * STEPS + t) * 8 + j
                    at = (i * 3 + k) * cells
                    weights[at : at + cells, span] = jnp.where(
                        here, parts[p][line : line + 1], 0.0
                    )
    return lax.dot_general(
        weights[...], picks[...], (((1,), (1,)), ((), ())), preferred_element_type=F32
    )


def first_kernel(got, free, c, first, even, odd, left, right, weights, picks):
    summed = gather_sources((0,), got, weights, picks)
    for k in range(3):
        for r in range(CR):
            at = (k * CR + r) * ROWS
            first[k, r] = free[k, r] + summed[at : at + ROWS] * c[r]
    lead, _ = end_layers()
    for k in range(3):
        odd[k] = first[k, lead]
    put_rest(first, even, left, right)


def sources_kernel(got, c, sources, weights, picks):
    summed = gather_sources(range(1, STEPS), got, weights, picks)
    for t in range(STEPS - 1):
        for k in range(3):
            for r in range(CR):
                at = ((t * 3 + k) * CR + r) * ROWS
                sources[t, k, r] = summed[at : at + ROWS] * c[r]


def lead_kernel(t, u, v, c, sources, odd, at_left, at_right, ar, al, au, ad, out):
    lead, _ = end_layers()
    rad, downwards = lax.axis_index("rad"), rad_is_even()
    joined = jnp.where(downwards, rad > 0, rad < lax.axis_size("rad") - 1)
    inner = jnp.where(downwards, 1, CR - 2)
    outer_face, inner_face = jnp.where(downwards, 0, CR), jnp.where(downwards, 1, CR - 1)
    for k in range(3):
        i, here = TABLE[k][0] // 2, u[k, lead]
        outer = jnp.where(joined, odd[k], 0.0)
        total = ar[i, outer_face] * (outer - here) + ar[i, inner_face] * (u[k, inner] - here)
        total = total + level(k, lead, here, at_left, at_right, al, au, ad)
        out[k] = 2.0 * here - v[k, lead] + c[lead] * total + sources[t - 1, k, lead]


def step_kernel(
    t, u, v, c, sources, even, odd, at_left, at_right, ar, al, au, ad, made, following, *rest
):
    lows, highs = radial_ends(even, odd, 3)
    for k in range(3):
        for r in range(CR):
            total = force(k, r, u, lows, highs, at_left, at_right, ar, al, au, ad)
            following[k, r] = 2.0 * u[k, r] - v[k, r] + c[r] * total + sources[t - 1, k, r]
    keep_lead(following, made)
    put_rest(following, *rest)


def last_kernel(
    u, v, c, sources, even, odd, at_left, at_right, ar, al, au, ad, made, final, before_final
):
    lows, highs = radial_ends(even, odd, 3)
    for k in range(3):
        for r in range(CR):
            total = force(k, r, u, lows, highs, at_left, at_right, ar, al, au, ad)
            value = 2.0 * u[k, r] - v[k, r] + c[r] * total + sources[STEPS - 2, k, r]
            final[k, r] = value[:CL]
            before_final[k, r] = u[k, r, 0:CL, :]
    lead, _ = end_layers()
    for k in range(3):
        final[k, lead] = made[k, 0:CL, :]


def call(kernel, outs, args, scratch=(), hbm=0, us=1.0):
    vmem = pl.BlockSpec(memory_space=pltpu.VMEM)
    specs = [pl.BlockSpec(memory_space=pltpu.HBM)] * hbm + [vmem] * (len(args) - hbm)
    return pl.pallas_call(
        kernel,
        out_shape=[jax.ShapeDtypeStruct(shape, F32) for shape in outs],
        in_specs=specs,
        out_specs=[vmem] * len(outs),
        scratch_shapes=[pltpu.VMEM(s, F32) if isinstance(s, tuple) else s for s in scratch],
        cost_estimate=pl.CostEstimate(
            flops=0, bytes_accessed=int(us * 3_000_000), transcendentals=0
        ),
        compiler_params=pltpu.CompilerParams(vmem_limit_bytes=(60 if hbm else 32) * 1024 * 1024),
    )(*args)


def shifted(block, axis, by):
    count = lax.axis_size(axis)
    return lax.ppermute(block, axis, [(i, (i + by) % count) for i in range(count)])


def swapped(block, axis, odd):
    count = lax.axis_size(axis)
    pairs = [(i, (i + (1 if (i + odd) % 2 == 0 else -1)) % count) for i in range(count)]
    return lax.ppermute(block, axis, pairs)


def swap_columns(left, right):
    return shifted(right, "span", 1), shifted(left, "span", -1)


def on_device(current, previous, moduli, density, traces, receivers, owners, offsets):
    wide = (3, CR, ROWS, CE)
    edge = (11, 2, 8, CE)
    layer, columns = (3, ROWS, CE), [(8, CE), (8, CE)]

    fields = (current, previous, moduli, density.reshape((1,) + density.shape))
    rooms = [(11, CR, 8, CE), pltpu.SemaphoreType.DMA((4,))]
    (high_rows,) = call(high_kernel, [edge], fields, scratch=rooms, hbm=4)
    from_low = shifted(high_rows, "lat", 1)
    packed, low_rows = call(
        pack_kernel,
        [(64, 1, 256), edge],
        (
            offsets.reshape(1, 128),
            receivers.reshape(1, 128),
            owners.reshape(1, 128),
            traces.transpose(1, 0, 2),
        )
        + fields,
        scratch=rooms
        + [
            (3, STATIONS, 512),
            pltpu.VMEM((8, 128), I32),
            pltpu.SemaphoreType.DMA(()),
            pltpu.SemaphoreType.DMA((3,)),
        ],
        hbm=8,
        us=2.0,
    )
    from_high = shifted(low_rows, "lat", -1)
    got = lax.all_to_all(packed, ("lat", "rad"), 0, 0, tiled=True)

    u, v, m, c, even, odd, *ends = call(
        widen_kernel,
        [wide, wide, (4, CR, ROWS, CE), (CR, ROWS, CE)]
        + [(5, ROWS, CE), (5, ROWS, CE), (8, CE), (8, CE)],
        (current, previous, moduli, density, from_low, from_high),
    )
    even, odd = swapped(even, "rad", 0), swapped(odd, "rad", 1)
    (odd,) = call(joined_kernel, [(5, ROWS, CE)], (odd,), us=0.3)
    *coefficients, free = call(
        prepare_kernel,
        [(2, CR + 1, ROWS, CE), wide, wide, wide, wide],
        (u, v, m, c, even, odd, *swap_columns(*ends)),
    )
    cells, lanes = CR * ROWS, 3 * SLOTS * 128
    first, even, odd, *ends = call(
        first_kernel,
        [wide, layer, layer] + columns,
        (got, free, c),
        scratch=[(3 * cells, lanes), (CE, lanes)],
    )
    (sources,) = call(
        sources_kernel,
        [(STEPS - 1,) + wide],
        (got, c),
        scratch=[(3 * (STEPS - 1) * cells, lanes), (CE, lanes)],
        us=3.0,
    )
    odd = swapped(odd, "rad", 1)
    v, u = u, first
    for t in range(1, STEPS):
        even = swapped(even, "rad", 0)
        at_left, at_right = swap_columns(*ends)
        before = (u, v, c, sources)
        after = (at_left, at_right, *coefficients)

        def lead(*refs, t=t):
            lead_kernel(t, *refs)

        def step(*refs, t=t):
            step_kernel(t, *refs)

        (made,) = call(lead, [layer], before + (odd,) + after)
        if t == STEPS - 1:
            args = before + (even, odd) + after + (made,)
            return tuple(call(last_kernel, [(3, CR, CL, CE)] * 2, args))
        next_odd = swapped(made, "rad", 1)
        following, even, *ends = call(
            step, [wide, layer] + columns, before + (even, odd) + after + (made,)
        )
        v, u, odd = u, following, next_odd


def solution(mesh):
    in_specs = (
        P(None, "rad", "lat", "span"),
        P(None, "rad", "lat", "span"),
        P(None, "rad", "lat", "span"),
        P("rad", "lat", "span"),
        P(("span", "lat", "rad"), None, None),
        P(("span", "lat", "rad")),
        P(("span", "lat", "rad"), None),
        P(("span", "lat", "rad")),
    )
    out_specs = (P(None, "rad", "lat", "span"), P(None, "rad", "lat", "span"))
    return jax.shard_map(
        on_device, mesh=mesh, in_specs=in_specs, out_specs=out_specs, check_vma=False
    )
```

```python
import jax
import jax.numpy as jnp
from jax import lax
from jax.experimental import pallas as pl
from jax.experimental.pallas import tpu as pltpu
from jax.sharding import PartitionSpec as P

STEPS = 4
STEP_SQUARE = 0.16
TABLE = ((0, 2, 2), (2, 1, 3), (2, 3, 1))
CR, CL, CE = 4, 16, 128
HALO = 4
ROWS = CL + 2 * HALO
CAP = 4
SLOTS = 6
STATIONS = 128
F32 = jnp.float32
I32 = jnp.int32


def iota(shape, dim):
    return lax.broadcasted_iota(I32, shape, dim)


def fold(tiles, at):
    lane, sub = iota((8, 128), 1), iota((8, 128), 0)
    rows = []
    for start in range(0, len(tiles), 16):
        gathered = jnp.zeros((8, 128), F32)
        for i, tile in enumerate(tiles[start : start + 16]):
            column = jnp.broadcast_to(tile[:, at : at + 1], (8, 128))
            gathered = jnp.where(lane == i * 8 + sub, column, gathered)
        rows.append(jnp.sum(gathered, axis=0, keepdims=True))
    return rows


def unfold(ref, first_row, tile):
    row = first_row + tile // 16
    spread = jnp.broadcast_to(ref[pl.ds(row, 1), :], (8, 128))
    return jnp.take_along_axis(spread, (tile % 16) * 8 + iota((8, 128), 0), axis=1)


def column(ref, first_row, k, r):
    first = (k * CR + r) * (ROWS // 8)
    return jnp.concatenate([unfold(ref, first_row, first + i) for i in range(ROWS // 8)], axis=0)


def tiles_of(ref, count, first=0):
    return [
        ref[first + k, r, 8 * i : 8 * i + 8, :]
        for k in range(count)
        for r in range(CR)
        for i in range(ROWS // 8)
    ]


def put_columns(tiles, left_ref, right_ref, first_row):
    for ref, at in ((left_ref, 0), (right_ref, CE - 1)):
        for i, row in enumerate(fold(tiles, at)):
            ref[first_row + i : first_row + i + 1, :] = row


def rad_is_even():
    return lax.axis_index("rad") % 2 == 0


def end_layers():
    lead = jnp.where(rad_is_even(), 0, CR - 1)
    return lead, CR - 1 - lead


def whole(layer):
    if layer.shape[0] == ROWS:
        return layer
    return jnp.concatenate([layer, jnp.zeros((ROWS - layer.shape[0], CE), F32)], axis=0)


def keep_lead(u_ref, made):
    lead, _ = end_layers()
    for k in range(3):
        u_ref[k, lead, : made.shape[1], :] = made[k]


def put_rest(u_ref, even_ref, left_ref, right_ref):
    _, rest = end_layers()
    for k in range(3):
        even_ref[k] = u_ref[k, rest, : even_ref.shape[1], :]
    left_ref[...] = jnp.zeros_like(left_ref)
    right_ref[...] = jnp.zeros_like(right_ref)
    put_columns(tiles_of(u_ref, 3), left_ref, right_ref, 0)


def edge_rows(start, fields, out, room, sems):
    first, copies = 0, []
    for i, ref in enumerate(fields):
        count = ref.shape[0]
        copies.append(
            pltpu.make_async_copy(
                ref.at[:, :, pl.ds(start, 8), :], room.at[pl.ds(first, count)], sems.at[i]
            )
        )
        first += count
    for copy in copies:
        copy.start()

    def finish():
        for copy in copies:
            copy.wait()
        inner = slice(0, HALO) if start == 0 else slice(8 - HALO, 8)
        for f in range(first):
            for r in range(CR):
                spot = slice(HALO * (r % 2), HALO * (r % 2) + HALO)
                out[f, r // 2, spot, :] = room[f, r, inner, :]

    return finish


def high_kernel(cur, prv, mod, den, high, room, sems):
    edge_rows(CL - 8, (cur, prv, mod, den), high, room, sems)()


def pack_kernel(
    offsets_in, receivers_in, owners_in, traces_in, cur, prv, mod, den, out, low,
    room, sems, traces, words_in, trace_sem, word_sems,
):
    copy = pltpu.make_async_copy(traces_in, traces, trace_sem)
    copy.start()
    small = [
        pltpu.make_async_copy(ref, words_in.at[pl.ds(i, 1)], word_sems.at[i])
        for i, ref in enumerate((offsets_in, receivers_in, owners_in))
    ]
    for one in small:
        one.start()
    finish_low = edge_rows(0, (cur, prv, mod, den), low, room, sems)
    for one in small:
        one.wait()
    offset_row, q, owner_row = words_in[0:1], words_in[1:2], words_in[2:3]
    r, l, e = q // 2048, (q // 128) % CL, q % 128
    wide_sub, wide_lane = iota((128, 128), 0), iota((128, 128), 1)
    sheet = jnp.transpose(
        jnp.concatenate(
            [owner_row.astype(F32), offset_row.astype(F32), jnp.zeros((6, 128), F32)], axis=0
        )
    )
    owner_cols = jnp.broadcast_to(sheet[:, 0:1], (128, 128)).astype(I32)
    offsets = jnp.broadcast_to(sheet[:, 1:2], (128, 128)).astype(I32)
    same = (owner_cols == owner_row) & (wide_sub < wide_lane)
    rank = jnp.sum(jnp.where(same, 1.0, 0.0), axis=0, keepdims=True).astype(I32)

    lefts, lines = [], [e.astype(F32)]
    for shift in (-1, 0, 1):
        slot = (shift + 1) * CAP + rank
        half, j = slot // SLOTS, slot % SLOTS
        if shift == 0:
            row, near = l, l >= 0
        elif shift == -1:
            row, near = CL + l, l <= HALO - 2
        else:
            row, near = l + HALO + HALO, l >= CL - HALO + 1
        target = owner_row + 8 * shift
        ok = near & (target >= 0) & (target < 64)
        place = jnp.where(ok, half * 64 + target, -1)
        lefts.append(jnp.where(wide_sub == place, 1.0, 0.0))
        lines += [j.astype(F32), (r * ROWS + row).astype(F32)]
    sheet = jnp.transpose(jnp.concatenate(lines + [jnp.zeros((1, 128), F32)], axis=0))
    finish_low()

    inside = offsets % 128
    tile = offsets // 128 + jnp.where(wide_lane < inside, 1, 0)
    index = (inside + (wide_lane // 8) % STEPS) % 128
    copy.wait()
    window = jnp.broadcast_to(sheet[:, 0:1], (128, 128))
    for k in range(3):
        parts = [traces[k, :, 128 * i : 128 * i + 128] for i in range(4)]
        merged = jnp.where(
            tile == 0,
            parts[0],
            jnp.where(tile == 1, parts[1], jnp.where(tile == 2, parts[2], parts[3])),
        )
        picked = jnp.take_along_axis(merged, index, axis=1)
        window = jnp.where(wide_lane // 32 == k, picked, window)
    rights = []
    for i in range(3):
        slots = jnp.broadcast_to(sheet[:, 2 * i + 1 : 2 * i + 2], (128, 128)).astype(I32)
        cells = jnp.broadcast_to(sheet[:, 2 * i + 2 : 2 * i + 3], (128, 128))
        words = jnp.where((wide_lane >= 96) & (wide_lane < 104), cells, window)
        rights.append(jnp.where((wide_lane % 8 == slots) & (wide_lane < 112), words, 0.0))
    packed = lax.dot_general(
        jnp.concatenate(lefts, axis=1),
        jnp.concatenate(rights, axis=0),
        (((1,), (0,)), ((), ())),
        precision=lax.Precision.HIGHEST,
        preferred_element_type=F32,
    )
    out[:, 0, :128] = packed[:64]
    out[:, 0, 128:] = packed[64:]


def widen_kernel(
    cur, prv, mod, den, from_low, from_high, u, v, m, c, even, odd, left, right
):
    lat = lax.axis_index("lat")
    has_low, has_high = lat > 0, lat < lax.axis_size("lat") - 1

    def ghosts(f, r):
        spot = slice(HALO * (r % 2), HALO * (r % 2) + HALO)
        return jnp.concatenate(
            [
                jnp.where(has_high, from_high[f, r // 2, spot, :], 0.0),
                jnp.where(has_low, from_low[f, r // 2, spot, :], 0.0),
            ],
            axis=0,
        )

    for r in range(CR):
        for k in range(3):
            u[k, r, 0:CL, :] = cur[k, r]
            u[k, r, CL:ROWS, :] = ghosts(k, r)
            v[k, r, 0:CL, :] = prv[k, r]
            v[k, r, CL:ROWS, :] = ghosts(3 + k, r)
        for j in range(4):
            m[j, r, 0:CL, :] = mod[j, r]
            m[j, r, CL:ROWS, :] = ghosts(6 + j, r)
        c[r, 0:CL, :] = STEP_SQUARE / den[r]
        spot = slice(HALO * (r % 2), HALO * (r % 2) + HALO)
        outer = STEP_SQUARE / jnp.concatenate(
            [from_high[10, r // 2, spot, :], from_low[10, r // 2, spot, :]], axis=0
        )
        present = jnp.where(iota((8, 128), 0) < HALO, has_high.astype(I32), has_low.astype(I32))
        c[r, CL:ROWS, :] = jnp.where(present > 0, outer, 0.0)
    lead, rest = end_layers()
    for i, (field, k) in enumerate(((u, 0), (u, 1), (u, 2), (m, 0), (m, 2))):
        even[i] = field[k, rest]
        odd[i] = field[k, lead]
    left[...] = jnp.zeros_like(left)
    right[...] = jnp.zeros_like(right)
    put_columns(tiles_of(u, 3), left, right, 0)
    put_columns(tiles_of(m, 3, 1), left, right, 3)


def level(k, r, here, at_left, at_right, al, au, ad):
    _, jl, je = TABLE[k]
    flux = al[jl - 1, r] * (pltpu.roll(here, ROWS - 1, 0) - here)
    total = flux - pltpu.roll(flux, 1, 0)
    lane = iota((ROWS, CE), 1)
    after = jnp.where(lane == CE - 1, column(at_right, 0, k, r), pltpu.roll(here, CE - 1, 1))
    before = jnp.where(lane == 0, column(at_left, 0, k, r), pltpu.roll(here, 1, 1))
    return total + (au[je - 1, r] * (after - here) + ad[je - 1, r] * (before - here))


def force(k, r, u, low, high, at_left, at_right, ar, al, au, ad):
    i, here = TABLE[k][0] // 2, u[k, r]
    below = u[k, r - 1] if r > 0 else low[k]
    above = u[k, r + 1] if r < CR - 1 else high[k]
    total = ar[i, r + 1] * (above - here) - ar[i, r] * (here - below)
    return total + level(k, r, here, at_left, at_right, al, au, ad)


def radial_ends(even, odd, count):
    rad, is_even = lax.axis_index("rad"), rad_is_even()
    lows, highs = [], []
    for k in range(count):
        low = jnp.where(is_even, whole(odd[k]), whole(even[k]))
        high = jnp.where(is_even, whole(even[k]), whole(odd[k]))
        lows.append(jnp.where(rad > 0, low, 0.0))
        highs.append(jnp.where(rad < lax.axis_size("rad") - 1, high, 0.0))
    return lows, highs


def prepare_kernel(u, v, m, c, even, odd, at_left, at_right, ar, al, au, ad, following):
    lows, highs = radial_ends(even, odd, 5)
    lane = iota((ROWS, CE), 1)
    for i, j in enumerate((0, 2)):
        layers = [lows[3 + i]] + [m[j, r] for r in range(CR)] + [highs[3 + i]]
        for face in range(CR + 1):
            ar[i, face] = 0.5 * (layers[face] + layers[face + 1])
    for j in (1, 2, 3):
        for r in range(CR):
            here = m[j, r]
            al[j - 1, r] = 0.5 * (here + pltpu.roll(here, ROWS - 1, 0))
            after = jnp.where(
                lane == CE - 1, column(at_right, 3, j - 1, r), pltpu.roll(here, CE - 1, 1)
            )
            before = jnp.where(lane == 0, column(at_left, 3, j - 1, r), pltpu.roll(here, 1, 1))
            au[j - 1, r] = 0.5 * (here + after)
            ad[j - 1, r] = 0.5 * (here + before)
    for k in range(3):
        for r in range(CR):
            total = force(k, r, u, lows, highs, at_left, at_right, ar, al, au, ad)
            following[k, r] = 2.0 * u[k, r] - v[k, r] + c[r] * total


def thirds(x):
    high = x.astype(jnp.bfloat16).astype(F32)
    rest = x - high
    middle = rest.astype(jnp.bfloat16).astype(F32)
    return high, middle, rest - middle


def gather_sources(steps, got, weights, picks, layer=0, layers=CR):
    turned = jnp.transpose(jnp.concatenate([got[:, 0, :128], got[:, 0, 128:]], axis=0))
    parts = thirds(turned)
    cells = layers * ROWS
    cell_rows, cell_lanes = iota((cells, 128), 0) + layer * ROWS, iota((CE, 128), 0)
    for j in range(SLOTS):
        place = turned[96 + j : 97 + j].astype(I32)
        around = turned[104 + j : 105 + j].astype(I32)
        pick = jnp.where(cell_lanes == around, 1.0, 0.0)
        here = cell_rows == place
        for p in range(3):
            span = slice((p * SLOTS + j) * 128, (p * SLOTS + j + 1) * 128)
            picks[:, span] = pick
            for i, t in enumerate(steps):
                for k in range(3):
                    line = (k * STEPS + t) * 8 + j
                    at = (i * 3 + k) * cells
                    weights[at : at + cells, span] = jnp.where(
                        here, parts[p][line : line + 1], 0.0
                    )
    return lax.dot_general(
        weights[...], picks[...], (((1,), (1,)), ((), ())), preferred_element_type=F32
    )


def first_kernel(got, free, c, first, even, odd, left, right, weights, picks):
    summed = gather_sources((0,), got, weights, picks)
    for k in range(3):
        for r in range(CR):
            at = (k * CR + r) * ROWS
            first[k, r] = free[k, r] + summed[at : at + ROWS] * c[r]
    lead, _ = end_layers()
    for k in range(3):
        odd[k] = first[k, lead]
    put_rest(first, even, left, right)


def sources_kernel(got, c, sources, weights, picks):
    summed = gather_sources(range(1, STEPS), got, weights, picks)
    for t in range(STEPS - 1):
        for k in range(3):
            for r in range(CR):
                at = ((t * 3 + k) * CR + r) * ROWS
                sources[t, k, r] = summed[at : at + ROWS] * c[r]


def lead_kernel(t, u, v, c, sources, odd, at_left, at_right, ar, al, au, ad, out):
    lead, _ = end_layers()
    rad, downwards = lax.axis_index("rad"), rad_is_even()
    joined = jnp.where(downwards, rad > 0, rad < lax.axis_size("rad") - 1)
    inner = jnp.where(downwards, 1, CR - 2)
    outer_face, inner_face = jnp.where(downwards, 0, CR), jnp.where(downwards, 1, CR - 1)
    for k in range(3):
        i, here = TABLE[k][0] // 2, u[k, lead]
        outer = jnp.where(joined, whole(odd[k]), 0.0)
        total = ar[i, outer_face] * (outer - here) + ar[i, inner_face] * (u[k, inner] - here)
        total = total + level(k, lead, here, at_left, at_right, al, au, ad)
        value = 2.0 * here - v[k, lead] + c[lead] * total + sources[t - 1, k, lead]
        out[k] = value[: out.shape[1]]


def step_kernel(
    t, u, v, c, sources, even, odd, at_left, at_right, ar, al, au, ad, made, following, *rest
):
    lows, highs = radial_ends(even, odd, 3)
    for k in range(3):
        for r in range(CR):
            total = force(k, r, u, lows, highs, at_left, at_right, ar, al, au, ad)
            following[k, r] = 2.0 * u[k, r] - v[k, r] + c[r] * total + sources[t - 1, k, r]
    keep_lead(following, made)
    put_rest(following, *rest)


def last_kernel(
    u, v, c, sources, even, odd, at_left, at_right, ar, al, au, ad, made, final, before_final
):
    lows, highs = radial_ends(even, odd, 3)
    for k in range(3):
        for r in range(CR):
            total = force(k, r, u, lows, highs, at_left, at_right, ar, al, au, ad)
            value = 2.0 * u[k, r] - v[k, r] + c[r] * total + sources[STEPS - 2, k, r]
            final[k, r] = value[:CL]
            before_final[k, r] = u[k, r, 0:CL, :]
    lead, _ = end_layers()
    for k in range(3):
        final[k, lead] = made[k, 0:CL, :]


def call(kernel, outs, args, scratch=(), hbm=0, us=1.0):
    vmem = pl.BlockSpec(memory_space=pltpu.VMEM)
    specs = [pl.BlockSpec(memory_space=pltpu.HBM)] * hbm + [vmem] * (len(args) - hbm)
    return pl.pallas_call(
        kernel,
        out_shape=[jax.ShapeDtypeStruct(shape, F32) for shape in outs],
        in_specs=specs,
        out_specs=[vmem] * len(outs),
        scratch_shapes=[pltpu.VMEM(s, F32) if isinstance(s, tuple) else s for s in scratch],
        cost_estimate=pl.CostEstimate(
            flops=0, bytes_accessed=int(us * 3_000_000), transcendentals=0
        ),
        compiler_params=pltpu.CompilerParams(vmem_limit_bytes=(60 if hbm else 32) * 1024 * 1024),
    )(*args)


def shifted(block, axis, by):
    count = lax.axis_size(axis)
    return lax.ppermute(block, axis, [(i, (i + by) % count) for i in range(count)])


def swapped(block, axis, odd):
    count = lax.axis_size(axis)
    pairs = [(i, (i + (1 if (i + odd) % 2 == 0 else -1)) % count) for i in range(count)]
    return lax.ppermute(block, axis, pairs)


def swap_columns(left, right):
    return shifted(right, "span", 1), shifted(left, "span", -1)


def on_device(current, previous, moduli, density, traces, receivers, owners, offsets):
    wide = (3, CR, ROWS, CE)
    edge = (11, 2, 8, CE)
    layer, columns = (3, ROWS, CE), [(8, CE), (8, CE)]

    fields = (current, previous, moduli, density.reshape((1,) + density.shape))
    rooms = [(11, CR, 8, CE), pltpu.SemaphoreType.DMA((4,))]
    (high_rows,) = call(high_kernel, [edge], fields, scratch=rooms, hbm=4)
    from_low = shifted(high_rows, "lat", 1)
    packed, low_rows = call(
        pack_kernel,
        [(64, 1, 256), edge],
        (
            offsets.reshape(1, 128),
            receivers.reshape(1, 128),
            owners.reshape(1, 128),
            traces.transpose(1, 0, 2),
        )
        + fields,
        scratch=rooms
        + [
            (3, STATIONS, 512),
            pltpu.VMEM((8, 128), I32),
            pltpu.SemaphoreType.DMA(()),
            pltpu.SemaphoreType.DMA((3,)),
        ],
        hbm=8,
        us=2.0,
    )
    from_high = shifted(low_rows, "lat", -1)
    got = lax.all_to_all(packed, ("lat", "rad"), 0, 0, tiled=True)

    u, v, m, c, even, odd, *ends = call(
        widen_kernel,
        [wide, wide, (4, CR, ROWS, CE), (CR, ROWS, CE)]
        + [(5, ROWS, CE), (5, ROWS, CE), (8, CE), (8, CE)],
        (current, previous, moduli, density, from_low, from_high),
    )
    *coefficients, free = call(
        prepare_kernel,
        [(2, CR + 1, ROWS, CE), wide, wide, wide, wide],
        (u, v, m, c, swapped(even, "rad", 0), swapped(odd, "rad", 1), *swap_columns(*ends)),
    )
    cells, lanes = CR * ROWS, 3 * SLOTS * 128
    first, even, odd, *ends = call(
        first_kernel,
        [wide, layer, layer] + columns,
        (got, free, c),
        scratch=[(3 * cells, lanes), (CE, lanes)],
    )
    (sources,) = call(
        sources_kernel,
        [(STEPS - 1,) + wide],
        (got, c),
        scratch=[(3 * (STEPS - 1) * cells, lanes), (CE, lanes)],
        us=3.0,
    )
    odd = swapped(odd, "rad", 1)
    v, u = u, first
    for t in range(1, STEPS):
        even = swapped(even, "rad", 0)
        at_left, at_right = swap_columns(*ends)
        before = (u, v, c, sources)
        after = (at_left, at_right, *coefficients)

        def lead(*refs, t=t):
            lead_kernel(t, *refs)

        def step(*refs, t=t):
            step_kernel(t, *refs)

        if t == STEPS - 2:
            layer = (3, CL, CE)
        (made,) = call(lead, [layer], before + (odd,) + after)
        if t == STEPS - 1:
            args = before + (even, odd) + after + (made,)
            return tuple(call(last_kernel, [(3, CR, CL, CE)] * 2, args))
        next_odd = swapped(made, "rad", 1)
        following, even, *ends = call(
            step, [wide, layer] + columns, before + (even, odd) + after + (made,)
        )
        v, u, odd = u, following, next_odd


def solution(mesh):
    in_specs = (
        P(None, "rad", "lat", "span"),
        P(None, "rad", "lat", "span"),
        P(None, "rad", "lat", "span"),
        P("rad", "lat", "span"),
        P(("span", "lat", "rad"), None, None),
        P(("span", "lat", "rad")),
        P(("span", "lat", "rad"), None),
        P(("span", "lat", "rad")),
    )
    out_specs = (P(None, "rad", "lat", "span"), P(None, "rad", "lat", "span"))
    return jax.shard_map(
        on_device, mesh=mesh, in_specs=in_specs, out_specs=out_specs, check_vma=False
    )
```

```python
import jax
import jax.numpy as jnp
from jax import lax
from jax.experimental import pallas as pl
from jax.experimental.pallas import tpu as pltpu
from jax.sharding import PartitionSpec as P

STEPS = 4
STEP_SQUARE = 0.16
TABLE = ((0, 2, 2), (2, 1, 3), (2, 3, 1))
CR, CL, CE = 4, 16, 128
HALO = 4
ROWS = CL + 2 * HALO
CAP = 4
SLOTS = 6
STATIONS = 128
F32 = jnp.float32
I32 = jnp.int32


def iota(shape, dim):
    return lax.broadcasted_iota(I32, shape, dim)


def fold(tiles, at):
    lane, sub = iota((8, 128), 1), iota((8, 128), 0)
    rows = []
    for start in range(0, len(tiles), 16):
        gathered = jnp.zeros((8, 128), F32)
        for i, tile in enumerate(tiles[start : start + 16]):
            column = jnp.broadcast_to(tile[:, at : at + 1], (8, 128))
            gathered = jnp.where(lane == i * 8 + sub, column, gathered)
        rows.append(jnp.sum(gathered, axis=0, keepdims=True))
    return rows


def unfold(ref, first_row, tile):
    row = first_row + tile // 16
    spread = jnp.broadcast_to(ref[pl.ds(row, 1), :], (8, 128))
    return jnp.take_along_axis(spread, (tile % 16) * 8 + iota((8, 128), 0), axis=1)


def column(ref, first_row, k, r):
    first = (k * CR + r) * (ROWS // 8)
    return jnp.concatenate([unfold(ref, first_row, first + i) for i in range(ROWS // 8)], axis=0)


def tiles_of(ref, count, first=0):
    return [
        ref[first + k, r, 8 * i : 8 * i + 8, :]
        for k in range(count)
        for r in range(CR)
        for i in range(ROWS // 8)
    ]


def put_columns(tiles, left_ref, right_ref, first_row):
    for ref, at in ((left_ref, 0), (right_ref, CE - 1)):
        for i, row in enumerate(fold(tiles, at)):
            ref[first_row + i : first_row + i + 1, :] = row


def rad_is_even():
    return lax.axis_index("rad") % 2 == 0


def end_layers():
    lead = jnp.where(rad_is_even(), 0, CR - 1)
    return lead, CR - 1 - lead


def keep_lead(u_ref, made):
    lead, _ = end_layers()
    for k in range(3):
        u_ref[k, lead] = made[k]


def put_rest(u_ref, even_ref, left_ref, right_ref):
    _, rest = end_layers()
    for k in range(3):
        even_ref[k] = u_ref[k, rest]
    left_ref[...] = jnp.zeros_like(left_ref)
    right_ref[...] = jnp.zeros_like(right_ref)
    put_columns(tiles_of(u_ref, 3), left_ref, right_ref, 0)


def edge_rows(start, fields, out, room, sems):
    first, copies = 0, []
    for i, ref in enumerate(fields):
        count = ref.shape[0]
        copies.append(
            pltpu.make_async_copy(
                ref.at[:, :, pl.ds(start, 8), :], room.at[pl.ds(first, count)], sems.at[i]
            )
        )
        first += count
    for copy in copies:
        copy.start()

    def finish():
        for copy in copies:
            copy.wait()
        inner = slice(0, HALO) if start == 0 else slice(8 - HALO, 8)
        for f in range(first):
            for r in range(CR):
                spot = slice(HALO * (r % 2), HALO * (r % 2) + HALO)
                out[f, r // 2, spot, :] = room[f, r, inner, :]

    return finish


def high_kernel(cur, prv, mod, den, high, room, sems):
    edge_rows(CL - 8, (cur, prv, mod, den), high, room, sems)()


def pack_kernel(
    offsets_in, receivers_in, owners_in, traces_in, cur, prv, mod, den, out, low,
    room, sems, traces, words_in, trace_sem, word_sems,
):
    copy = pltpu.make_async_copy(traces_in, traces, trace_sem)
    copy.start()
    small = [
        pltpu.make_async_copy(ref, words_in.at[pl.ds(i, 1)], word_sems.at[i])
        for i, ref in enumerate((offsets_in, receivers_in, owners_in))
    ]
    for one in small:
        one.start()
    finish_low = edge_rows(0, (cur, prv, mod, den), low, room, sems)
    for one in small:
        one.wait()
    offset_row, q, owner_row = words_in[0:1], words_in[1:2], words_in[2:3]
    r, l, e = q // 2048, (q // 128) % CL, q % 128
    wide_sub, wide_lane = iota((128, 128), 0), iota((128, 128), 1)
    sheet = jnp.transpose(
        jnp.concatenate(
            [owner_row.astype(F32), offset_row.astype(F32), jnp.zeros((6, 128), F32)], axis=0
        )
    )
    owner_cols = jnp.broadcast_to(sheet[:, 0:1], (128, 128)).astype(I32)
    offsets = jnp.broadcast_to(sheet[:, 1:2], (128, 128)).astype(I32)
    same = (owner_cols == owner_row) & (wide_sub < wide_lane)
    rank = jnp.sum(jnp.where(same, 1.0, 0.0), axis=0, keepdims=True).astype(I32)

    lefts, lines = [], [e.astype(F32)]
    for shift in (-1, 0, 1):
        slot = (shift + 1) * CAP + rank
        half, j = slot // SLOTS, slot % SLOTS
        if shift == 0:
            row, near = l, l >= 0
        elif shift == -1:
            row, near = CL + l, l <= HALO - 2
        else:
            row, near = l + HALO + HALO, l >= CL - HALO + 1
        target = owner_row + 8 * shift
        ok = near & (target >= 0) & (target < 64)
        place = jnp.where(ok, half * 64 + target, -1)
        lefts.append(jnp.where(wide_sub == place, 1.0, 0.0))
        lines += [j.astype(F32), (r * ROWS + row).astype(F32)]
    sheet = jnp.transpose(jnp.concatenate(lines + [jnp.zeros((1, 128), F32)], axis=0))
    finish_low()

    inside = offsets % 128
    tile = offsets // 128 + jnp.where(wide_lane < inside, 1, 0)
    index = (inside + (wide_lane // 8) % STEPS) % 128
    copy.wait()
    window = jnp.broadcast_to(sheet[:, 0:1], (128, 128))
    for k in range(3):
        parts = [traces[k, :, 128 * i : 128 * i + 128] for i in range(4)]
        merged = jnp.where(
            tile == 0,
            parts[0],
            jnp.where(tile == 1, parts[1], jnp.where(tile == 2, parts[2], parts[3])),
        )
        picked = jnp.take_along_axis(merged, index, axis=1)
        window = jnp.where(wide_lane // 32 == k, picked, window)
    rights = []
    for i in range(3):
        slots = jnp.broadcast_to(sheet[:, 2 * i + 1 : 2 * i + 2], (128, 128)).astype(I32)
        cells = jnp.broadcast_to(sheet[:, 2 * i + 2 : 2 * i + 3], (128, 128))
        words = jnp.where((wide_lane >= 96) & (wide_lane < 104), cells, window)
        rights.append(jnp.where((wide_lane % 8 == slots) & (wide_lane < 112), words, 0.0))
    packed = lax.dot_general(
        jnp.concatenate(lefts, axis=1),
        jnp.concatenate(rights, axis=0),
        (((1,), (0,)), ((), ())),
        precision=lax.Precision.HIGHEST,
        preferred_element_type=F32,
    )
    out[:, 0, :128] = packed[:64]
    out[:, 0, 128:] = packed[64:]


def widen_kernel(
    cur, prv, mod, den, from_low, from_high, u, v, m, c, even, odd, left, right
):
    lat = lax.axis_index("lat")
    has_low, has_high = lat > 0, lat < lax.axis_size("lat") - 1

    def ghosts(f, r):
        spot = slice(HALO * (r % 2), HALO * (r % 2) + HALO)
        return jnp.concatenate(
            [
                jnp.where(has_high, from_high[f, r // 2, spot, :], 0.0),
                jnp.where(has_low, from_low[f, r // 2, spot, :], 0.0),
            ],
            axis=0,
        )

    for r in range(CR):
        for k in range(3):
            u[k, r, 0:CL, :] = cur[k, r]
            u[k, r, CL:ROWS, :] = ghosts(k, r)
            v[k, r, 0:CL, :] = prv[k, r]
            v[k, r, CL:ROWS, :] = ghosts(3 + k, r)
        for j in range(4):
            m[j, r, 0:CL, :] = mod[j, r]
            m[j, r, CL:ROWS, :] = ghosts(6 + j, r)
        c[r, 0:CL, :] = STEP_SQUARE / den[r]
        spot = slice(HALO * (r % 2), HALO * (r % 2) + HALO)
        outer = STEP_SQUARE / jnp.concatenate(
            [from_high[10, r // 2, spot, :], from_low[10, r // 2, spot, :]], axis=0
        )
        present = jnp.where(iota((8, 128), 0) < HALO, has_high.astype(I32), has_low.astype(I32))
        c[r, CL:ROWS, :] = jnp.where(present > 0, outer, 0.0)
    lead, rest = end_layers()
    for i, (field, k) in enumerate(((u, 0), (u, 1), (u, 2), (m, 0), (m, 2))):
        even[i] = field[k, rest]
        odd[i] = field[k, lead]
    left[...] = jnp.zeros_like(left)
    right[...] = jnp.zeros_like(right)
    put_columns(tiles_of(u, 3), left, right, 0)
    put_columns(tiles_of(m, 3, 1), left, right, 3)


def level(k, r, here, at_left, at_right, al, au, ad):
    _, jl, je = TABLE[k]
    flux = al[jl - 1, r] * (pltpu.roll(here, ROWS - 1, 0) - here)
    total = flux - pltpu.roll(flux, 1, 0)
    lane = iota((ROWS, CE), 1)
    after = jnp.where(lane == CE - 1, column(at_right, 0, k, r), pltpu.roll(here, CE - 1, 1))
    before = jnp.where(lane == 0, column(at_left, 0, k, r), pltpu.roll(here, 1, 1))
    return total + (au[je - 1, r] * (after - here) + ad[je - 1, r] * (before - here))


def force(k, r, u, low, high, at_left, at_right, ar, al, au, ad):
    i, here = TABLE[k][0] // 2, u[k, r]
    below = u[k, r - 1] if r > 0 else low[k]
    above = u[k, r + 1] if r < CR - 1 else high[k]
    total = ar[i, r + 1] * (above - here) - ar[i, r] * (here - below)
    return total + level(k, r, here, at_left, at_right, al, au, ad)


def radial_ends(even, odd, count):
    rad, is_even = lax.axis_index("rad"), rad_is_even()
    lows, highs = [], []
    for k in range(count):
        low = jnp.where(is_even, odd[k], even[k])
        high = jnp.where(is_even, even[k], odd[k])
        lows.append(jnp.where(rad > 0, low, 0.0))
        highs.append(jnp.where(rad < lax.axis_size("rad") - 1, high, 0.0))
    return lows, highs


def joined_kernel(odd, out):
    rad = lax.axis_index("rad")
    joined = jnp.where(rad_is_even(), rad > 0, rad < lax.axis_size("rad") - 1)
    for k in range(odd.shape[0]):
        out[k] = jnp.where(joined, odd[k], 0.0)


def prepare_kernel(u, v, m, c, even, odd, at_left, at_right, ar, al, au, ad, following):
    lows, highs = radial_ends(even, odd, 5)
    lane = iota((ROWS, CE), 1)
    for i, j in enumerate((0, 2)):
        layers = [lows[3 + i]] + [m[j, r] for r in range(CR)] + [highs[3 + i]]
        for face in range(CR + 1):
            ar[i, face] = 0.5 * (layers[face] + layers[face + 1])
    for j in (1, 2, 3):
        for r in range(CR):
            here = m[j, r]
            al[j - 1, r] = 0.5 * (here + pltpu.roll(here, ROWS - 1, 0))
            after = jnp.where(
                lane == CE - 1, column(at_right, 3, j - 1, r), pltpu.roll(here, CE - 1, 1)
            )
            before = jnp.where(lane == 0, column(at_left, 3, j - 1, r), pltpu.roll(here, 1, 1))
            au[j - 1, r] = 0.5 * (here + after)
            ad[j - 1, r] = 0.5 * (here + before)
    for k in range(3):
        for r in range(CR):
            total = force(k, r, u, lows, highs, at_left, at_right, ar, al, au, ad)
            following[k, r] = 2.0 * u[k, r] - v[k, r] + c[r] * total


def thirds(x):
    high = x.astype(jnp.bfloat16).astype(F32)
    rest = x - high
    middle = rest.astype(jnp.bfloat16).astype(F32)
    return high, middle, rest - middle


def gather_sources(steps, got, weights, picks, layer=0, layers=CR):
    turned = jnp.transpose(jnp.concatenate([got[:, 0, :128], got[:, 0, 128:]], axis=0))
    parts = thirds(turned)
    cells = layers * ROWS
    cell_rows, cell_lanes = iota((cells, 128), 0) + layer * ROWS, iota((CE, 128), 0)
    for j in range(SLOTS):
        place = turned[96 + j : 97 + j].astype(I32)
        around = turned[104 + j : 105 + j].astype(I32)
        pick = jnp.where(cell_lanes == around, 1.0, 0.0)
        here = cell_rows == place
        for p in range(3):
            span = slice((p * SLOTS + j) * 128, (p * SLOTS + j + 1) * 128)
            picks[:, span] = pick
            for i, t in enumerate(steps):
                for k in range(3):
                    line = (k * STEPS + t) * 8 + j
                    at = (i * 3 + k) * cells
                    weights[at : at + cells, span] = jnp.where(
                        here, parts[p][line : line + 1], 0.0
                    )
    return lax.dot_general(
        weights[...], picks[...], (((1,), (1,)), ((), ())), preferred_element_type=F32
    )


def first_kernel(got, free, c, first, even, odd, left, right, weights, picks):
    summed = gather_sources((0,), got, weights, picks)
    for k in range(3):
        for r in range(CR):
            at = (k * CR + r) * ROWS
            first[k, r] = free[k, r] + summed[at : at + ROWS] * c[r]
    lead, _ = end_layers()
    for k in range(3):
        odd[k] = first[k, lead]
    put_rest(first, even, left, right)


def sources_kernel(got, c, sources, weights, picks):
    summed = gather_sources(range(1, STEPS), got, weights, picks)
    for t in range(STEPS - 1):
        for k in range(3):
            for r in range(CR):
                at = ((t * 3 + k) * CR + r) * ROWS
                sources[t, k, r] = summed[at : at + ROWS] * c[r]


def lead_kernel(t, u, v, c, sources, odd, at_left, at_right, ar, al, au, ad, out):
    lead, _ = end_layers()
    rad, downwards = lax.axis_index("rad"), rad_is_even()
    joined = jnp.where(downwards, rad > 0, rad < lax.axis_size("rad") - 1)
    inner = jnp.where(downwards, 1, CR - 2)
    outer_face, inner_face = jnp.where(downwards, 0, CR), jnp.where(downwards, 1, CR - 1)
    for k in range(3):
        i, here = TABLE[k][0] // 2, u[k, lead]
        outer = jnp.where(joined, odd[k], 0.0)
        total = ar[i, outer_face] * (outer - here) + ar[i, inner_face] * (u[k, inner] - here)
        total = total + level(k, lead, here, at_left, at_right, al, au, ad)
        out[k] = 2.0 * here - v[k, lead] + c[lead] * total + sources[t - 1, k, lead]


def step_kernel(
    t, u, v, c, sources, even, odd, at_left, at_right, ar, al, au, ad, made, following, *rest
):
    lows, highs = radial_ends(even, odd, 3)
    for k in range(3):
        for r in range(CR):
            total = force(k, r, u, lows, highs, at_left, at_right, ar, al, au, ad)
            following[k, r] = 2.0 * u[k, r] - v[k, r] + c[r] * total + sources[t - 1, k, r]
    keep_lead(following, made)
    put_rest(following, *rest)


def base_kernel(u, v, c, sources, ar, al, base, before_final):
    for k in range(3):
        i, jl = TABLE[k][0] // 2, TABLE[k][1] - 1
        for r in range(CR):
            here = u[k, r]
            flux = al[jl, r] * (pltpu.roll(here, ROWS - 1, 0) - here)
            total = flux - pltpu.roll(flux, 1, 0)
            if r < CR - 1:
                total = total + ar[i, r + 1] * (u[k, r + 1] - here)
            if r > 0:
                total = total - ar[i, r] * (here - u[k, r - 1])
            value = 2.0 * here - v[k, r] + c[r] * total + sources[STEPS - 2, k, r]
            base[k, r] = value[:CL]
            before_final[k, r] = here[:CL]


def end_kernel(u, c, odd, ar, out):
    lead, _ = end_layers()
    rad, downwards = lax.axis_index("rad"), rad_is_even()
    joined = jnp.where(downwards, rad > 0, rad < lax.axis_size("rad") - 1)
    face = jnp.where(downwards, 0, CR)
    for k in range(3):
        outer = jnp.where(joined, odd[k, 0:CL, :], 0.0)
        coefficient = c[lead, 0:CL, :] * ar[TABLE[k][0] // 2, face, 0:CL, :]
        out[k] = coefficient * (outer - u[k, lead, 0:CL, :])


def last_kernel(u, c, base, even, made, at_left, at_right, ar, au, ad, final):
    lane = iota((CL, CE), 1)
    for k in range(3):
        je = TABLE[k][2] - 1
        for r in range(CR):
            here = u[k, r, 0:CL, :]
            right, left = column(at_right, 0, k, r)[:CL], column(at_left, 0, k, r)[:CL]
            after = jnp.where(lane == CE - 1, right, pltpu.roll(here, CE - 1, 1))
            before = jnp.where(lane == 0, left, pltpu.roll(here, 1, 1))
            total = au[je, r, 0:CL, :] * (after - here) + ad[je, r, 0:CL, :] * (before - here)
            final[k, r] = base[k, r] + c[r, 0:CL, :] * total
    lead, rest = end_layers()
    face = jnp.where(rad_is_even(), CR, 0)
    for k in range(3):
        coefficient = c[rest, 0:CL, :] * ar[TABLE[k][0] // 2, face, 0:CL, :]
        flux = coefficient * (even[k, 0:CL, :] - u[k, rest, 0:CL, :])
        final[k, rest] = final[k, rest] + flux
        final[k, lead] = final[k, lead] + made[k]


def call(kernel, outs, args, scratch=(), hbm=0, us=1.0):
    vmem = pl.BlockSpec(memory_space=pltpu.VMEM)
    specs = [pl.BlockSpec(memory_space=pltpu.HBM)] * hbm + [vmem] * (len(args) - hbm)
    return pl.pallas_call(
        kernel,
        out_shape=[jax.ShapeDtypeStruct(shape, F32) for shape in outs],
        in_specs=specs,
        out_specs=[vmem] * len(outs),
        scratch_shapes=[pltpu.VMEM(s, F32) if isinstance(s, tuple) else s for s in scratch],
        cost_estimate=pl.CostEstimate(
            flops=0, bytes_accessed=int(us * 3_000_000), transcendentals=0
        ),
        compiler_params=pltpu.CompilerParams(vmem_limit_bytes=(60 if hbm else 32) * 1024 * 1024),
    )(*args)


def shifted(block, axis, by):
    count = lax.axis_size(axis)
    return lax.ppermute(block, axis, [(i, (i + by) % count) for i in range(count)])


def swapped(block, axis, odd):
    count = lax.axis_size(axis)
    pairs = [(i, (i + (1 if (i + odd) % 2 == 0 else -1)) % count) for i in range(count)]
    return lax.ppermute(block, axis, pairs)


def swap_columns(left, right):
    return shifted(right, "span", 1), shifted(left, "span", -1)


def on_device(current, previous, moduli, density, traces, receivers, owners, offsets):
    wide = (3, CR, ROWS, CE)
    edge = (11, 2, 8, CE)
    layer, columns = (3, ROWS, CE), [(8, CE), (8, CE)]

    fields = (current, previous, moduli, density.reshape((1,) + density.shape))
    rooms = [(11, CR, 8, CE), pltpu.SemaphoreType.DMA((4,))]
    (high_rows,) = call(high_kernel, [edge], fields, scratch=rooms, hbm=4)
    from_low = shifted(high_rows, "lat", 1)
    packed, low_rows = call(
        pack_kernel,
        [(64, 1, 256), edge],
        (
            offsets.reshape(1, 128),
            receivers.reshape(1, 128),
            owners.reshape(1, 128),
            traces.transpose(1, 0, 2),
        )
        + fields,
        scratch=rooms
        + [
            (3, STATIONS, 512),
            pltpu.VMEM((8, 128), I32),
            pltpu.SemaphoreType.DMA(()),
            pltpu.SemaphoreType.DMA((3,)),
        ],
        hbm=8,
        us=2.0,
    )
    from_high = shifted(low_rows, "lat", -1)
    got = lax.all_to_all(packed, ("lat", "rad"), 0, 0, tiled=True)

    u, v, m, c, even, odd, *ends = call(
        widen_kernel,
        [wide, wide, (4, CR, ROWS, CE), (CR, ROWS, CE)]
        + [(5, ROWS, CE), (5, ROWS, CE), (8, CE), (8, CE)],
        (current, previous, moduli, density, from_low, from_high),
    )
    even, odd = swapped(even, "rad", 0), swapped(odd, "rad", 1)
    (odd,) = call(joined_kernel, [(5, ROWS, CE)], (odd,), us=0.3)
    *coefficients, free = call(
        prepare_kernel,
        [(2, CR + 1, ROWS, CE), wide, wide, wide, wide],
        (u, v, m, c, even, odd, *swap_columns(*ends)),
    )
    cells, lanes = CR * ROWS, 3 * SLOTS * 128
    first, even, odd, *ends = call(
        first_kernel,
        [wide, layer, layer] + columns,
        (got, free, c),
        scratch=[(3 * cells, lanes), (CE, lanes)],
    )
    (sources,) = call(
        sources_kernel,
        [(STEPS - 1,) + wide],
        (got, c),
        scratch=[(3 * (STEPS - 1) * cells, lanes), (CE, lanes)],
        us=3.0,
    )
    odd = swapped(odd, "rad", 1)
    v, u = u, first
    for t in range(1, STEPS):
        even = swapped(even, "rad", 0)
        at_left, at_right = swap_columns(*ends)
        if t == STEPS - 1:
            ar, al, au, ad = coefficients
            own = (3, CR, CL, CE)
            base, before_final = call(base_kernel, [own, own], (u, v, c, sources, ar, al))
            (made,) = call(end_kernel, [(3, CL, CE)], (u, c, odd, ar), us=0.3)
            (final,) = call(
                last_kernel, [own], (u, c, base, even, made, at_left, at_right, ar, au, ad)
            )
            return final, before_final
        before = (u, v, c, sources)
        after = (at_left, at_right, *coefficients)

        def lead(*refs, t=t):
            lead_kernel(t, *refs)

        def step(*refs, t=t):
            step_kernel(t, *refs)

        (made,) = call(lead, [layer], before + (odd,) + after)
        next_odd = swapped(made, "rad", 1)
        following, even, *ends = call(
            step, [wide, layer] + columns, before + (even, odd) + after + (made,)
        )
        v, u, odd = u, following, next_odd


def solution(mesh):
    in_specs = (
        P(None, "rad", "lat", "span"),
        P(None, "rad", "lat", "span"),
        P(None, "rad", "lat", "span"),
        P("rad", "lat", "span"),
        P(("span", "lat", "rad"), None, None),
        P(("span", "lat", "rad")),
        P(("span", "lat", "rad"), None),
        P(("span", "lat", "rad")),
    )
    out_specs = (P(None, "rad", "lat", "span"), P(None, "rad", "lat", "span"))
    return jax.shard_map(
        on_device, mesh=mesh, in_specs=in_specs, out_specs=out_specs, check_vma=False
    )
```
